32 devices in a mesh: shard: 4 (over z), ctx: 2 (over y), tensor: 4 (over x, core).
Axes of the slice: x: 2, y: 2, z: 4, core: 2. Of those that a mesh axis runs over, the one named last changes fastest.
Arguments:
- tokens: bfloat16 [4, 4096, 768], P('shard', ('ctx', 'tensor')), may hold values from -6 to 6
- doc_lengths: int32 [4, 4], P('shard'), may hold values from 1 to 2048, 4096 in all within a row
- attn_gain: bfloat16 [768], P(('shard', 'ctx')), may hold values from 0.5 to 1.5
- mlp_gain: bfloat16 [768], P(('shard', 'ctx')), may hold values from 0.5 to 1.5
- w_qkv: bfloat16 [768, 2304], P(('shard', 'ctx')), may hold values from -0.21875 to 0.21875
- w_attn_out: bfloat16 [768, 768], P(('shard', 'ctx')), may hold values from -0.875 to 0.875
- w_in: bfloat16 [768, 2, 1152], P(('shard', 'ctx'), None, 'tensor'), may hold values from -0.21875 to 0.21875
- w_down: bfloat16 [1152, 768], P('tensor', ('shard', 'ctx')), may hold values from -0.1875 to 0.1875
- cotangent: bfloat16 [4, 4096, 768], P('shard', ('ctx', 'tensor')), may hold values from -6 to 6
Outputs:
- layer_out: bfloat16 [4, 4096, 768], P('shard', ('ctx', 'tensor'))
- grad_tokens: float32 [4, 4096, 768], P('shard', ('ctx', 'tensor'))
- d_attn_gain: float32 [768], P(('shard', 'ctx', 'tensor'))
- d_mlp_gain: float32 [768], P(('shard', 'ctx', 'tensor'))
- d_w_qkv: float32 [768, 2304], P(('shard', 'ctx', 'tensor'))
- d_w_attn_out: float32 [768, 768], P(('shard', 'ctx', 'tensor'))
- d_w_in: float32 [768, 2, 1152], P(('shard', 'ctx'), None, 'tensor')
- d_w_down: float32 [1152, 768], P('tensor', ('shard', 'ctx'))
The draws below stay inside these ranges and needn't reach their ends.
Inputs may be any that keep to these rules, and one draw needn't show every extreme that they name: `doc_lengths`: row s holds, in order, the lengths of the 4 documents packed into sequence s; they sum to 4096 and the longest is 2048.
All inputs are finite; a program needn't handle non-finite values.
Results may differ from the reference program's by a relative error of at most 0.017.
Values may be sent and summed in bfloat16 or wider, within the bound.
No kernel may reach another device: no remote copies, remote signals or barrier semaphores. Data moves between devices by JAX's collectives and lax.ppermute only.
A program may use at most 192 MiB of HBM per device.

```python
import math
import jax
import jax.numpy as jnp
import numpy as np
from jax import lax

D = 768
HEADS = 12
HEAD_DIM = 64
FF = 1152
SEQ = 4096
DOCS = 4
DOC_MOST = 2048
SEQS = 4


def levels(own_key, extent, split, least, high):
    def one(position, blocks):
        heights = jax.random.uniform(jax.random.fold_in(jax.random.fold_in(own_key, 6), position), (blocks,), jnp.float32, least / len(split), high / len(split))
        return jnp.repeat(jnp.exp(heights), extent[position] // blocks).reshape((-1,) + (1,) * (len(extent) - position - 1))

    level = one(*split[0])
    for cut in split[1:]:
        level = level * one(*cut)
    return level


def length_profile(amount, total, most, slope):
    loads = [(1 << 20) // math.isqrt(rank ** slope) + 1 for rank in range(2, amount + 1)]
    rest, given = total - most - (amount - 1), [1] * (amount - 1)
    while rest > 0:
        movable = [i for i in range(amount - 1) if given[i] < most]
        pool, remaining = sum([loads[i] for i in movable]), rest
        for i in movable:
            extra = min(most - given[i], max(1, remaining * loads[i] // pool), rest)
            given[i] = given[i] + extra
            rest = rest - extra
    return np.array([most] + given)


def ragged_sizes(own_key, amount, total, bound, skew):
    if amount == 2:
        one = jax.random.randint(own_key, (), max(1, total - bound), min(bound, total - 1) + 1)
        return jnp.stack([one, total - one])
    sizes = jnp.asarray(length_profile(amount, total, bound, skew), jnp.int32)
    pairs = (amount - 1) // 2
    donor, receiver = sizes[1:1 + 2 * pairs:2], sizes[2:2 + 2 * pairs:2]
    margin = jnp.minimum(donor - 1, bound - receiver)
    passed = jax.random.randint(jax.random.fold_in(own_key, 1), (pairs,), 0, 1 << 20) % (margin + 1)
    sizes = sizes.at[1:1 + 2 * pairs:2].set(donor - passed).at[2:2 + 2 * pairs:2].set(receiver + passed)
    return sizes[jax.random.permutation(jax.random.fold_in(own_key, 2), amount)]


def bell_draw(rng, dims, deviation, bound, cuts=(), kind=jnp.bfloat16):
    values = jax.random.normal(rng, dims, jnp.float32) * deviation
    if len(cuts) > 0:
        values = levels(rng, dims, cuts, -0.22, 0.18) * values
    return jnp.clip(values, min=-bound, max=bound).astype(kind)


def setup_inputs(seed: int = 0) -> dict:
    key_of = jax.random.split(jax.random.key(seed), 10)
    tokens = bell_draw(key_of[0], (SEQS, SEQ, D), 1.0, 6.0, ((0, 4), (1, 8)))
    doc_lengths = jax.vmap(lambda own: ragged_sizes(own, DOCS, SEQ, DOC_MOST, 1))(jax.random.split(key_of[1], SEQS)).reshape((SEQS, DOCS)).astype(jnp.int32)
    attn_gain = jnp.clip(1.0 + 0.1 * jax.random.normal(key_of[2], (D,), jnp.float32), 0.5, 1.5).astype(jnp.bfloat16)
    mlp_gain = jnp.clip(1.0 + 0.1 * jax.random.normal(key_of[3], (D,), jnp.float32), 0.5, 1.5).astype(jnp.bfloat16)
    w_qkv = bell_draw(key_of[4], (D, 3 * D), D ** -0.5, 0.21875, ((0, 8),))
    w_attn_out = bell_draw(key_of[5], (D, D), (D // 16) ** -0.5, 0.875, ((0, 8),))
    w_in = bell_draw(key_of[6], (D, 2, FF), D ** -0.5, 0.21875, ((0, 8), (2, 4)))
    w_down = bell_draw(key_of[7], (FF, D), FF ** -0.5, 0.1875, ((0, 4), (1, 8)))
    cotangent = bell_draw(key_of[8], (SEQS, SEQ, D), 1.0, 6.0, ((0, 4), (1, 8)))
    return {"tokens": tokens, "doc_lengths": doc_lengths, "attn_gain": attn_gain, "mlp_gain": mlp_gain, "w_qkv": w_qkv, "w_attn_out": w_attn_out, "w_in": w_in, "w_down": w_down, "cotangent": cotangent}


EPSILON = 1e-05
ROPE_THETA = 160000.0
SCORE_SCALE = 0.125
MASKED_SCORE = -1e+30
ROOT_HALF = 0.7071067811865476
BEST_PRECISION = lax.Precision.HIGHEST

@jax.custom_vjp
def low(v):
    return lax.optimization_barrier(v.astype(jnp.bfloat16)).astype(jnp.float32)

@jax.custom_vjp
def low_back(v):
    return v

def low_keep(v):
    return (low(v), None)

def low_pass(kept, grad):
    return (grad,)

def back_keep(v):
    return (v, None)

def back_low(kept, grad):
    return (low(grad),)
low.defvjp(low_keep, low_pass)
low_back.defvjp(back_keep, back_low)

def exact_gelu(values):
    return 0.5 * values * (1.0 + jax.scipy.special.erf(values * ROOT_HALF))

def gated_gelu(both_proj):
    return exact_gelu(both_proj[..., 0, :]) * both_proj[..., 1, :]

def layer_norm(values, gain):
    mean_value = lax.optimization_barrier(jnp.mean(values, -1, keepdims=True))
    centred = values - mean_value
    spread = lax.optimization_barrier(jnp.mean(centred * centred, -1, keepdims=True))
    return centred * lax.rsqrt(spread + EPSILON) * gain

def rotate(values, positions):
    half_dim = values.shape[-1] // 2
    steps_index = jnp.arange(half_dim).astype(jnp.float32)
    inverse = ROPE_THETA ** (-2.0 * steps_index / values.shape[-1])
    angles = positions.astype(jnp.float32)[:, None] * inverse[None, :]
    angles = jnp.concatenate([angles, angles], -1)
    cosine = jnp.cos(angles)[:, None, :]
    sine = jnp.sin(angles)[:, None, :]
    turned = jnp.concatenate([-values[..., half_dim:], values[..., :half_dim]], -1)
    return values * cosine + turned * sine

def segment_ids(lengths, positions):
    doc_ends = jnp.cumsum(lengths, -1)[:, :-1]
    return lax.optimization_barrier(jnp.sum((positions[None, :, None] >= doc_ends[:, None, :]).astype(jnp.int32), -1))

def forward(inputs, segments, positions, attn_gain, mlp_gain, w_qkv, w_attn_out, w_in, w_down):
    length = inputs.shape[0]
    normed = low(layer_norm(inputs, attn_gain))
    raw_proj = low_back(jnp.dot(normed, w_qkv, precision=BEST_PRECISION)).reshape(length, 3, HEADS, HEAD_DIM)
    query_all = low(low_back(rotate(raw_proj[:, 0], positions)))
    key_all = low(low_back(rotate(raw_proj[:, 1], positions)))
    value_all = low(low_back(raw_proj[:, 2]))
    same_doc = segments[:, None] == segments[None, :]

    def one_head(head_parts):
        query_head, key_head, value_head = head_parts
        scores = low_back(jnp.dot(query_head, key_head.T, precision=BEST_PRECISION) * SCORE_SCALE)
        scores = jnp.where(same_doc, scores, MASKED_SCORE)
        row_top = lax.optimization_barrier(jnp.max(scores, -1, keepdims=True))
        weights = jnp.exp(scores - row_top)
        prob_rows = weights / lax.optimization_barrier(jnp.sum(weights, -1, keepdims=True))
        return low(low_back(jnp.dot(low(prob_rows), value_head, precision=BEST_PRECISION)))
    head_outs = lax.map(jax.checkpoint(one_head), (query_all.transpose(1, 0, 2), key_all.transpose(1, 0, 2), value_all.transpose(1, 0, 2)))
    attended = head_outs.transpose(1, 0, 2).reshape(length, HEADS * HEAD_DIM)
    hidden = inputs + low_back(jnp.dot(attended, w_attn_out, precision=BEST_PRECISION))
    normed_m = low(layer_norm(hidden, mlp_gain))
    both_proj = low_back(jnp.dot(normed_m, w_in.reshape(w_in.shape[0], -1), precision=BEST_PRECISION)).reshape(length, 2, -1)
    gated = low(gated_gelu(both_proj))
    return hidden + jnp.dot(gated, w_down, precision=BEST_PRECISION)

def reference(tokens, doc_lengths, attn_gain, mlp_gain, w_qkv, w_attn_out, w_in, w_down, cotangent):
    params = (attn_gain.astype(jnp.float32), mlp_gain.astype(jnp.float32), w_qkv.astype(jnp.float32), w_attn_out.astype(jnp.float32), w_in.astype(jnp.float32), w_down.astype(jnp.float32))
    positions = jnp.arange(SEQ).astype(jnp.int32)

    def one_sequence(totals, sequence):
        inputs, lengths, grad_out = sequence
        segments = segment_ids(lengths[None, :], positions)[0]

        def layer_fn(inputs_f, *weight_args):
            return forward(inputs_f, segments, positions, *weight_args)
        out_value, pull_back = jax.vjp(layer_fn, inputs.astype(jnp.float32), *params)
        grad_list = pull_back(grad_out.astype(jnp.float32))
        totals = tuple((carry_sum + grad_part for carry_sum, grad_part in zip(totals, grad_list[1:])))
        return (totals, (out_value.astype(jnp.bfloat16), grad_list[0]))
    zero_sums = tuple((jnp.zeros_like(weight_arg) for weight_arg in params))
    totals, (layer_out, grad_tokens) = lax.scan(one_sequence, zero_sums, (tokens, doc_lengths, cotangent))
    return (layer_out, grad_tokens, totals[0], totals[1], totals[2], totals[3], totals[4], totals[5])
```

```python
import functools

import jax
import jax.numpy as jnp
from jax import lax
from jax.experimental import pallas as pl
from jax.experimental.pallas import tpu as pltpu
from jax.sharding import PartitionSpec as P

HEAD_DIM = 64
EPSILON = 1e-05
ROPE_THETA = 160000.0
SCORE_SCALE = 0.125
MASKED_SCORE = -1e30
ROOT_HALF = 0.7071067811865476
VMEM_LIMIT = 56 * 1024 * 1024

NT = (((1,), (1,)), ((), ()))
NN = (((1,), (0,)), ((), ()))


def dot(a, b, dims):
    return lax.dot_general(a, b, dims, preferred_element_type=jnp.float32)


def seg_of(position, ends):
    seg = (position >= ends[0]).astype(jnp.int32)
    for end in ends[1:]:
        seg = seg + (position >= end).astype(jnp.int32)
    return seg


def stack_heads(values, group):
    lane_head = lax.broadcasted_iota(jnp.int32, values.shape, 1) // HEAD_DIM
    return jnp.concatenate(
        [jnp.where(lane_head == h, values, jnp.zeros_like(values)) for h in range(group)], 0
    )


def each_key_block(meta, docs, q_at, q_rows, k_first, k_rows, k_blocks, group, body):
    ends = [meta[i] for i in range(docs - 1)]
    q_lo, q_hi = seg_of(q_at, ends), seg_of(q_at + q_rows - 1, ends)
    q_seg = seg_of(q_at + lax.broadcasted_iota(jnp.int32, (1, q_rows), 1), ends)
    q_seg = jnp.concatenate([q_seg] * group, 1)

    def step(j, carry):
        k_at = meta[k_first + j]
        k_lo, k_hi = seg_of(k_at, ends), seg_of(k_at + k_rows - 1, ends)
        meets = (k_lo <= q_hi) & (q_lo <= k_hi)
        same = (k_lo == k_hi) & (q_lo == q_hi)

        @pl.when(meets & same)
        def _():
            body(j, None)

        @pl.when(meets & jnp.logical_not(same))
        def _():
            k_seg = seg_of(k_at + lax.broadcasted_iota(jnp.int32, (k_rows, 1), 0), ends)
            body(j, k_seg == q_seg)

        return carry

    lax.fori_loop(0, k_blocks, step, 0)


def attend_kernel(docs, k_rows, meta, q_ref, k_ref, v_ref, o_ref, lse_ref, vt_ref, m_ref, l_ref, acc_ref):
    q_rows, wide = q_ref.shape[1], q_ref.shape[2]
    group = wide // HEAD_DIM
    k_blocks = k_ref.shape[1] // k_rows
    q_blocks = pl.num_programs(1)
    i = pl.program_id(1)

    @pl.when(i == 0)
    def _():
        for j in range(k_blocks):
            at = pl.ds(j * k_rows, k_rows)
            vt_ref[:, at] = v_ref[0, at, :].T

    q_st = stack_heads(q_ref[0] * SCORE_SCALE, group)
    m_ref[...] = jnp.full(m_ref.shape, MASKED_SCORE, jnp.float32)
    l_ref[...] = jnp.zeros_like(l_ref)
    acc_ref[...] = jnp.zeros_like(acc_ref)

    def body(j, mask):
        at = pl.ds(pl.multiple_of(j * k_rows, k_rows), k_rows)
        scores = dot(k_ref[0, at, :], q_st, NT)
        if mask is not None:
            scores = jnp.where(mask, scores, MASKED_SCORE)
        m_old = m_ref[...]
        m_new = jnp.maximum(m_old, jnp.max(scores, 0, keepdims=True))
        shrink = jnp.exp(m_old - m_new)
        weights = jnp.exp(scores - m_new)
        if mask is not None:
            weights = jnp.where(mask, weights, 0.0)
        m_ref[...] = m_new
        l_ref[...] = l_ref[...] * shrink + jnp.sum(weights, 0, keepdims=True)
        low = weights.astype(jnp.bfloat16)
        for h in range(group):
            rows = pl.ds(h * HEAD_DIM, HEAD_DIM)
            cols = slice(h * q_rows, (h + 1) * q_rows)
            acc_ref[rows, :] = acc_ref[rows, :] * shrink[:, cols] + dot(vt_ref[rows, at], low[:, cols], NN)

    each_key_block(meta, docs, meta[docs - 1 + i], q_rows, docs - 1 + q_blocks, k_rows, k_blocks, group, body)
    total = l_ref[...]
    outs = []
    for h in range(group):
        cols = slice(h * q_rows, (h + 1) * q_rows)
        outs.append(acc_ref[h * HEAD_DIM : (h + 1) * HEAD_DIM, :] / total[:, cols])
    o_ref[0] = jnp.concatenate(outs, 0).T.astype(jnp.bfloat16)
    lse_ref[0, 0] = m_ref[...] + jnp.log(total)


def attend_back_kernel(
    docs, k_rows, meta, q_ref, k_ref, v_ref, o_ref, do_ref, lse_ref, dq_ref, dk_ref, dv_ref,
    kt_ref, dqt_ref, dk_acc, dv_acc,
):
    q_rows, wide = q_ref.shape[1], q_ref.shape[2]
    group = wide // HEAD_DIM
    k_blocks = k_ref.shape[1] // k_rows
    q_blocks = pl.num_programs(1)
    i = pl.program_id(1)

    @pl.when(i == 0)
    def _():
        dk_acc[...] = jnp.zeros_like(dk_acc)
        dv_acc[...] = jnp.zeros_like(dv_acc)
        for j in range(k_blocks):
            at = pl.ds(j * k_rows, k_rows)
            kt_ref[:, at] = k_ref[0, at, :].T

    q_st = stack_heads(q_ref[0] * SCORE_SCALE, group)
    grad_out = do_ref[0]
    do_st = stack_heads(grad_out, group)
    product = (grad_out.astype(jnp.float32) * o_ref[0].astype(jnp.float32)).T
    delta = jnp.concatenate(
        [jnp.sum(product[h * HEAD_DIM : (h + 1) * HEAD_DIM], 0, keepdims=True) for h in range(group)], 1
    )
    log_total = lse_ref[0, 0]
    dqt_ref[...] = jnp.zeros_like(dqt_ref)

    def body(j, mask):
        at = pl.ds(pl.multiple_of(j * k_rows, k_rows), k_rows)
        scores = dot(k_ref[0, at, :], q_st, NT)
        if mask is not None:
            scores = jnp.where(mask, scores, MASKED_SCORE)
        probs = jnp.exp(scores - log_total)
        dv_acc[at, :] += dot(probs.astype(jnp.bfloat16), do_st, NN)
        grad_probs = dot(v_ref[0, at, :], do_st, NT)
        grad_scores = (probs * (grad_probs - delta)).astype(jnp.bfloat16)
        dk_acc[at, :] += dot(grad_scores, q_st, NN)
        for h in range(group):
            rows = pl.ds(h * HEAD_DIM, HEAD_DIM)
            cols = slice(h * q_rows, (h + 1) * q_rows)
            dqt_ref[rows, :] += dot(kt_ref[rows, at], grad_scores[:, cols], NN)

    each_key_block(meta, docs, meta[docs - 1 + i], q_rows, docs - 1 + q_blocks, k_rows, k_blocks, group, body)
    dq_ref[0] = (dqt_ref[...].T * SCORE_SCALE).astype(jnp.bfloat16)

    @pl.when(i == q_blocks - 1)
    def _():
        dk_ref[0] = dk_acc[...].astype(jnp.bfloat16)
        dv_ref[0] = dv_acc[...].astype(jnp.bfloat16)


def attend_call(meta, query, key, value, docs, q_rows, k_rows):
    items, length, wide = query.shape
    keys = key.shape[1]
    group = wide // HEAD_DIM
    q_blocks = length // q_rows
    block = pl.BlockSpec((1, q_rows, wide), lambda g, i, m: (g, i, 0))
    whole = pl.BlockSpec((1, keys, wide), lambda g, i, m: (g, 0, 0))
    stat = pl.BlockSpec((1, 1, 1, group * q_rows), lambda g, i, m: (g, i, 0, 0))
    return pl.pallas_call(
        functools.partial(attend_kernel, docs, k_rows),
        grid_spec=pltpu.PrefetchScalarGridSpec(
            num_scalar_prefetch=1,
            grid=(items, q_blocks),
            in_specs=[block, whole, whole],
            out_specs=[block, stat],
            scratch_shapes=[
                pltpu.VMEM((wide, keys), jnp.bfloat16),
                pltpu.VMEM((1, group * q_rows), jnp.float32),
                pltpu.VMEM((1, group * q_rows), jnp.float32),
                pltpu.VMEM((wide, q_rows), jnp.float32),
            ],
        ),
        out_shape=[
            jax.ShapeDtypeStruct(query.shape, jnp.bfloat16),
            jax.ShapeDtypeStruct((items, q_blocks, 1, group * q_rows), jnp.float32),
        ],
        compiler_params=pltpu.CompilerParams(vmem_limit_bytes=VMEM_LIMIT),
        name="attend",
    )(meta, query, key, value)


def attend_back_call(meta, query, key, value, out, grad_out, log_total, docs, q_rows, k_rows):
    items, length, wide = query.shape
    keys = key.shape[1]
    group = wide // HEAD_DIM
    q_blocks = length // q_rows
    block = pl.BlockSpec((1, q_rows, wide), lambda g, i, m: (g, i, 0))
    whole = pl.BlockSpec((1, keys, wide), lambda g, i, m: (g, 0, 0))
    stat = pl.BlockSpec((1, 1, 1, group * q_rows), lambda g, i, m: (g, i, 0, 0))
    return pl.pallas_call(
        functools.partial(attend_back_kernel, docs, k_rows),
        grid_spec=pltpu.PrefetchScalarGridSpec(
            num_scalar_prefetch=1,
            grid=(items, q_blocks),
            in_specs=[block, whole, whole, block, block, stat],
            out_specs=[block, whole, whole],
            scratch_shapes=[
                pltpu.VMEM((wide, keys), jnp.bfloat16),
                pltpu.VMEM((wide, q_rows), jnp.float32),
                pltpu.VMEM((keys, wide), jnp.float32),
                pltpu.VMEM((keys, wide), jnp.float32),
            ],
        ),
        out_shape=[
            jax.ShapeDtypeStruct(query.shape, jnp.bfloat16),
            jax.ShapeDtypeStruct(key.shape, jnp.bfloat16),
            jax.ShapeDtypeStruct(key.shape, jnp.bfloat16),
        ],
        compiler_params=pltpu.CompilerParams(vmem_limit_bytes=VMEM_LIMIT),
        name="attend_back",
    )(meta, query, key, value, out, grad_out, log_total)


def exact_gelu(values):
    return 0.5 * values * (1.0 + jax.scipy.special.erf(values * ROOT_HALF))


def gated_gelu(half_a, half_b):
    return exact_gelu(half_a) * half_b


def layer_norm(values, gain):
    mean_value = jnp.mean(values, -1, keepdims=True)
    centred = values - mean_value
    spread = jnp.mean(centred * centred, -1, keepdims=True)
    return centred * lax.rsqrt(spread + EPSILON) * gain


def turn_matrix(width):
    row = lax.broadcasted_iota(jnp.int32, (width, width), 0)
    col = lax.broadcasted_iota(jnp.int32, (width, width), 1)
    half = HEAD_DIM // 2
    first = (col % HEAD_DIM) < half
    plus = jnp.logical_not(first) & (row == col - half)
    minus = first & (row == col + half)
    return plus.astype(jnp.bfloat16) - minus.astype(jnp.bfloat16)


def angle_tables(positions, width):
    half = HEAD_DIM // 2
    steps_index = (jnp.arange(width) % half).astype(jnp.float32)
    inverse = ROPE_THETA ** (-2.0 * steps_index / HEAD_DIM)
    angles = positions.astype(jnp.float32)[:, None] * inverse[None, :]
    return jnp.cos(angles), jnp.sin(angles)


def mm(a, b):
    return jnp.dot(a, b, preferred_element_type=jnp.float32)


def mm_nt(a, b):
    return lax.dot_general(a, b, (((1,), (1,)), ((), ())), preferred_element_type=jnp.float32)


def mm_tn(a, b):
    return lax.dot_general(a, b, (((0,), (0,)), ((), ())), preferred_element_type=jnp.float32)


PLANE = ("ctx", "tensor")
ROWS = ("shard", "ctx")


def plane_permute(array, target):
    pairs = []
    for c in range(2):
        for x in range(2):
            for h in range(2):
                to_c, to_x, to_h = target(c, x, h)
                pairs.append((c * 4 + x * 2 + h, to_c * 4 + to_x * 2 + to_h))
    return lax.ppermute(array, PLANE, pairs)


def tensor_permute(array, flip):
    return lax.ppermute(array, "tensor", [(t, t ^ flip) for t in range(4)])


def pick(array, index, axis):
    return lax.dynamic_index_in_dim(array, index, axis, keepdims=False)


def local(tokens, doc_lengths, attn_gain, mlp_gain, w_qkv, w_attn_out, w_in, w_down, cotangent):
    _, block, width = tokens.shape
    assert lax.axis_size("ctx") == 2 and lax.axis_size("tensor") == 4 and tokens.shape[0] == 1
    row_parts = lax.axis_size("shard") * 2
    rows = w_qkv.shape[0]
    ff = w_in.shape[2]
    docs = doc_lengths.shape[1]
    c = lax.axis_index("ctx")
    t = lax.axis_index("tensor")
    x, h = t // 2, t % 2
    wide = width // 4
    bf16 = jnp.bfloat16

    own = tokens[0]
    by_x = tensor_permute(own, 2)
    by_y = plane_permute(own, lambda c, x, h: (1 - c, x, h))
    by_xy = plane_permute(own, lambda c, x, h: (1 - c, 1 - x, h))
    chunks = []
    for part in (own, by_x, by_y, by_xy):
        chunks += [part, tensor_permute(part, 1)]

    group_cols = pick(w_qkv.reshape(rows, 3, 4, wide), t, 2).reshape(rows, 3 * wide)
    pack_1 = jnp.concatenate(
        [group_cols, jnp.broadcast_to(attn_gain[:, None], (rows, 64))], 1
    )
    pack_1 = lax.all_gather(pack_1, ROWS, axis=0, tiled=True)
    pack_2 = jnp.concatenate(
        [w_in.reshape(rows, 2 * ff), w_down.T, w_attn_out, jnp.broadcast_to(mlp_gain[:, None], (rows, 32))], 1
    )
    pack_2 = lax.all_gather(pack_2, ROWS, axis=0, tiled=True)
    slices = [pack_2[:, : 3 * ff]]
    slices.append(tensor_permute(slices[0], 2))
    slices += [tensor_permute(slices[0], 1), tensor_permute(slices[1], 1)]
    slice_flips = (0, 2, 1, 3)
    w_a = jnp.concatenate([s[:, :ff] for s in slices], 1)
    w_b = jnp.concatenate([s[:, ff : 2 * ff] for s in slices], 1)
    w_dt = jnp.concatenate([s[:, 2 * ff :] for s in slices], 1)
    w_o = pack_2[:, 3 * ff : 3 * ff + width]
    gain_mlp = pack_2[:, 3 * ff + width].astype(jnp.float32)

    chunk_at = []
    for dc in range(2):
        for dx in range(2):
            for dh in range(2):
                chunk_at.append(((c ^ dc) * 4 + (x ^ dx) * 2 + (h ^ dh)) * block)
    all_pos = jnp.concatenate([at + jnp.arange(block) for at in chunk_at])
    cosine, sine = angle_tables(all_pos, wide)
    q_rows = min(512, block)
    k_rows = min(512, block)
    pick_core = h ^ c

    def query_rows(values):
        return pick(values.reshape(4, 2, block, values.shape[1]), pick_core, 1).reshape(4 * block, -1)

    key_starts = [at + k * k_rows for at in chunk_at for k in range(block // k_rows)]
    query_starts = [
        ((c ^ dc) * 4 + (x ^ dx) * 2 + c) * block + k * q_rows
        for dc in range(2)
        for dx in range(2)
        for k in range(block // q_rows)
    ]
    doc_ends = jnp.cumsum(doc_lengths[0])[: docs - 1].astype(jnp.int32)
    meta = jnp.concatenate([doc_ends, jnp.stack(query_starts + key_starts).astype(jnp.int32)])

    gain_attn = pack_1[:, 3 * wide].astype(jnp.float32)
    w_q, w_k, w_v = (pack_1[:, i * wide : (i + 1) * wide] for i in range(3))
    turn = turn_matrix(wide)
    w_q2 = jnp.concatenate([w_q, mm(w_q, turn).astype(bf16)], 1)
    w_k3 = jnp.concatenate([w_k, mm(w_k, turn).astype(bf16), w_v], 1)
    everything = jnp.concatenate(chunks, 0).astype(jnp.float32)
    normed_all = layer_norm(everything, gain_attn).astype(bf16)
    raw_k = mm(normed_all, w_k3)
    raw_q = mm(query_rows(normed_all), w_q2)
    cosine_q, sine_q = query_rows(cosine), query_rows(sine)
    query = (raw_q[:, :wide] * cosine_q + raw_q[:, wide:] * sine_q).astype(bf16)
    key = (raw_k[:, :wide] * cosine + raw_k[:, wide : 2 * wide] * sine).astype(bf16)
    value = raw_k[:, 2 * wide :].astype(bf16)

    out, log_total = attend_call(meta, query[None], key[None], value[None], docs, q_rows, k_rows)

    steps = [(a, b) for b in range(2) for a in range(2)]

    def forth(a, b):
        return lambda c, x, h: (h ^ a, x ^ b, c)

    def back(a, b):
        return lambda c, x, h: (h, x ^ b, c ^ a)

    out_parts = out.reshape(2, 2, block, wide)
    arrived = [plane_permute(pick(out_parts, pick_core ^ a, 0)[b], forth(a, b)) for a, b in steps]
    arrived = jnp.stack(arrived).reshape(2, 2, block, wide)
    attended = jnp.concatenate(
        [pick(pick(arrived, (g // 2) ^ x, 0), (g % 2) ^ c, 0) for g in range(4)], 1
    )

    tokens_f = own.astype(jnp.float32)
    grad_out = cotangent[0]
    hidden = tokens_f + mm(attended, w_o)
    normed_mf, norm_pull_mlp = jax.vjp(layer_norm, hidden, gain_mlp)
    normed_m = normed_mf.astype(bf16)
    gated_f, gate_pull = jax.vjp(gated_gelu, mm(normed_m, w_a), mm(normed_m, w_b))
    gated = gated_f.astype(bf16)
    layer_out = (hidden + mm_nt(gated, w_dt)).astype(bf16)
    grad_a, grad_b = gate_pull(mm(grad_out, w_dt))
    grad_a, grad_b = grad_a.astype(bf16), grad_b.astype(bf16)
    grad_normed_m = mm_nt(grad_a, w_a) + mm_nt(grad_b, w_b)
    grad_hidden_norm, d_gain_mlp = norm_pull_mlp(grad_normed_m)
    grad_hidden = grad_out.astype(jnp.float32) + grad_hidden_norm
    grad_branch = grad_hidden.astype(bf16)
    grad_mixed = mm_nt(grad_branch, w_o).astype(bf16)

    grad_groups = grad_mixed.reshape(block, 2, 2, wide)
    grad_parts = [
        plane_permute(pick(pick(grad_groups, x ^ b, 1), c ^ a, 1), back(a, b)) for a, b in steps
    ]
    grad_parts = jnp.stack(grad_parts).reshape(2, 2, block, wide)
    grad_items = jnp.stack(
        [jnp.stack([pick(grad_parts[b], pick_core ^ dc, 0) for b in range(2)]) for dc in range(2)]
    ).reshape(1, 4 * block, wide)

    d_a = mm_tn(normed_m, grad_a).astype(bf16)
    d_b = mm_tn(normed_m, grad_b).astype(bf16)
    d_dt = mm_tn(grad_out, gated).astype(bf16)
    d_o = mm_tn(attended, grad_branch).astype(bf16)
    d_o = d_o.reshape(row_parts, 4, rows // 4, 4, wide)
    packs = []
    for place, flip in enumerate(slice_flips):
        at = slice(place * ff, (place + 1) * ff)
        o_part = pick(d_o, t ^ flip, 1).reshape(row_parts * rows, wide)
        gain_part = jnp.broadcast_to(d_gain_mlp.astype(bf16)[:, None], (width, 96))
        packs.append(jnp.concatenate([d_a[:, at], d_b[:, at], d_dt[:, at], o_part, gain_part], 1))

    def add(one, two):
        return (one.astype(jnp.float32) + two.astype(jnp.float32)).astype(bf16)

    packs = [add(packs[0], tensor_permute(packs[2], 1)), add(packs[1], tensor_permute(packs[3], 1))]
    pack = add(packs[0], tensor_permute(packs[1], 2))
    pack = lax.all_to_all(pack.reshape(row_parts, rows, -1), ROWS, split_axis=0, concat_axis=0, tiled=True)
    pack = pack.astype(jnp.float32).sum(0)
    d_in = pack[:, : 2 * ff].reshape(rows, 2, ff)
    d_down = pack[:, 2 * ff : 3 * ff].T
    d_attn_out = pack[:, 3 * ff : 3 * ff + wide].reshape(rows // 4, width)
    d_gain_mlp = pick(pack[:, 3 * ff + wide].reshape(4, rows // 4), t, 0)

    grad_query, grad_key, grad_value = attend_back_call(
        meta, query[None], key[None], value[None], out, grad_items, log_total, docs, q_rows, k_rows
    )

    def turn_back(grad, cos, sin):
        return (grad.astype(jnp.float32) * cos + mm_nt(grad, turn) * sin).astype(bf16)

    grad_q = turn_back(grad_query[0], cosine_q, sine_q).reshape(4, 1, block, wide)
    grad_q = lax.dynamic_update_slice_in_dim(
        jnp.zeros((4, 2, block, wide), bf16), grad_q, pick_core, 1
    ).reshape(8 * block, wide)
    grad_k = turn_back(grad_key[0], cosine, sine)
    grad_raw = jnp.concatenate([grad_q, grad_k, grad_value[0]], 1)
    w_group = pack_1[:, : 3 * wide]
    partial = mm_nt(grad_raw, w_group).astype(bf16).reshape(4, 2, block, width)
    d_qkv = mm_tn(normed_all, grad_raw).astype(bf16)

    chip_sum = add(partial[:, 0], tensor_permute(partial[:, 1], 1))
    sent = [
        tensor_permute(chip_sum[1], 2),
        plane_permute(chip_sum[2], lambda c, x, h: (1 - c, x, h)),
        plane_permute(chip_sum[3], lambda c, x, h: (1 - c, 1 - x, h)),
    ]
    d_qkv = lax.all_to_all(d_qkv.reshape(row_parts, rows, -1), ROWS, split_axis=0, concat_axis=0, tiled=True)
    d_qkv = d_qkv.astype(jnp.float32).sum(0).astype(bf16)
    d_qkv = lax.all_to_all(d_qkv.reshape(4, rows // 4, 3 * wide), "tensor", split_axis=0, concat_axis=0, tiled=True)
    d_qkv = d_qkv.reshape(4, rows // 4, 3, wide).transpose(1, 2, 0, 3).reshape(rows // 4, 3 * width)
    d_qkv = d_qkv.astype(jnp.float32)
    own_rows = pick(w_qkv.reshape(4, rows // 4, 3 * width), t, 0).astype(jnp.float32)
    own_gain = pick(attn_gain.reshape(4, rows // 4), t, 0).astype(jnp.float32)
    d_gain_attn = jnp.sum(d_qkv * own_rows, 1) / own_gain

    grad_normed = chip_sum[0].astype(jnp.float32)
    for part in sent:
        grad_normed = grad_normed + part.astype(jnp.float32)
    _, norm_pull_attn = jax.vjp(lambda values: layer_norm(values, gain_attn), tokens_f)
    grad_tokens = grad_hidden + norm_pull_attn(grad_normed)[0]
    return (layer_out[None], grad_tokens[None], d_gain_attn, d_gain_mlp, d_qkv, d_attn_out, d_in, d_down)


def solution(mesh):
    return jax.shard_map(
        local,
        mesh=mesh,
        in_specs=(
            P("shard", ("ctx", "tensor"), None),
            P("shard", None),
            P(("shard", "ctx")),
            P(("shard", "ctx")),
            P(("shard", "ctx"), None),
            P(("shard", "ctx"), None),
            P(("shard", "ctx"), None, "tensor"),
            P("tensor", ("shard", "ctx")),
            P("shard", ("ctx", "tensor"), None),
        ),
        out_specs=(
            P("shard", ("ctx", "tensor"), None),
            P("shard", ("ctx", "tensor"), None),
            P(("shard", "ctx", "tensor")),
            P(("shard", "ctx", "tensor")),
            P(("shard", "ctx", "tensor"), None),
            P(("shard", "ctx", "tensor"), None),
            P(("shard", "ctx"), None, "tensor"),
            P("tensor", ("shard", "ctx")),
        ),
        check_vma=False,
    )
```

```python
import functools

import jax
import jax.numpy as jnp
from jax import lax
from jax.experimental import pallas as pl
from jax.experimental.pallas import tpu as pltpu
from jax.sharding import PartitionSpec as P

HEAD_DIM = 64
EPSILON = 1e-05
ROPE_THETA = 160000.0
SCORE_SCALE = 0.125
MASKED_SCORE = -1e30
ROOT_HALF = 0.7071067811865476
INVERSE_ROOT_TAU = 0.3989422804014327
VMEM_LIMIT = 56 * 1024 * 1024

NT = (((1,), (1,)), ((), ()))
NN = (((1,), (0,)), ((), ()))


def dot(a, b, dims):
    return lax.dot_general(a, b, dims, preferred_element_type=jnp.float32)


def seg_of(position, ends):
    seg = (position >= ends[0]).astype(jnp.int32)
    for end in ends[1:]:
        seg = seg + (position >= end).astype(jnp.int32)
    return seg


def stack_heads(values, group):
    lane_head = lax.broadcasted_iota(jnp.int32, values.shape, 1) // HEAD_DIM
    return jnp.concatenate(
        [jnp.where(lane_head == h, values, jnp.zeros_like(values)) for h in range(group)], 0
    )


def each_key_block(meta, docs, q_at, q_rows, k_first, k_rows, k_blocks, group, body):
    ends = [meta[i] for i in range(docs - 1)]
    q_lo, q_hi = seg_of(q_at, ends), seg_of(q_at + q_rows - 1, ends)
    q_seg = seg_of(q_at + lax.broadcasted_iota(jnp.int32, (1, q_rows), 1), ends)
    q_seg = jnp.concatenate([q_seg] * group, 1)

    def step(j, carry):
        k_at = meta[k_first + j]
        k_lo, k_hi = seg_of(k_at, ends), seg_of(k_at + k_rows - 1, ends)
        meets = (k_lo <= q_hi) & (q_lo <= k_hi)
        same = (k_lo == k_hi) & (q_lo == q_hi)

        @pl.when(meets & same)
        def _():
            body(j, None)

        @pl.when(meets & jnp.logical_not(same))
        def _():
            k_seg = seg_of(k_at + lax.broadcasted_iota(jnp.int32, (k_rows, 1), 0), ends)
            body(j, k_seg == q_seg)

        return carry

    lax.fori_loop(0, k_blocks, step, 0)


def attend_kernel(docs, k_rows, meta, q_ref, k_ref, v_ref, o_ref, lse_ref, vt_ref, m_ref, l_ref, acc_ref):
    q_rows, wide = q_ref.shape[1], q_ref.shape[2]
    group = wide // HEAD_DIM
    k_blocks = k_ref.shape[1] // k_rows
    q_blocks = pl.num_programs(1)
    i = pl.program_id(1)

    @pl.when(i == 0)
    def _():
        for j in range(k_blocks):
            at = pl.ds(j * k_rows, k_rows)
            vt_ref[:, at] = v_ref[0, at, :].T

    q_st = stack_heads(q_ref[0] * SCORE_SCALE, group)
    m_ref[...] = jnp.full(m_ref.shape, MASKED_SCORE, jnp.float32)
    l_ref[...] = jnp.zeros_like(l_ref)
    acc_ref[...] = jnp.zeros_like(acc_ref)

    def body(j, mask):
        at = pl.ds(pl.multiple_of(j * k_rows, k_rows), k_rows)
        scores = dot(k_ref[0, at, :], q_st, NT)
        if mask is not None:
            scores = jnp.where(mask, scores, MASKED_SCORE)
        m_old = m_ref[...]
        m_new = jnp.maximum(m_old, jnp.max(scores, 0, keepdims=True))
        shrink = jnp.exp(m_old - m_new)
        weights = jnp.exp(scores - m_new)
        if mask is not None:
            weights = jnp.where(mask, weights, 0.0)
        m_ref[...] = m_new
        l_ref[...] = l_ref[...] * shrink + jnp.sum(weights, 0, keepdims=True)
        low = weights.astype(jnp.bfloat16)
        for h in range(group):
            rows = pl.ds(h * HEAD_DIM, HEAD_DIM)
            cols = slice(h * q_rows, (h + 1) * q_rows)
            acc_ref[rows, :] = acc_ref[rows, :] * shrink[:, cols] + dot(vt_ref[rows, at], low[:, cols], NN)

    each_key_block(meta, docs, meta[docs - 1 + i], q_rows, docs - 1 + q_blocks, k_rows, k_blocks, group, body)
    total = l_ref[...]
    outs = []
    for h in range(group):
        cols = slice(h * q_rows, (h + 1) * q_rows)
        outs.append(acc_ref[h * HEAD_DIM : (h + 1) * HEAD_DIM, :] / total[:, cols])
    o_ref[0] = jnp.concatenate(outs, 0).T.astype(jnp.bfloat16)
    lse_ref[0, 0] = m_ref[...] + jnp.log(total)


def attend_back_kernel(
    docs, k_rows, meta, q_ref, k_ref, v_ref, o_ref, do_ref, lse_ref, dq_ref, dk_ref, dv_ref,
    kt_ref, dqt_ref, dk_acc, dv_acc,
):
    q_rows, wide = q_ref.shape[1], q_ref.shape[2]
    group = wide // HEAD_DIM
    k_blocks = k_ref.shape[1] // k_rows
    q_blocks = pl.num_programs(1)
    i = pl.program_id(1)

    @pl.when(i == 0)
    def _():
        dk_acc[...] = jnp.zeros_like(dk_acc)
        dv_acc[...] = jnp.zeros_like(dv_acc)
        for j in range(k_blocks):
            at = pl.ds(j * k_rows, k_rows)
            kt_ref[:, at] = k_ref[0, at, :].T

    q_st = stack_heads(q_ref[0] * SCORE_SCALE, group)
    grad_out = do_ref[0]
    do_st = stack_heads(grad_out, group)
    product = (grad_out.astype(jnp.float32) * o_ref[0].astype(jnp.float32)).T
    delta = jnp.concatenate(
        [jnp.sum(product[h * HEAD_DIM : (h + 1) * HEAD_DIM], 0, keepdims=True) for h in range(group)], 1
    )
    log_total = lse_ref[0, 0]
    dqt_ref[...] = jnp.zeros_like(dqt_ref)

    def body(j, mask):
        at = pl.ds(pl.multiple_of(j * k_rows, k_rows), k_rows)
        scores = dot(k_ref[0, at, :], q_st, NT)
        if mask is not None:
            scores = jnp.where(mask, scores, MASKED_SCORE)
        probs = jnp.exp(scores - log_total)
        dv_acc[at, :] += dot(probs.astype(jnp.bfloat16), do_st, NN)
        grad_probs = dot(v_ref[0, at, :], do_st, NT)
        grad_scores = (probs * (grad_probs - delta)).astype(jnp.bfloat16)
        dk_acc[at, :] += dot(grad_scores, q_st, NN)
        for h in range(group):
            rows = pl.ds(h * HEAD_DIM, HEAD_DIM)
            cols = slice(h * q_rows, (h + 1) * q_rows)
            dqt_ref[rows, :] += dot(kt_ref[rows, at], grad_scores[:, cols], NN)

    each_key_block(meta, docs, meta[docs - 1 + i], q_rows, docs - 1 + q_blocks, k_rows, k_blocks, group, body)
    dq_ref[0] = (dqt_ref[...].T * SCORE_SCALE).astype(jnp.bfloat16)

    @pl.when(i == q_blocks - 1)
    def _():
        dk_ref[0] = dk_acc[...].astype(jnp.bfloat16)
        dv_ref[0] = dv_acc[...].astype(jnp.bfloat16)


def attend_call(meta, query, key, value, docs, q_rows, k_rows):
    items, length, wide = query.shape
    keys = key.shape[1]
    group = wide // HEAD_DIM
    q_blocks = length // q_rows
    block = pl.BlockSpec((1, q_rows, wide), lambda g, i, m: (g, i, 0))
    whole = pl.BlockSpec((1, keys, wide), lambda g, i, m: (g, 0, 0))
    stat = pl.BlockSpec((1, 1, 1, group * q_rows), lambda g, i, m: (g, i, 0, 0))
    return pl.pallas_call(
        functools.partial(attend_kernel, docs, k_rows),
        grid_spec=pltpu.PrefetchScalarGridSpec(
            num_scalar_prefetch=1,
            grid=(items, q_blocks),
            in_specs=[block, whole, whole],
            out_specs=[block, stat],
            scratch_shapes=[
                pltpu.VMEM((wide, keys), jnp.bfloat16),
                pltpu.VMEM((1, group * q_rows), jnp.float32),
                pltpu.VMEM((1, group * q_rows), jnp.float32),
                pltpu.VMEM((wide, q_rows), jnp.float32),
            ],
        ),
        out_shape=[
            jax.ShapeDtypeStruct(query.shape, jnp.bfloat16),
            jax.ShapeDtypeStruct((items, q_blocks, 1, group * q_rows), jnp.float32),
        ],
        compiler_params=pltpu.CompilerParams(vmem_limit_bytes=VMEM_LIMIT),
        name="attend",
    )(meta, query, key, value)


def attend_back_call(meta, query, key, value, out, grad_out, log_total, docs, q_rows, k_rows):
    items, length, wide = query.shape
    keys = key.shape[1]
    group = wide // HEAD_DIM
    q_blocks = length // q_rows
    block = pl.BlockSpec((1, q_rows, wide), lambda g, i, m: (g, i, 0))
    whole = pl.BlockSpec((1, keys, wide), lambda g, i, m: (g, 0, 0))
    stat = pl.BlockSpec((1, 1, 1, group * q_rows), lambda g, i, m: (g, i, 0, 0))
    return pl.pallas_call(
        functools.partial(attend_back_kernel, docs, k_rows),
        grid_spec=pltpu.PrefetchScalarGridSpec(
            num_scalar_prefetch=1,
            grid=(items, q_blocks),
            in_specs=[block, whole, whole, block, block, stat],
            out_specs=[block, whole, whole],
            scratch_shapes=[
                pltpu.VMEM((wide, keys), jnp.bfloat16),
                pltpu.VMEM((wide, q_rows), jnp.float32),
                pltpu.VMEM((keys, wide), jnp.float32),
                pltpu.VMEM((keys, wide), jnp.float32),
            ],
        ),
        out_shape=[
            jax.ShapeDtypeStruct(query.shape, jnp.bfloat16),
            jax.ShapeDtypeStruct(key.shape, jnp.bfloat16),
            jax.ShapeDtypeStruct(key.shape, jnp.bfloat16),
        ],
        compiler_params=pltpu.CompilerParams(vmem_limit_bytes=VMEM_LIMIT),
        name="attend_back",
    )(meta, query, key, value, out, grad_out, log_total)


def layer_norm(values, gain):
    mean_value = jnp.mean(values, -1, keepdims=True)
    centred = values - mean_value
    spread = jnp.mean(centred * centred, -1, keepdims=True)
    return centred * lax.rsqrt(spread + EPSILON) * gain


def norm_parts(values):
    centred = values - jnp.mean(values, -1, keepdims=True)
    inverse = lax.rsqrt(jnp.mean(centred * centred, -1, keepdims=True) + EPSILON)
    return centred * inverse, inverse


def turn_matrix(width):
    row = lax.broadcasted_iota(jnp.int32, (width, width), 0)
    col = lax.broadcasted_iota(jnp.int32, (width, width), 1)
    half = HEAD_DIM // 2
    first = (col % HEAD_DIM) < half
    plus = jnp.logical_not(first) & (row == col - half)
    minus = first & (row == col + half)
    return plus.astype(jnp.bfloat16) - minus.astype(jnp.bfloat16)


def angles(positions, width):
    half = HEAD_DIM // 2
    steps_index = (jnp.arange(width) % half).astype(jnp.float32)
    inverse = ROPE_THETA ** (-2.0 * steps_index / HEAD_DIM)
    return positions.astype(jnp.float32)[:, None] * inverse[None, :]


def turned_tables(cos_row, sin_row, base):
    cos_base, sin_base = base[0:1, :], base[1:2, :]
    return cos_row * cos_base - sin_row * sin_base, sin_row * cos_base + cos_row * sin_base


def full(shape):
    return pl.BlockSpec(shape, lambda *_: (0,) * len(shape))


def padded(wide):
    return -(-wide // 128) * 128


def project_kernel(meta, *refs):
    chunk_refs = refs[:8]
    w_ref, turn_ref, cos_ref, sin_ref, base_ref, normed_ref, q_ref, k_ref, v_ref, x_ref, w_all, gain_row = refs[8:]
    wide = q_ref.shape[2]
    slot = padded(wide)
    i = pl.program_id(0)
    bf16 = jnp.bfloat16

    @pl.when(i == 0)
    def _():
        for p, at in ((1, 0), (2, 2), (0, 3)):
            w_all[:, at * slot : at * slot + wide] = w_ref[:, p * wide : (p + 1) * wide]
        for p, at in ((1, 1), (0, 4)):
            turned = dot(w_ref[:, p * wide : (p + 1) * wide], turn_ref[...], NN)
            w_all[:, at * slot : at * slot + wide] = turned.astype(bf16)
        last = w_ref[:, w_ref.shape[1] - 128 :].astype(jnp.float32).T
        gain_row[...] = last[127:128, :]

    for n in range(8):
        @pl.when(i == n)
        def _(n=n):
            x_ref[...] = chunk_refs[n][...]

    normed, _ = norm_parts(x_ref[...].astype(jnp.float32))
    normed = (normed * gain_row[...]).astype(bf16)
    normed_ref[0] = normed
    cos, sin = turned_tables(cos_ref[...], sin_ref[...], base_ref[0])
    raw = dot(normed, w_all[:, : 3 * slot], NN)
    k_ref[0] = (raw[:, :wide] * cos + raw[:, slot : slot + wide] * sin).astype(bf16)
    v_ref[0] = raw[:, 2 * slot : 2 * slot + wide].astype(bf16)

    @pl.when(i % 2 == meta[0])
    def _():
        raw_q = dot(normed, w_all[:, 3 * slot : 5 * slot], NN)
        q_ref[0] = (raw_q[:, :wide] * cos + raw_q[:, slot : slot + wide] * sin).astype(bf16)


def project_call(meta, chunks, w, turn, cos_row, sin_row, bases, wide):
    block, width = chunks[0].shape
    bf16 = jnp.bfloat16
    one = lambda i, m: (i, 0, 0)
    return pl.pallas_call(
        project_kernel,
        grid_spec=pltpu.PrefetchScalarGridSpec(
            num_scalar_prefetch=1,
            grid=(8,),
            in_specs=[full((block, width))] * 8
            + [full(w.shape), full(turn.shape), full(cos_row.shape), full(sin_row.shape), pl.BlockSpec((1, 2, wide), one)],
            out_specs=[
                pl.BlockSpec((1, block, width), one),
                pl.BlockSpec((1, block, wide), lambda i, m: (i // 2, 0, 0)),
                pl.BlockSpec((1, block, wide), one),
                pl.BlockSpec((1, block, wide), one),
            ],
            scratch_shapes=[
                pltpu.VMEM((block, width), bf16),
                pltpu.VMEM((width, 5 * padded(wide)), bf16),
                pltpu.VMEM((1, width), jnp.float32),
            ],
        ),
        out_shape=[
            jax.ShapeDtypeStruct((8, block, width), bf16),
            jax.ShapeDtypeStruct((4, block, wide), bf16),
            jax.ShapeDtypeStruct((8, block, wide), bf16),
            jax.ShapeDtypeStruct((8, block, wide), bf16),
        ],
        compiler_params=pltpu.CompilerParams(vmem_limit_bytes=VMEM_LIMIT),
        name="project",
    )(meta, *chunks, w, turn, cos_row, sin_row, bases)


def feed_kernel(ff, meta, *refs):
    parts, slices = refs[0:4], refs[4:8]
    tok_ref, cot_ref = refs[8:10]
    out_ref, gh_ref, normed_ref, att_ref, gated_ref, ga_ref, gb_ref, gbr_ref, dgain_ref = refs[10:19]
    grad_parts = refs[19:23]
    w_a, w_b, w_dt, w_o, gain_row, att_scr = refs[23:29]
    wide = parts[0].shape[1]
    i = pl.program_id(0)
    bf16 = jnp.bfloat16

    @pl.when(i == 0)
    def _():
        for n in range(4):
            at = slice(n * ff, (n + 1) * ff)
            w_a[:, at] = slices[n][:, :ff]
            w_b[:, at] = slices[n][:, ff : 2 * ff]
            w_dt[:, at] = slices[n][:, 2 * ff : 3 * ff]
            for g in range(4):
                @pl.when(meta[n] == g)
                def _(n=n, g=g):
                    w_o[:, g * wide : (g + 1) * wide] = slices[n][:, 3 * ff : 3 * ff + wide]
        last = slices[0][:, slices[0].shape[1] - 128 :].astype(jnp.float32).T
        gain_row[...] = last[127:128, :]
        dgain_ref[...] = jnp.zeros_like(dgain_ref)

    for g in range(4):
        for n in range(4):
            @pl.when(meta[4 + n] == g)
            def _(n=n, g=g):
                att_scr[:, g * wide : (g + 1) * wide] = parts[n][...]

    attended = att_scr[...]
    att_ref[...] = attended
    gain = gain_row[...]
    hidden = tok_ref[...].astype(jnp.float32) + dot(attended, w_o[...], NN)
    normal, inverse = norm_parts(hidden)
    normed = (normal * gain).astype(bf16)
    normed_ref[...] = normed
    half_a = dot(normed, w_a[...], NN)
    half_b = dot(normed, w_b[...], NN)
    phi = 0.5 * (1.0 + lax.erf(half_a * ROOT_HALF))
    gelu = half_a * phi
    slope = phi + half_a * (jnp.exp(-0.5 * half_a * half_a) * INVERSE_ROOT_TAU)
    gated = (gelu * half_b).astype(bf16)
    out_ref[...] = (hidden + dot(gated, w_dt[...], NT)).astype(bf16)
    cot = cot_ref[...]
    grad_gated = dot(cot, w_dt[...], NN)
    grad_a = (grad_gated * half_b * slope).astype(bf16)
    grad_b = (grad_gated * gelu).astype(bf16)
    for n in range(4):
        at = slice(n * ff, (n + 1) * ff)
        gated_ref[n] = gated[:, at]
        ga_ref[n] = grad_a[:, at]
        gb_ref[n] = grad_b[:, at]
    grad_normed = dot(grad_a, w_a[...], NT) + dot(grad_b, w_b[...], NT)
    dgain_ref[...] += jnp.sum(grad_normed * normal, 0, keepdims=True)
    scaled = grad_normed * gain
    inner = jnp.mean(scaled * normal, -1, keepdims=True)
    grad_hidden = cot.astype(jnp.float32) + inverse * (
        scaled - jnp.mean(scaled, -1, keepdims=True) - normal * inner
    )
    gh_ref[...] = grad_hidden
    grad_branch = grad_hidden.astype(bf16)
    for g in range(4):
        gbr_ref[g] = grad_branch[:, g * wide : (g + 1) * wide]
    grad_mixed = dot(grad_branch, w_o[...], NT).astype(bf16)
    for g in range(4):
        for n in range(4):
            @pl.when(meta[4 + n] == g)
            def _(n=n, g=g):
                grad_parts[n][...] = grad_mixed[:, g * wide : (g + 1) * wide]


def feed_call(meta, parts, slices, tokens, cotangent, ff):
    block, width = tokens.shape
    wide = parts[0].shape[1]
    bf16, f32 = jnp.bfloat16, jnp.float32
    rows = min(256, block)
    part = pl.BlockSpec((rows, wide), lambda i, m: (i, 0))
    row = pl.BlockSpec((rows, width), lambda i, m: (i, 0))
    hid = pl.BlockSpec((4, rows, ff), lambda i, m: (0, i, 0))
    grp = pl.BlockSpec((4, rows, wide), lambda i, m: (0, i, 0))
    sds = jax.ShapeDtypeStruct
    return pl.pallas_call(
        functools.partial(feed_kernel, ff),
        grid_spec=pltpu.PrefetchScalarGridSpec(
            num_scalar_prefetch=1,
            grid=(block // rows,),
            in_specs=[part] * 4 + [full(slices[0].shape)] * 4 + [row, row],
            out_specs=[row, row, row, row, hid, hid, hid, grp, full((1, width))] + [part] * 4,
            scratch_shapes=[pltpu.VMEM((width, 4 * ff), bf16)] * 3
            + [pltpu.VMEM((width, width), bf16), pltpu.VMEM((1, width), f32), pltpu.VMEM((rows, width), bf16)],
        ),
        out_shape=[
            sds((block, width), bf16),
            sds((block, width), f32),
            sds((block, width), bf16),
            sds((block, width), bf16),
            sds((4, block, ff), bf16),
            sds((4, block, ff), bf16),
            sds((4, block, ff), bf16),
            sds((4, block, wide), bf16),
            sds((1, width), f32),
        ]
        + [sds((block, wide), bf16)] * 4,
        compiler_params=pltpu.CompilerParams(vmem_limit_bytes=VMEM_LIMIT),
        name="feed",
    )(meta, *parts, *slices, tokens, cotangent)


def pack_kernel(meta, nm_ref, cot_ref, att_ref, ga_ref, gb_ref, gated_ref, gbr_ref, dgain_ref, out_ref, nm_t, cot_t, att_t):
    ff, wide = ga_ref.shape[2], gbr_ref.shape[2]
    bf16 = jnp.bfloat16

    @pl.when(pl.program_id(0) == 0)
    def _():
        nm_t[...] = nm_ref[...].T
        cot_t[...] = cot_ref[...].T
        att_t[...] = att_ref[...].T

    width = nm_t.shape[0]
    gain = jnp.broadcast_to(dgain_ref[...], (128, width)).T
    last = out_ref.shape[2] - (3 * ff + wide)
    out_ref[0] = jnp.concatenate(
        [
            dot(nm_t[...], ga_ref[0], NN),
            dot(nm_t[...], gb_ref[0], NN),
            dot(cot_t[...], gated_ref[0], NN),
            dot(att_t[...], gbr_ref[0], NN),
            gain[:, :last],
        ],
        1,
    ).astype(bf16)


def pack_call(meta, normed, cotangent, attended, grad_a, grad_b, gated, grad_branch, d_gain, first):
    block, width = normed.shape
    ff, wide = grad_a.shape[2], grad_branch.shape[2]
    bf16 = jnp.bfloat16
    packed = padded(3 * ff + wide + 1)
    hid = pl.BlockSpec((1, block, ff), lambda i, m: (first + i, 0, 0))
    return pl.pallas_call(
        pack_kernel,
        grid_spec=pltpu.PrefetchScalarGridSpec(
            num_scalar_prefetch=1,
            grid=(2,),
            in_specs=[full((block, width))] * 3
            + [hid] * 3
            + [pl.BlockSpec((1, block, wide), lambda i, m: (m[first + i], 0, 0)), full((1, width))],
            out_specs=pl.BlockSpec((1, width, packed), lambda i, m: (i, 0, 0)),
            scratch_shapes=[pltpu.VMEM((width, block), bf16)] * 3,
        ),
        out_shape=jax.ShapeDtypeStruct((2, width, packed), bf16),
        compiler_params=pltpu.CompilerParams(vmem_limit_bytes=VMEM_LIMIT),
        name="pack",
    )(meta, normed, cotangent, attended, grad_a, grad_b, gated, grad_branch, d_gain)


def unproject_kernel(
    core, meta, normed_ref, dq_ref, dk_ref, dv_ref, w_ref, turn_ref, cos_ref, sin_ref, base_ref, before_ref,
    partial_ref, dw_ref, raw_ref,
):
    wide = dk_ref.shape[2]
    i = pl.program_id(0)
    bf16 = jnp.bfloat16

    @pl.when(i == 0)
    def _():
        dw_ref[...] = before_ref[...]

    cos, sin = turned_tables(cos_ref[...], sin_ref[...], base_ref[0])

    def turn_back(grad):
        return (grad.astype(jnp.float32) * cos + dot(grad, turn_ref[...], NT) * sin).astype(bf16)

    mine = meta[0] == core
    raw_ref[:, wide : 2 * wide] = turn_back(dk_ref[0])
    raw_ref[:, 2 * wide : 3 * wide] = dv_ref[0]

    @pl.when(mine)
    def _():
        raw_ref[:, :wide] = turn_back(dq_ref[0])

    @pl.when(jnp.logical_not(mine))
    def _():
        raw_ref[:, :wide] = jnp.zeros_like(dk_ref[0])

    raw = raw_ref[...]
    partial_ref[0] = dot(raw, w_ref[:, : 3 * wide], NT).astype(bf16)
    dw_ref[...] += lax.dot_general(
        normed_ref[0], raw, (((0,), (0,)), ((), ())), preferred_element_type=jnp.float32
    )


def unproject_call(core, meta, normed, dq, dk, dv, w, turn, cos_row, sin_row, bases, before):
    _, block, width = normed.shape
    wide = dk.shape[2]
    chunk = lambda i, m: (2 * i + core, 0, 0)
    one = lambda i, m: (i, 0, 0)
    return pl.pallas_call(
        functools.partial(unproject_kernel, core),
        grid_spec=pltpu.PrefetchScalarGridSpec(
            num_scalar_prefetch=1,
            grid=(4,),
            in_specs=[
                pl.BlockSpec((1, block, width), chunk),
                pl.BlockSpec((1, block, wide), one),
                pl.BlockSpec((1, block, wide), chunk),
                pl.BlockSpec((1, block, wide), chunk),
                full(w.shape),
                full(turn.shape),
                full(cos_row.shape),
                full(sin_row.shape),
                pl.BlockSpec((1, 2, wide), chunk),
                full((width, 3 * wide)),
            ],
            out_specs=[pl.BlockSpec((1, block, width), one), full((width, 3 * wide))],
            scratch_shapes=[pltpu.VMEM((block, 3 * wide), jnp.bfloat16)],
        ),
        out_shape=[
            jax.ShapeDtypeStruct((4, block, width), jnp.bfloat16),
            jax.ShapeDtypeStruct((width, 3 * wide), jnp.float32),
        ],
        compiler_params=pltpu.CompilerParams(vmem_limit_bytes=VMEM_LIMIT),
        name="unproject",
    )(meta, normed, dq, dk, dv, w, turn, cos_row, sin_row, bases, before)


PLANE = ("ctx", "tensor")
ROWS = ("shard", "ctx")


def plane_permute(array, target):
    pairs = []
    for c in range(2):
        for x in range(2):
            for h in range(2):
                to_c, to_x, to_h = target(c, x, h)
                pairs.append((c * 4 + x * 2 + h, to_c * 4 + to_x * 2 + to_h))
    return lax.ppermute(array, PLANE, pairs)


def tensor_permute(array, flip):
    return lax.ppermute(array, "tensor", [(t, t ^ flip) for t in range(4)])


def pick(array, index, axis):
    return lax.dynamic_index_in_dim(array, index, axis, keepdims=False)


def local(tokens, doc_lengths, attn_gain, mlp_gain, w_qkv, w_attn_out, w_in, w_down, cotangent):
    _, block, width = tokens.shape
    assert lax.axis_size("ctx") == 2 and lax.axis_size("tensor") == 4 and tokens.shape[0] == 1
    row_parts = lax.axis_size("shard") * 2
    rows = w_qkv.shape[0]
    ff = w_in.shape[2]
    docs = doc_lengths.shape[1]
    c = lax.axis_index("ctx")
    t = lax.axis_index("tensor")
    x, h = t // 2, t % 2
    wide = width // 4
    bf16 = jnp.bfloat16

    own = tokens[0]
    by_x = tensor_permute(own, 2)
    by_y = plane_permute(own, lambda c, x, h: (1 - c, x, h))
    by_xy = plane_permute(own, lambda c, x, h: (1 - c, 1 - x, h))
    chunks = []
    for part in (own, by_x, by_y, by_xy):
        chunks += [part, tensor_permute(part, 1)]

    group_cols = pick(w_qkv.reshape(rows, 3, 4, wide), t, 2).reshape(rows, 3 * wide)
    gain_cols = padded(3 * wide + 1) - 3 * wide
    pack_1 = jnp.concatenate([group_cols, jnp.broadcast_to(attn_gain[:, None], (rows, gain_cols))], 1)
    pack_1 = lax.all_gather(pack_1, ROWS, axis=0, tiled=True)
    own_cols = pick(w_attn_out.reshape(rows, 4, wide), t, 1)
    gain_cols = padded(3 * ff + wide + 1) - 3 * ff - wide
    pack_2 = jnp.concatenate(
        [w_in.reshape(rows, 2 * ff), w_down.T, own_cols, jnp.broadcast_to(mlp_gain[:, None], (rows, gain_cols))], 1
    )
    pack_2 = lax.all_gather(pack_2, ROWS, axis=0, tiled=True)
    slices = [pack_2, tensor_permute(pack_2, 2)]
    slices += [tensor_permute(slices[0], 1), tensor_permute(slices[1], 1)]
    slice_flips = (0, 2, 1, 3)

    chunk_at = []
    for dc in range(2):
        for dx in range(2):
            for dh in range(2):
                chunk_at.append(((c ^ dc) * 4 + (x ^ dx) * 2 + (h ^ dh)) * block)
    row_angles = angles(jnp.arange(block), wide)
    base_angles = angles(jnp.stack(chunk_at), wide)
    cos_row, sin_row = jnp.cos(row_angles), jnp.sin(row_angles)
    bases = jnp.stack([jnp.cos(base_angles), jnp.sin(base_angles)], 1)
    q_rows = min(512, block)
    k_rows = min(512, block)
    pick_core = h ^ c
    key_starts = [at + k * k_rows for at in chunk_at for k in range(block // k_rows)]
    query_starts = [
        ((c ^ dc) * 4 + (x ^ dx) * 2 + c) * block + k * q_rows
        for dc in range(2)
        for dx in range(2)
        for k in range(block // q_rows)
    ]
    doc_ends = jnp.cumsum(doc_lengths[0])[: docs - 1].astype(jnp.int32)
    meta = jnp.concatenate([doc_ends, jnp.stack(query_starts + key_starts).astype(jnp.int32)])
    core_meta = jnp.stack([pick_core]).astype(jnp.int32)
    steps = [(a, b) for b in range(2) for a in range(2)]
    feed_meta = jnp.stack(
        [t ^ flip for flip in slice_flips] + [(x ^ b) * 2 + (c ^ a) for a, b in steps]
    ).astype(jnp.int32)

    turn = turn_matrix(wide)
    normed_all, query, key, value = project_call(core_meta, chunks, pack_1, turn, cos_row, sin_row, bases, wide)
    query = query.reshape(1, 4 * block, wide)
    key = key.reshape(1, 8 * block, wide)
    value = value.reshape(1, 8 * block, wide)
    out, log_total = attend_call(meta, query, key, value, docs, q_rows, k_rows)

    def forth(a, b):
        return lambda c, x, h: (h ^ a, x ^ b, c)

    def back(a, b):
        return lambda c, x, h: (h, x ^ b, c ^ a)

    out_parts = out.reshape(2, 2, block, wide)
    arrived = [plane_permute(pick(out_parts, pick_core ^ a, 0)[b], forth(a, b)) for a, b in steps]

    (layer_out, grad_hidden, normed_m, attended, gated, grad_a, grad_b, grad_branch, d_gain_mlp, *grad_parts) = feed_call(
        feed_meta, arrived, slices, own, cotangent[0], ff
    )
    grad_parts = [plane_permute(part, back(a, b)) for part, (a, b) in zip(grad_parts, steps)]
    grad_parts = jnp.stack(grad_parts).reshape(2, 2, block, wide)
    grad_items = jnp.stack(
        [jnp.stack([pick(grad_parts[b], pick_core ^ dc, 0) for b in range(2)]) for dc in range(2)]
    ).reshape(1, 4 * block, wide)

    def add(one, two):
        return (one.astype(jnp.float32) + two.astype(jnp.float32)).astype(bf16)

    grads = (normed_m, cotangent[0], attended, grad_a, grad_b, gated, grad_branch, d_gain_mlp)
    sent_packs = tensor_permute(pack_call(feed_meta, *grads, 2), 1)
    packs = add(pack_call(feed_meta, *grads, 0), sent_packs)
    pack = add(packs[0], tensor_permute(packs[1], 2))
    pack = lax.all_to_all(pack.reshape(row_parts, rows, -1), ROWS, split_axis=0, concat_axis=0, tiled=True)
    pack = pack.astype(jnp.float32).sum(0)
    d_in = pack[:, : 2 * ff].reshape(rows, 2, ff)
    d_down = pack[:, 2 * ff : 3 * ff].T
    d_group_out = pack[:, 3 * ff : 3 * ff + wide].astype(bf16)
    d_gain_mlp = pick(pack[:, 3 * ff + wide].reshape(4, rows // 4), t, 0)

    grad_query, grad_key, grad_value = attend_back_call(
        meta, query, key, value, out, grad_items, log_total, docs, q_rows, k_rows
    )
    grad_query = grad_query.reshape(4, block, wide)
    grad_key = grad_key.reshape(8, block, wide)
    grad_value = grad_value.reshape(8, block, wide)
    d_qkv = jnp.zeros((width, 3 * wide), jnp.float32)
    partial = [None, None]
    for core in (1, 0):
        partial[core], d_qkv = unproject_call(
            core, core_meta, normed_all, grad_query, grad_key, grad_value, pack_1, turn, cos_row, sin_row, bases, d_qkv
        )

    from_core = tensor_permute(partial[1], 1)
    chip_sum = [add(partial[0][n], from_core[n]) for n in range(4)]
    sent = [
        tensor_permute(chip_sum[1], 2),
        plane_permute(chip_sum[2], lambda c, x, h: (1 - c, x, h)),
        plane_permute(chip_sum[3], lambda c, x, h: (1 - c, 1 - x, h)),
    ]
    d_qkv = d_qkv.astype(bf16).reshape(row_parts, rows, -1)
    d_qkv = lax.all_to_all(d_qkv, ROWS, split_axis=0, concat_axis=0, tiled=True)
    d_qkv = d_qkv.astype(jnp.float32).sum(0).astype(bf16)
    d_both = jnp.concatenate([d_qkv, d_group_out], 1).reshape(4, rows // 4, 4 * wide)
    d_both = lax.all_to_all(d_both, "tensor", split_axis=0, concat_axis=0, tiled=True)
    d_both = d_both.reshape(4, rows // 4, 4, wide).transpose(1, 2, 0, 3).reshape(rows // 4, 4 * width)
    d_both = d_both.astype(jnp.float32)
    d_qkv, d_attn_out = d_both[:, : 3 * width], d_both[:, 3 * width :]
    own_rows = pick(w_qkv.reshape(4, rows // 4, 3 * width), t, 0).astype(jnp.float32)
    own_gain = pick(attn_gain.reshape(4, rows // 4), t, 0).astype(jnp.float32)
    d_gain_attn = jnp.sum(d_qkv * own_rows, 1) / own_gain

    grad_normed = chip_sum[0].astype(jnp.float32)
    for part in sent:
        grad_normed = grad_normed + part.astype(jnp.float32)
    gain_attn = pack_1[:, 3 * wide].astype(jnp.float32)
    _, norm_pull_attn = jax.vjp(lambda values: layer_norm(values, gain_attn), own.astype(jnp.float32))
    grad_tokens = grad_hidden + norm_pull_attn(grad_normed)[0]
    return (layer_out[None], grad_tokens[None], d_gain_attn, d_gain_mlp, d_qkv, d_attn_out, d_in, d_down)


def solution(mesh):
    return jax.shard_map(
        local,
        mesh=mesh,
        in_specs=(
            P("shard", ("ctx", "tensor"), None),
            P("shard", None),
            P(("shard", "ctx")),
            P(("shard", "ctx")),
            P(("shard", "ctx"), None),
            P(("shard", "ctx"), None),
            P(("shard", "ctx"), None, "tensor"),
            P("tensor", ("shard", "ctx")),
            P("shard", ("ctx", "tensor"), None),
        ),
        out_specs=(
            P("shard", ("ctx", "tensor"), None),
            P("shard", ("ctx", "tensor"), None),
            P(("shard", "ctx", "tensor")),
            P(("shard", "ctx", "tensor")),
            P(("shard", "ctx", "tensor"), None),
            P(("shard", "ctx", "tensor"), None),
            P(("shard", "ctx"), None, "tensor"),
            P("tensor", ("shard", "ctx")),
        ),
        check_vma=False,
    )
```

```python
import functools

import jax
import jax.numpy as jnp
from jax import lax
from jax.experimental import pallas as pl
from jax.experimental.pallas import tpu as pltpu
from jax.sharding import PartitionSpec as P

HEAD_DIM = 64
EPSILON = 1e-05
ROPE_THETA = 160000.0
SCORE_SCALE = 0.125
MASKED_SCORE = -1e30
ROOT_HALF = 0.7071067811865476
INVERSE_ROOT_TAU = 0.3989422804014327
VMEM_LIMIT = 56 * 1024 * 1024

NT = (((1,), (1,)), ((), ()))
NN = (((1,), (0,)), ((), ()))


def dot(a, b, dims):
    return lax.dot_general(a, b, dims, preferred_element_type=jnp.float32)


def seg_of(position, ends):
    seg = (position >= ends[0]).astype(jnp.int32)
    for end in ends[1:]:
        seg = seg + (position >= end).astype(jnp.int32)
    return seg


def stack_heads(values, group):
    lane_head = lax.broadcasted_iota(jnp.int32, values.shape, 1) // HEAD_DIM
    return jnp.concatenate(
        [jnp.where(lane_head == h, values, jnp.zeros_like(values)) for h in range(group)], 0
    )


def each_key_block(meta, docs, q_at, q_rows, k_first, k_rows, k_blocks, group, body, masked=True):
    ends = [meta[i] for i in range(docs - 1)]
    q_lo, q_hi = seg_of(q_at, ends), seg_of(q_at + q_rows - 1, ends)
    q_seg = seg_of(q_at + lax.broadcasted_iota(jnp.int32, (1, q_rows), 1), ends)
    q_seg = jnp.concatenate([q_seg] * group, 1)

    def step(j, carry):
        k_at = meta[k_first + j]
        k_lo, k_hi = seg_of(k_at, ends), seg_of(k_at + k_rows - 1, ends)
        meets = (k_lo <= q_hi) & (q_lo <= k_hi)
        same = (k_lo == k_hi) & (q_lo == q_hi)

        @pl.when(meets & same if masked else meets)
        def _():
            body(j, None)

        if masked:
            @pl.when(meets & jnp.logical_not(same))
            def _():
                k_seg = seg_of(k_at + lax.broadcasted_iota(jnp.int32, (k_rows, 1), 0), ends)
                body(j, k_seg == q_seg)

        return carry

    lax.fori_loop(0, k_blocks, step, 0)


def attend_kernel(docs, k_rows, meta, q_ref, k_ref, v_ref, o_ref, lse_ref, vt_ref, s_ref, m_ref, l_ref, acc_ref):
    q_rows, wide = q_ref.shape[1], q_ref.shape[2]
    group = wide // HEAD_DIM
    k_blocks = k_ref.shape[1] // k_rows
    q_blocks = pl.num_programs(1)
    i = pl.program_id(1)

    @pl.when(i == 0)
    def _():
        for j in range(k_blocks):
            at = pl.ds(j * k_rows, k_rows)
            vt_ref[:, at] = v_ref[0, at, :].T

    q_st = stack_heads(q_ref[0] * SCORE_SCALE, group)
    m_ref[...] = jnp.full(m_ref.shape, MASKED_SCORE, jnp.float32)
    l_ref[...] = jnp.zeros_like(l_ref)
    acc_ref[...] = jnp.zeros_like(acc_ref)
    place = (docs, meta[docs - 1 + i], q_rows, docs - 1 + q_blocks, k_rows, k_blocks, group)

    def find_top(j, mask):
        at = pl.ds(pl.multiple_of(j * k_rows, k_rows), k_rows)
        scores = dot(k_ref[0, at, :], q_st, NT)
        if mask is not None:
            scores = jnp.where(mask, scores, MASKED_SCORE)
        s_ref[at, :] = scores
        m_ref[...] = jnp.maximum(m_ref[...], jnp.max(scores, 0, keepdims=True))

    each_key_block(meta, *place, find_top)
    row_top = m_ref[...]

    def add_up(j, mask):
        at = pl.ds(pl.multiple_of(j * k_rows, k_rows), k_rows)
        weights = jnp.exp(s_ref[at, :] - row_top)
        l_ref[...] += jnp.sum(weights, 0, keepdims=True)
        low = weights.astype(jnp.bfloat16)
        for h in range(group):
            rows = pl.ds(h * HEAD_DIM, HEAD_DIM)
            cols = slice(h * q_rows, (h + 1) * q_rows)
            acc_ref[rows, :] += dot(vt_ref[rows, at], low[:, cols], NN)

    each_key_block(meta, *place, add_up, False)
    total = l_ref[...]
    outs = []
    for h in range(group):
        cols = slice(h * q_rows, (h + 1) * q_rows)
        outs.append(acc_ref[h * HEAD_DIM : (h + 1) * HEAD_DIM, :] / total[:, cols])
    o_ref[0] = jnp.concatenate(outs, 0).T.astype(jnp.bfloat16)
    lse_ref[0, 0] = row_top + jnp.log(total)


def attend_back_kernel(
    docs, k_rows, meta, q_ref, k_ref, v_ref, o_ref, do_ref, lse_ref, dq_ref, dk_ref, dv_ref,
    kt_ref, dqt_ref, dk_acc, dv_acc,
):
    q_rows, wide = q_ref.shape[1], q_ref.shape[2]
    group = wide // HEAD_DIM
    k_blocks = k_ref.shape[1] // k_rows
    q_blocks = pl.num_programs(1)
    i = pl.program_id(1)

    @pl.when(i == 0)
    def _():
        dk_acc[...] = jnp.zeros_like(dk_acc)
        dv_acc[...] = jnp.zeros_like(dv_acc)
        for j in range(k_blocks):
            at = pl.ds(j * k_rows, k_rows)
            kt_ref[:, at] = k_ref[0, at, :].T

    q_st = stack_heads(q_ref[0] * SCORE_SCALE, group)
    grad_out = do_ref[0]
    do_st = stack_heads(grad_out, group)
    product = (grad_out.astype(jnp.float32) * o_ref[0].astype(jnp.float32)).T
    delta = jnp.concatenate(
        [jnp.sum(product[h * HEAD_DIM : (h + 1) * HEAD_DIM], 0, keepdims=True) for h in range(group)], 1
    )
    log_total = lse_ref[0, 0]
    dqt_ref[...] = jnp.zeros_like(dqt_ref)

    def body(j, mask):
        at = pl.ds(pl.multiple_of(j * k_rows, k_rows), k_rows)
        scores = dot(k_ref[0, at, :], q_st, NT)
        if mask is not None:
            scores = jnp.where(mask, scores, MASKED_SCORE)
        probs = jnp.exp(scores - log_total)
        dv_acc[at, :] += dot(probs.astype(jnp.bfloat16), do_st, NN)
        grad_probs = dot(v_ref[0, at, :], do_st, NT)
        grad_scores = (probs * (grad_probs - delta)).astype(jnp.bfloat16)
        dk_acc[at, :] += dot(grad_scores, q_st, NN)
        for h in range(group):
            rows = pl.ds(h * HEAD_DIM, HEAD_DIM)
            cols = slice(h * q_rows, (h + 1) * q_rows)
            dqt_ref[rows, :] += dot(kt_ref[rows, at], grad_scores[:, cols], NN)

    each_key_block(meta, docs, meta[docs - 1 + i], q_rows, docs - 1 + q_blocks, k_rows, k_blocks, group, body)
    dq_ref[0] = (dqt_ref[...].T * SCORE_SCALE).astype(jnp.bfloat16)

    @pl.when(i == q_blocks - 1)
    def _():
        dk_ref[0] = dk_acc[...].astype(jnp.bfloat16)
        dv_ref[0] = dv_acc[...].astype(jnp.bfloat16)


def attend_call(meta, query, key, value, docs, q_rows, k_rows):
    items, length, wide = query.shape
    keys = key.shape[1]
    group = wide // HEAD_DIM
    q_blocks = length // q_rows
    block = pl.BlockSpec((1, q_rows, wide), lambda g, i, m: (g, i, 0))
    whole = pl.BlockSpec((1, keys, wide), lambda g, i, m: (g, 0, 0))
    stat = pl.BlockSpec((1, 1, 1, group * q_rows), lambda g, i, m: (g, i, 0, 0))
    return pl.pallas_call(
        functools.partial(attend_kernel, docs, k_rows),
        grid_spec=pltpu.PrefetchScalarGridSpec(
            num_scalar_prefetch=1,
            grid=(items, q_blocks),
            in_specs=[block, whole, whole],
            out_specs=[block, stat],
            scratch_shapes=[
                pltpu.VMEM((wide, keys), jnp.bfloat16),
                pltpu.VMEM((keys, group * q_rows), jnp.float32),
                pltpu.VMEM((1, group * q_rows), jnp.float32),
                pltpu.VMEM((1, group * q_rows), jnp.float32),
                pltpu.VMEM((wide, q_rows), jnp.float32),
            ],
        ),
        out_shape=[
            jax.ShapeDtypeStruct(query.shape, jnp.bfloat16),
            jax.ShapeDtypeStruct((items, q_blocks, 1, group * q_rows), jnp.float32),
        ],
        compiler_params=pltpu.CompilerParams(vmem_limit_bytes=VMEM_LIMIT),
        name="attend",
    )(meta, query, key, value)


def attend_back_call(meta, query, key, value, out, grad_out, log_total, docs, q_rows, k_rows):
    items, length, wide = query.shape
    keys = key.shape[1]
    group = wide // HEAD_DIM
    q_blocks = length // q_rows
    block = pl.BlockSpec((1, q_rows, wide), lambda g, i, m: (g, i, 0))
    whole = pl.BlockSpec((1, keys, wide), lambda g, i, m: (g, 0, 0))
    stat = pl.BlockSpec((1, 1, 1, group * q_rows), lambda g, i, m: (g, i, 0, 0))
    return pl.pallas_call(
        functools.partial(attend_back_kernel, docs, k_rows),
        grid_spec=pltpu.PrefetchScalarGridSpec(
            num_scalar_prefetch=1,
            grid=(items, q_blocks),
            in_specs=[block, whole, whole, block, block, stat],
            out_specs=[block, whole, whole],
            scratch_shapes=[
                pltpu.VMEM((wide, keys), jnp.bfloat16),
                pltpu.VMEM((wide, q_rows), jnp.float32),
                pltpu.VMEM((keys, wide), jnp.float32),
                pltpu.VMEM((keys, wide), jnp.float32),
            ],
        ),
        out_shape=[
            jax.ShapeDtypeStruct(query.shape, jnp.bfloat16),
            jax.ShapeDtypeStruct(key.shape, jnp.bfloat16),
            jax.ShapeDtypeStruct(key.shape, jnp.bfloat16),
        ],
        compiler_params=pltpu.CompilerParams(vmem_limit_bytes=VMEM_LIMIT),
        name="attend_back",
    )(meta, query, key, value, out, grad_out, log_total)


def layer_norm(values, gain):
    mean_value = jnp.mean(values, -1, keepdims=True)
    centred = values - mean_value
    spread = jnp.mean(centred * centred, -1, keepdims=True)
    return centred * lax.rsqrt(spread + EPSILON) * gain


def norm_parts(values):
    centred = values - jnp.mean(values, -1, keepdims=True)
    inverse = lax.rsqrt(jnp.mean(centred * centred, -1, keepdims=True) + EPSILON)
    return centred * inverse, inverse


def turn_matrix(width):
    row = lax.broadcasted_iota(jnp.int32, (width, width), 0)
    col = lax.broadcasted_iota(jnp.int32, (width, width), 1)
    half = HEAD_DIM // 2
    first = (col % HEAD_DIM) < half
    plus = jnp.logical_not(first) & (row == col - half)
    minus = first & (row == col + half)
    return plus.astype(jnp.bfloat16) - minus.astype(jnp.bfloat16)


def angles(positions, width):
    half = HEAD_DIM // 2
    steps_index = (jnp.arange(width) % half).astype(jnp.float32)
    inverse = ROPE_THETA ** (-2.0 * steps_index / HEAD_DIM)
    return positions.astype(jnp.float32)[:, None] * inverse[None, :]


def turned_tables(cos_row, sin_row, base):
    cos_base, sin_base = base[0:1, :], base[1:2, :]
    return cos_row * cos_base - sin_row * sin_base, sin_row * cos_base + cos_row * sin_base


def full(shape):
    return pl.BlockSpec(shape, lambda *_: (0,) * len(shape))


def padded(wide):
    return -(-wide // 128) * 128


def project_kernel(meta, *refs):
    chunk_refs = refs[:8]
    w_ref, turn_ref, cos_ref, sin_ref, base_ref, normed_ref, q_ref, k_ref, v_ref, x_ref, w_all, gain_row = refs[8:]
    wide = q_ref.shape[2]
    slot = padded(wide)
    i = pl.program_id(0)
    bf16 = jnp.bfloat16

    @pl.when(i == 0)
    def _():
        for p, at in ((1, 0), (2, 2), (0, 3)):
            w_all[:, at * slot : at * slot + wide] = w_ref[:, p * wide : (p + 1) * wide]
        for p, at in ((1, 1), (0, 4)):
            turned = dot(w_ref[:, p * wide : (p + 1) * wide], turn_ref[...], NN)
            w_all[:, at * slot : at * slot + wide] = turned.astype(bf16)
        last = w_ref[:, w_ref.shape[1] - 128 :].astype(jnp.float32).T
        gain_row[...] = last[127:128, :]

    for n in range(8):
        @pl.when(i == n)
        def _(n=n):
            x_ref[...] = chunk_refs[n][...]

    normed, _ = norm_parts(x_ref[...].astype(jnp.float32))
    normed = (normed * gain_row[...]).astype(bf16)
    normed_ref[0] = normed.T
    cos, sin = turned_tables(cos_ref[...], sin_ref[...], base_ref[0])
    raw = dot(normed, w_all[:, : 3 * slot], NN)
    k_ref[0] = (raw[:, :wide] * cos + raw[:, slot : slot + wide] * sin).astype(bf16)
    v_ref[0] = raw[:, 2 * slot : 2 * slot + wide].astype(bf16)

    @pl.when(i % 2 == meta[0])
    def _():
        raw_q = dot(normed, w_all[:, 3 * slot : 5 * slot], NN)
        q_ref[0] = (raw_q[:, :wide] * cos + raw_q[:, slot : slot + wide] * sin).astype(bf16)


def project_call(meta, chunks, w, turn, cos_row, sin_row, bases, wide):
    block, width = chunks[0].shape
    bf16 = jnp.bfloat16
    one = lambda i, m: (i, 0, 0)
    return pl.pallas_call(
        project_kernel,
        grid_spec=pltpu.PrefetchScalarGridSpec(
            num_scalar_prefetch=1,
            grid=(8,),
            in_specs=[full((block, width))] * 8
            + [full(w.shape), full(turn.shape), full(cos_row.shape), full(sin_row.shape), pl.BlockSpec((1, 2, wide), one)],
            out_specs=[
                pl.BlockSpec((1, width, block), one),
                pl.BlockSpec((1, block, wide), lambda i, m: (i // 2, 0, 0)),
                pl.BlockSpec((1, block, wide), one),
                pl.BlockSpec((1, block, wide), one),
            ],
            scratch_shapes=[
                pltpu.VMEM((block, width), bf16),
                pltpu.VMEM((width, 5 * padded(wide)), bf16),
                pltpu.VMEM((1, width), jnp.float32),
            ],
        ),
        out_shape=[
            jax.ShapeDtypeStruct((8, width, block), bf16),
            jax.ShapeDtypeStruct((4, block, wide), bf16),
            jax.ShapeDtypeStruct((8, block, wide), bf16),
            jax.ShapeDtypeStruct((8, block, wide), bf16),
        ],
        compiler_params=pltpu.CompilerParams(vmem_limit_bytes=VMEM_LIMIT),
        name="project",
    )(meta, *chunks, w, turn, cos_row, sin_row, bases)


def feed_kernel(ff, meta, *refs):
    parts, slices = refs[0:4], refs[4:8]
    tok_ref, cot_ref = refs[8:10]
    out_ref, gh_ref, normed_ref, att_ref, cot_t_ref, gated_ref, ga_ref, gb_ref, gbr_ref, dgain_ref = refs[10:20]
    grad_parts = refs[20:24]
    w_a, w_b, w_dt, w_o, gain_row, att_scr = refs[24:30]
    wide = parts[0].shape[1]
    i = pl.program_id(0)
    bf16 = jnp.bfloat16

    @pl.when(i == 0)
    def _():
        for n in range(4):
            at = slice(n * ff, (n + 1) * ff)
            w_a[:, at] = slices[n][:, :ff]
            w_b[:, at] = slices[n][:, ff : 2 * ff]
            w_dt[:, at] = slices[n][:, 2 * ff : 3 * ff]
            for g in range(4):
                @pl.when(meta[n] == g)
                def _(n=n, g=g):
                    w_o[:, g * wide : (g + 1) * wide] = slices[n][:, 3 * ff : 3 * ff + wide]
        last = slices[0][:, slices[0].shape[1] - 128 :].astype(jnp.float32).T
        gain_row[...] = last[127:128, :]
        dgain_ref[...] = jnp.zeros_like(dgain_ref)

    for g in range(4):
        for n in range(4):
            @pl.when(meta[4 + n] == g)
            def _(n=n, g=g):
                att_scr[:, g * wide : (g + 1) * wide] = parts[n][...]

    attended = att_scr[...]
    att_ref[...] = attended.T
    gain = gain_row[...]
    hidden = tok_ref[...].astype(jnp.float32) + dot(attended, w_o[...], NN)
    normal, inverse = norm_parts(hidden)
    normed = (normal * gain).astype(bf16)
    normed_ref[...] = normed.T
    half_a = dot(normed, w_a[...], NN)
    half_b = dot(normed, w_b[...], NN)
    phi = 0.5 * (1.0 + lax.erf(half_a * ROOT_HALF))
    gelu = half_a * phi
    slope = phi + half_a * (jnp.exp(-0.5 * half_a * half_a) * INVERSE_ROOT_TAU)
    gated = (gelu * half_b).astype(bf16)
    out_ref[...] = (hidden + dot(gated, w_dt[...], NT)).astype(bf16)
    cot = cot_ref[...]
    cot_t_ref[...] = cot.T
    grad_gated = dot(cot, w_dt[...], NN)
    grad_a = (grad_gated * half_b * slope).astype(bf16)
    grad_b = (grad_gated * gelu).astype(bf16)
    for n in range(4):
        at = slice(n * ff, (n + 1) * ff)
        gated_ref[n] = gated[:, at]
        ga_ref[n] = grad_a[:, at]
        gb_ref[n] = grad_b[:, at]
    grad_normed = dot(grad_a, w_a[...], NT) + dot(grad_b, w_b[...], NT)
    dgain_ref[...] += jnp.sum(grad_normed * normal, 0, keepdims=True)
    scaled = grad_normed * gain
    inner = jnp.mean(scaled * normal, -1, keepdims=True)
    grad_hidden = cot.astype(jnp.float32) + inverse * (
        scaled - jnp.mean(scaled, -1, keepdims=True) - normal * inner
    )
    gh_ref[...] = grad_hidden
    grad_branch = grad_hidden.astype(bf16)
    for g in range(4):
        gbr_ref[g] = grad_branch[:, g * wide : (g + 1) * wide]
    grad_mixed = dot(grad_branch, w_o[...], NT).astype(bf16)
    for g in range(4):
        for n in range(4):
            @pl.when(meta[4 + n] == g)
            def _(n=n, g=g):
                grad_parts[n][...] = grad_mixed[:, g * wide : (g + 1) * wide]


def feed_call(meta, parts, slices, tokens, cotangent, ff):
    block, width = tokens.shape
    wide = parts[0].shape[1]
    bf16, f32 = jnp.bfloat16, jnp.float32
    rows = min(256, block)
    part = pl.BlockSpec((rows, wide), lambda i, m: (i, 0))
    row = pl.BlockSpec((rows, width), lambda i, m: (i, 0))
    hid = pl.BlockSpec((4, rows, ff), lambda i, m: (0, i, 0))
    flat = pl.BlockSpec((width, rows), lambda i, m: (0, i))
    grp = pl.BlockSpec((4, rows, wide), lambda i, m: (0, i, 0))
    sds = jax.ShapeDtypeStruct
    return pl.pallas_call(
        functools.partial(feed_kernel, ff),
        grid_spec=pltpu.PrefetchScalarGridSpec(
            num_scalar_prefetch=1,
            grid=(block // rows,),
            in_specs=[part] * 4 + [full(slices[0].shape)] * 4 + [row, row],
            out_specs=[row, row, flat, flat, flat, hid, hid, hid, grp, full((1, width))] + [part] * 4,
            scratch_shapes=[pltpu.VMEM((width, 4 * ff), bf16)] * 3
            + [pltpu.VMEM((width, width), bf16), pltpu.VMEM((1, width), f32), pltpu.VMEM((rows, width), bf16)],
        ),
        out_shape=[
            sds((block, width), bf16),
            sds((block, width), f32),
            sds((width, block), bf16),
            sds((width, block), bf16),
            sds((width, block), bf16),
            sds((4, block, ff), bf16),
            sds((4, block, ff), bf16),
            sds((4, block, ff), bf16),
            sds((4, block, wide), bf16),
            sds((1, width), f32),
        ]
        + [sds((block, wide), bf16)] * 4,
        compiler_params=pltpu.CompilerParams(vmem_limit_bytes=VMEM_LIMIT),
        name="feed",
    )(meta, *parts, *slices, tokens, cotangent)


def pack_kernel(meta, nm_t, cot_t, att_t, ga_ref, gb_ref, gated_ref, gbr_ref, dgain_ref, out_ref):
    ff, wide = ga_ref.shape[2], gbr_ref.shape[2]
    bf16 = jnp.bfloat16

    width = nm_t.shape[0]
    gain = jnp.broadcast_to(dgain_ref[...], (128, width)).T
    last = out_ref.shape[2] - (3 * ff + wide)
    out_ref[0] = jnp.concatenate(
        [
            dot(nm_t[...], ga_ref[0], NN),
            dot(nm_t[...], gb_ref[0], NN),
            dot(cot_t[...], gated_ref[0], NN),
            dot(att_t[...], gbr_ref[0], NN),
            gain[:, :last],
        ],
        1,
    ).astype(bf16)


def pack_call(meta, normed, cotangent, attended, grad_a, grad_b, gated, grad_branch, d_gain, first):
    width, block = normed.shape
    ff, wide = grad_a.shape[2], grad_branch.shape[2]
    bf16 = jnp.bfloat16
    packed = padded(3 * ff + wide + 1)
    hid = pl.BlockSpec((1, block, ff), lambda i, m: (first + i, 0, 0))
    return pl.pallas_call(
        pack_kernel,
        grid_spec=pltpu.PrefetchScalarGridSpec(
            num_scalar_prefetch=1,
            grid=(2,),
            in_specs=[full((width, block))] * 3
            + [hid] * 3
            + [pl.BlockSpec((1, block, wide), lambda i, m: (m[first + i], 0, 0)), full((1, width))],
            out_specs=pl.BlockSpec((1, width, packed), lambda i, m: (i, 0, 0)),
        ),
        out_shape=jax.ShapeDtypeStruct((2, width, packed), bf16),
        compiler_params=pltpu.CompilerParams(vmem_limit_bytes=VMEM_LIMIT),
        name="pack",
    )(meta, normed, cotangent, attended, grad_a, grad_b, gated, grad_branch, d_gain)


def unturn_kernel(meta, normed_ref, dq_ref, dk_ref, dv_ref, turn_ref, cos_ref, sin_ref, base_ref, raw_ref, dw_ref, acc_ref):
    wide = dk_ref.shape[2]
    i = pl.program_id(0)

    @pl.when(i == 0)
    def _():
        acc_ref[...] = jnp.zeros_like(acc_ref)

    cos, sin = turned_tables(cos_ref[...], sin_ref[...], base_ref[0])

    def turn_back(grad):
        return (grad.astype(jnp.float32) * cos + dot(grad, turn_ref[...], NT) * sin).astype(jnp.bfloat16)

    mine = meta[0] == i % 2
    raw_ref[0, :, wide : 2 * wide] = turn_back(dk_ref[0])
    raw_ref[0, :, 2 * wide : 3 * wide] = dv_ref[0]

    @pl.when(mine)
    def _():
        raw_ref[0, :, :wide] = turn_back(dq_ref[0])

    @pl.when(jnp.logical_not(mine))
    def _():
        raw_ref[0, :, :wide] = jnp.zeros_like(dk_ref[0])

    acc_ref[...] += dot(normed_ref[0], raw_ref[0], NN)

    @pl.when(i == pl.num_programs(0) - 1)
    def _():
        dw_ref[...] = acc_ref[...].astype(jnp.bfloat16)


def unturn_call(meta, normed_t, dq, dk, dv, turn, cos_row, sin_row, bases):
    _, width, block = normed_t.shape
    wide = dk.shape[2]
    one = lambda i, m: (i, 0, 0)
    return pl.pallas_call(
        unturn_kernel,
        grid_spec=pltpu.PrefetchScalarGridSpec(
            num_scalar_prefetch=1,
            grid=(8,),
            in_specs=[
                pl.BlockSpec((1, width, block), one),
                pl.BlockSpec((1, block, wide), lambda i, m: (i // 2, 0, 0)),
                pl.BlockSpec((1, block, wide), one),
                pl.BlockSpec((1, block, wide), one),
                full(turn.shape),
                full(cos_row.shape),
                full(sin_row.shape),
                pl.BlockSpec((1, 2, wide), one),
            ],
            out_specs=[pl.BlockSpec((1, block, 3 * wide), one), full((width, 3 * wide))],
            scratch_shapes=[pltpu.VMEM((width, 3 * wide), jnp.float32)],
        ),
        out_shape=[
            jax.ShapeDtypeStruct((8, block, 3 * wide), jnp.bfloat16),
            jax.ShapeDtypeStruct((width, 3 * wide), jnp.bfloat16),
        ],
        compiler_params=pltpu.CompilerParams(vmem_limit_bytes=VMEM_LIMIT),
        name="unturn",
    )(meta, normed_t, dq, dk, dv, turn, cos_row, sin_row, bases)


def unproject_kernel(raw_ref, w_ref, partial_ref):
    partial_ref[0] = dot(raw_ref[0], w_ref[:, : raw_ref.shape[2]], NT).astype(jnp.bfloat16)


def unproject_call(core, grad_raw, w):
    _, block, columns = grad_raw.shape
    width = w.shape[0]
    return pl.pallas_call(
        unproject_kernel,
        grid=(4,),
        in_specs=[pl.BlockSpec((1, block, columns), lambda i: (2 * i + core, 0, 0)), full(w.shape)],
        out_specs=pl.BlockSpec((1, block, width), lambda i: (i, 0, 0)),
        out_shape=jax.ShapeDtypeStruct((4, block, width), jnp.bfloat16),
        compiler_params=pltpu.CompilerParams(vmem_limit_bytes=VMEM_LIMIT),
        name="unproject",
    )(grad_raw, w)


PLANE = ("ctx", "tensor")


def plane_permute(array, target):
    pairs = []
    for c in range(2):
        for x in range(2):
            for h in range(2):
                to_c, to_x, to_h = target(c, x, h)
                pairs.append((c * 4 + x * 2 + h, to_c * 4 + to_x * 2 + to_h))
    return lax.ppermute(array, PLANE, pairs)


def tensor_permute(array, flip):
    return lax.ppermute(array, "tensor", [(t, t ^ flip) for t in range(4)])


def pick(array, index, axis):
    return lax.dynamic_index_in_dim(array, index, axis, keepdims=False)


def local(tokens, doc_lengths, attn_gain, mlp_gain, w_qkv, w_attn_out, w_in, w_down, cotangent):
    _, block, width = tokens.shape
    assert lax.axis_size("ctx") == 2 and lax.axis_size("tensor") == 4 and tokens.shape[0] == 1
    rows = w_qkv.shape[0]
    ff = w_in.shape[2]
    docs = doc_lengths.shape[1]
    c = lax.axis_index("ctx")
    t = lax.axis_index("tensor")
    x, h = t // 2, t % 2
    wide = width // 4
    bf16 = jnp.bfloat16

    own = tokens[0]
    half = block // 2
    over_y = lambda c, x, h: (1 - c, x, h)
    shards = lax.axis_size("shard")
    shard_at = lax.axis_index("shard")

    def shard_gather(part):
        whole = jnp.zeros((shards,) + part.shape, part.dtype)
        pieces = [part]
        for k in range(1, shards):
            pieces.append(lax.ppermute(part, "shard", [(z, (z + k) % shards) for z in range(shards)]))
        for k, piece in enumerate(pieces):
            whole = lax.dynamic_update_index_in_dim(whole, piece, lax.rem(shard_at + shards - k, shards), 0)
        return whole

    def both_ctx(mine, other, axis):
        return jnp.where(c == 0, jnp.stack([mine, other], axis), jnp.stack([other, mine], axis))

    group_cols = pick(w_qkv.reshape(rows, 3, 4, wide), t, 2).reshape(rows, 3 * wide)
    gain_cols = padded(3 * wide + 1) - 3 * wide
    pack_1 = jnp.concatenate([group_cols, jnp.broadcast_to(attn_gain[:, None], (rows, gain_cols))], 1)
    own_cols = pick(w_attn_out.reshape(rows, 4, wide), t, 1)
    gain_cols = padded(3 * ff + wide + 1) - 3 * ff - wide
    pack_2 = jnp.concatenate(
        [w_in.reshape(rows, 2 * ff), w_down.T, own_cols, jnp.broadcast_to(mlp_gain[:, None], (rows, gain_cols))], 1
    )
    slice_flips = (0, 2, 1, 3)

    by_x = tensor_permute(own, 2)
    by_y = plane_permute(own, over_y)
    pack_1 = shard_gather(pack_1)
    pack_1, pack_2, by_x, by_y = lax.optimization_barrier((pack_1, pack_2, by_x, by_y))
    pack_1 = both_ctx(pack_1, plane_permute(pack_1, over_y), 1).reshape(width, -1)
    pack_2 = shard_gather(pack_2)
    pack_2 = both_ctx(pack_2, plane_permute(pack_2, over_y), 1).reshape(width, -1)
    by_xy = jnp.concatenate([plane_permute(by_x[:half], over_y), tensor_permute(by_y[half:], 2)], 0)
    chunks = []
    for part in (own, by_x, by_y, by_xy):
        chunks += [part, tensor_permute(part, 1)]

    chunk_at = []
    for dc in range(2):
        for dx in range(2):
            for dh in range(2):
                chunk_at.append(((c ^ dc) * 4 + (x ^ dx) * 2 + (h ^ dh)) * block)
    row_angles = angles(jnp.arange(block), wide)
    base_angles = angles(jnp.stack(chunk_at), wide)
    cos_row, sin_row = jnp.cos(row_angles), jnp.sin(row_angles)
    bases = jnp.stack([jnp.cos(base_angles), jnp.sin(base_angles)], 1)
    q_rows = min(512, block)
    k_rows = min(512, block)
    pick_core = h ^ c
    key_starts = [at + k * k_rows for at in chunk_at for k in range(block // k_rows)]
    query_starts = [
        ((c ^ dc) * 4 + (x ^ dx) * 2 + c) * block + k * q_rows
        for dc in range(2)
        for dx in range(2)
        for k in range(block // q_rows)
    ]
    doc_ends = jnp.cumsum(doc_lengths[0])[: docs - 1].astype(jnp.int32)
    meta = jnp.concatenate([doc_ends, jnp.stack(query_starts + key_starts).astype(jnp.int32)])
    core_meta = jnp.stack([pick_core]).astype(jnp.int32)
    steps = [(a, b) for b in range(2) for a in range(2)]
    feed_meta = jnp.stack(
        [t ^ flip for flip in slice_flips] + [(x ^ b) * 2 + (c ^ a) for a, b in steps]
    ).astype(jnp.int32)

    turn = turn_matrix(wide)
    normed_t, query, key, value = project_call(core_meta, chunks, pack_1, turn, cos_row, sin_row, bases, wide)
    query, pack_2 = lax.optimization_barrier((query, pack_2))
    slices = [pack_2, tensor_permute(pack_2, 2), tensor_permute(pack_2, 1)]
    query = query.reshape(1, 4 * block, wide)
    key = key.reshape(1, 8 * block, wide)
    value = value.reshape(1, 8 * block, wide)
    out, log_total = attend_call(meta, query, key, value, docs, q_rows, k_rows)

    out, slices[1] = lax.optimization_barrier((out, slices[1]))
    slices.append(tensor_permute(slices[1], 1))

    def forth(a, b):
        return lambda c, x, h: (h ^ a, x ^ b, c)

    def back(a, b):
        return lambda c, x, h: (h, x ^ b, c ^ a)

    out_parts = out.reshape(2, 2, block, wide)
    arrived = [plane_permute(pick(out_parts, pick_core ^ a, 0)[b], forth(a, b)) for a, b in steps]

    (layer_out, grad_hidden, normed_m, attended, cot_t, gated, grad_a, grad_b, grad_branch, d_gain_mlp, *grad_parts) = feed_call(
        feed_meta, arrived, slices, own, cotangent[0], ff
    )
    grad_parts = [plane_permute(part, back(a, b)) for part, (a, b) in zip(grad_parts, steps)]
    arrived_parts = grad_parts
    grad_parts = jnp.stack(grad_parts).reshape(2, 2, block, wide)
    grad_items = jnp.stack(
        [jnp.stack([pick(grad_parts[b], pick_core ^ dc, 0) for b in range(2)]) for dc in range(2)]
    ).reshape(1, 4 * block, wide)

    def add(one, two):
        return (one.astype(jnp.float32) + two.astype(jnp.float32)).astype(bf16)

    grads = (normed_m, cot_t, attended, grad_a, grad_b, gated, grad_branch, d_gain_mlp)
    sent_packs = tensor_permute(pack_call(feed_meta, *grads, 2), 1)
    grads = lax.optimization_barrier((grads, arrived_parts))[0]
    packs = add(pack_call(feed_meta, *grads, 0), sent_packs)
    pack_own, to_x = packs[0], packs[1]
    pack_x = tensor_permute(to_x, 2)
    grad_items, pack_own = lax.optimization_barrier((grad_items, pack_own))

    grad_query, grad_key, grad_value = attend_back_call(
        meta, query, key, value, out, grad_items, log_total, docs, q_rows, k_rows
    )
    pack = add(pack_own, pack_x).reshape(-1, 2, rows, pack_own.shape[1])
    grad_key, pack = lax.optimization_barrier((grad_key, pack))
    pack_y = plane_permute(pick(pack, 1 - c, 1), lambda c, x, h: (1 - c, x, h))
    pack_own = pick(pack, c, 1)
    grad_query = grad_query.reshape(4, block, wide)
    grad_key = grad_key.reshape(8, block, wide)
    grad_value = grad_value.reshape(8, block, wide)
    grad_raw, d_qkv = unturn_call(
        core_meta, normed_t, grad_query, grad_key, grad_value, turn, cos_row, sin_row, bases
    )
    d_qkv = d_qkv.reshape(-1, 2, rows, 3 * wide)
    d_qkv_y = plane_permute(pick(d_qkv, 1 - c, 1), lambda c, x, h: (1 - c, x, h))
    d_qkv_own = pick(d_qkv, c, 1)
    grad_raw, pack_y = lax.optimization_barrier((grad_raw, pack_y))
    from_core = tensor_permute(unproject_call(1, grad_raw, pack_1), 1)
    partial = unproject_call(0, grad_raw, pack_1)
    partial, d_qkv_y = lax.optimization_barrier((partial, d_qkv_y))

    chip_sum = [add(partial[n], from_core[n]) for n in range(4)]
    low_half, high_half = slice(0, half), slice(half, block)
    sent_x = tensor_permute(jnp.stack([chip_sum[1][low_half], chip_sum[3][low_half]]), 2)
    sent_y = plane_permute(jnp.stack([chip_sum[2][high_half], chip_sum[3][high_half]]), over_y)
    pack_y, sent_x, sent_y = lax.optimization_barrier((pack_y, sent_x, sent_y))
    last_y = plane_permute(add(chip_sum[2][low_half], sent_x[1]), over_y)
    last_x = tensor_permute(add(chip_sum[1][high_half], sent_y[1]), 2)
    own_sum = chip_sum[0].astype(jnp.float32)
    sent = jnp.concatenate(
        [
            own_sum[low_half] + sent_x[0].astype(jnp.float32) + last_y.astype(jnp.float32),
            own_sum[high_half] + sent_y[0].astype(jnp.float32) + last_x.astype(jnp.float32),
        ],
        0,
    )

    def shard_sum(parts):
        total = pick(parts, shard_at, 0).astype(jnp.float32)
        for k in range(1, shards):
            part = pick(parts, lax.rem(shard_at + k, shards), 0)
            total = total + lax.ppermute(part, "shard", [(z, (z + k) % shards) for z in range(shards)]).astype(jnp.float32)
        return total

    pack = shard_sum(add(pack_own, pack_y))
    d_in = pack[:, : 2 * ff].reshape(rows, 2, ff)
    d_down = pack[:, 2 * ff : 3 * ff].T
    d_group_out = pack[:, 3 * ff : 3 * ff + wide].astype(bf16)
    d_gain_mlp = pick(pack[:, 3 * ff + wide].reshape(4, rows // 4), t, 0)
    d_qkv = shard_sum(add(d_qkv_own, d_qkv_y)).astype(bf16)
    d_qkv, sent = lax.optimization_barrier((d_qkv, sent))
    d_both = jnp.concatenate([d_qkv, d_group_out], 1).reshape(4, rows // 4, 4 * wide)
    d_both = lax.all_to_all(d_both, "tensor", split_axis=0, concat_axis=0, tiled=True)
    d_both = d_both.reshape(4, rows // 4, 4, wide).transpose(1, 2, 0, 3).reshape(rows // 4, 4 * width)
    d_both = d_both.astype(jnp.float32)
    d_qkv, d_attn_out = d_both[:, : 3 * width], d_both[:, 3 * width :]
    own_rows = pick(w_qkv.reshape(4, rows // 4, 3 * width), t, 0).astype(jnp.float32)
    own_gain = pick(attn_gain.reshape(4, rows // 4), t, 0).astype(jnp.float32)
    d_gain_attn = jnp.sum(d_qkv * own_rows, 1) / own_gain

    grad_normed = sent
    gain_attn = pack_1[:, 3 * wide].astype(jnp.float32)
    _, norm_pull_attn = jax.vjp(lambda values: layer_norm(values, gain_attn), own.astype(jnp.float32))
    grad_tokens = grad_hidden + norm_pull_attn(grad_normed)[0]
    return (layer_out[None], grad_tokens[None], d_gain_attn, d_gain_mlp, d_qkv, d_attn_out, d_in, d_down)


def solution(mesh):
    return jax.shard_map(
        local,
        mesh=mesh,
        in_specs=(
            P("shard", ("ctx", "tensor"), None),
            P("shard", None),
            P(("shard", "ctx")),
            P(("shard", "ctx")),
            P(("shard", "ctx"), None),
            P(("shard", "ctx"), None),
            P(("shard", "ctx"), None, "tensor"),
            P("tensor", ("shard", "ctx")),
            P("shard", ("ctx", "tensor"), None),
        ),
        out_specs=(
            P("shard", ("ctx", "tensor"), None),
            P("shard", ("ctx", "tensor"), None),
            P(("shard", "ctx", "tensor")),
            P(("shard", "ctx", "tensor")),
            P(("shard", "ctx", "tensor"), None),
            P(("shard", "ctx", "tensor"), None),
            P(("shard", "ctx"), None, "tensor"),
            P("tensor", ("shard", "ctx")),
        ),
        check_vma=False,
    )
```

```python
import functools

import jax
import jax.numpy as jnp
from jax import lax
from jax.experimental import pallas as pl
from jax.experimental.pallas import tpu as pltpu
from jax.sharding import PartitionSpec as P

HEAD_DIM = 64
EPSILON = 1e-05
ROPE_THETA = 160000.0
SCORE_SCALE = 0.125
MASKED_SCORE = -1e30
ROOT_HALF = 0.7071067811865476
INVERSE_ROOT_TAU = 0.3989422804014327
VMEM_LIMIT = 56 * 1024 * 1024

NT = (((1,), (1,)), ((), ()))
NN = (((1,), (0,)), ((), ()))


def dot(a, b, dims):
    return lax.dot_general(a, b, dims, preferred_element_type=jnp.float32)


def seg_of(position, ends):
    seg = (position >= ends[0]).astype(jnp.int32)
    for end in ends[1:]:
        seg = seg + (position >= end).astype(jnp.int32)
    return seg


def stack_heads(values, group):
    lane_head = lax.broadcasted_iota(jnp.int32, values.shape, 1) // HEAD_DIM
    return jnp.concatenate(
        [jnp.where(lane_head == h, values, jnp.zeros_like(values)) for h in range(group)], 0
    )


def each_key_block(meta, docs, q_at, q_rows, k_first, k_rows, k_blocks, group, body, masked=True):
    ends = [meta[i] for i in range(docs - 1)]
    q_lo, q_hi = seg_of(q_at, ends), seg_of(q_at + q_rows - 1, ends)
    q_seg = seg_of(q_at + lax.broadcasted_iota(jnp.int32, (1, q_rows), 1), ends)
    q_seg = jnp.concatenate([q_seg] * group, 1)

    def step(j, carry):
        k_at = meta[k_first + j]
        k_lo, k_hi = seg_of(k_at, ends), seg_of(k_at + k_rows - 1, ends)
        meets = (k_lo <= q_hi) & (q_lo <= k_hi)
        same = (k_lo == k_hi) & (q_lo == q_hi)

        @pl.when(meets & same if masked else meets)
        def _():
            body(j, None)

        if masked:
            @pl.when(meets & jnp.logical_not(same))
            def _():
                k_seg = seg_of(k_at + lax.broadcasted_iota(jnp.int32, (k_rows, 1), 0), ends)
                body(j, k_seg == q_seg)

        return carry

    lax.fori_loop(0, k_blocks, step, 0)


def attend_kernel(docs, k_rows, meta, q_ref, k_ref, v_ref, o_ref, lse_ref, vt_ref, s_ref, m_ref, l_ref, acc_ref):
    q_rows, wide = q_ref.shape[1], q_ref.shape[2]
    group = wide // HEAD_DIM
    k_blocks = k_ref.shape[1] // k_rows
    q_blocks = pl.num_programs(1)
    i = pl.program_id(1)

    @pl.when(i == 0)
    def _():
        for j in range(k_blocks):
            at = pl.ds(j * k_rows, k_rows)
            vt_ref[:, at] = v_ref[0, at, :].T

    q_st = stack_heads(q_ref[0] * SCORE_SCALE, group)
    m_ref[...] = jnp.full(m_ref.shape, MASKED_SCORE, jnp.float32)
    l_ref[...] = jnp.zeros_like(l_ref)
    acc_ref[...] = jnp.zeros_like(acc_ref)
    place = (docs, meta[docs - 1 + i], q_rows, docs - 1 + q_blocks, k_rows, k_blocks, group)

    def find_top(j, mask):
        at = pl.ds(pl.multiple_of(j * k_rows, k_rows), k_rows)
        scores = dot(k_ref[0, at, :], q_st, NT)
        if mask is not None:
            scores = jnp.where(mask, scores, MASKED_SCORE)
        s_ref[at, :] = scores
        m_ref[...] = jnp.maximum(m_ref[...], jnp.max(scores, 0, keepdims=True))

    each_key_block(meta, *place, find_top)
    row_top = m_ref[...]

    def add_up(j, mask):
        at = pl.ds(pl.multiple_of(j * k_rows, k_rows), k_rows)
        weights = jnp.exp(s_ref[at, :] - row_top)
        l_ref[...] += jnp.sum(weights, 0, keepdims=True)
        low = weights.astype(jnp.bfloat16)
        for h in range(group):
            rows = pl.ds(h * HEAD_DIM, HEAD_DIM)
            cols = slice(h * q_rows, (h + 1) * q_rows)
            acc_ref[rows, :] += dot(vt_ref[rows, at], low[:, cols], NN)

    each_key_block(meta, *place, add_up, False)
    total = l_ref[...]
    outs = []
    for h in range(group):
        cols = slice(h * q_rows, (h + 1) * q_rows)
        outs.append(acc_ref[h * HEAD_DIM : (h + 1) * HEAD_DIM, :] / total[:, cols])
    o_ref[0] = jnp.concatenate(outs, 0).T.astype(jnp.bfloat16)
    lse_ref[0, 0] = row_top + jnp.log(total)


def attend_back_kernel(
    docs, k_rows, meta, q_ref, k_ref, v_ref, o_ref, do_0, do_1, do_2, do_3, lse_ref, dq_ref, dk_ref, dv_ref,
    kt_ref, dqt_ref, dk_acc, dv_acc, do_ref,
):
    q_rows, wide = q_ref.shape[1], q_ref.shape[2]
    group = wide // HEAD_DIM
    k_blocks = k_ref.shape[1] // k_rows
    q_blocks = pl.num_programs(1)
    i = pl.program_id(1)

    @pl.when(i == 0)
    def _():
        dk_acc[...] = jnp.zeros_like(dk_acc)
        dv_acc[...] = jnp.zeros_like(dv_acc)
        for j in range(k_blocks):
            at = pl.ds(j * k_rows, k_rows)
            kt_ref[:, at] = k_ref[0, at, :].T

    q_st = stack_heads(q_ref[0] * SCORE_SCALE, group)
    source = (i % 2) * 2 + ((i // 2) ^ meta[docs - 1 + q_blocks + k_blocks])
    for n, part in enumerate((do_0, do_1, do_2, do_3)):
        @pl.when(source == n)
        def _(part=part):
            do_ref[...] = part[...]

    grad_out = do_ref[...]
    do_st = stack_heads(grad_out, group)
    product = (grad_out.astype(jnp.float32) * o_ref[0].astype(jnp.float32)).T
    delta = jnp.concatenate(
        [jnp.sum(product[h * HEAD_DIM : (h + 1) * HEAD_DIM], 0, keepdims=True) for h in range(group)], 1
    )
    log_total = lse_ref[0, 0]
    dqt_ref[...] = jnp.zeros_like(dqt_ref)

    def body(j, mask):
        at = pl.ds(pl.multiple_of(j * k_rows, k_rows), k_rows)
        scores = dot(k_ref[0, at, :], q_st, NT)
        if mask is not None:
            scores = jnp.where(mask, scores, MASKED_SCORE)
        probs = jnp.exp(scores - log_total)
        dv_acc[at, :] += dot(probs.astype(jnp.bfloat16), do_st, NN)
        grad_probs = dot(v_ref[0, at, :], do_st, NT)
        grad_scores = (probs * (grad_probs - delta)).astype(jnp.bfloat16)
        dk_acc[at, :] += dot(grad_scores, q_st, NN)
        for h in range(group):
            rows = pl.ds(h * HEAD_DIM, HEAD_DIM)
            cols = slice(h * q_rows, (h + 1) * q_rows)
            dqt_ref[rows, :] += dot(kt_ref[rows, at], grad_scores[:, cols], NN)

    each_key_block(meta, docs, meta[docs - 1 + i], q_rows, docs - 1 + q_blocks, k_rows, k_blocks, group, body)
    dq_ref[0] = (dqt_ref[...].T * SCORE_SCALE).astype(jnp.bfloat16)

    @pl.when(i == q_blocks - 1)
    def _():
        dk_ref[0] = dk_acc[...].astype(jnp.bfloat16)
        dv_ref[0] = dv_acc[...].astype(jnp.bfloat16)


def attend_call(meta, query, key, value, docs, q_rows, k_rows):
    items, length, wide = query.shape
    keys = key.shape[1]
    group = wide // HEAD_DIM
    q_blocks = length // q_rows
    block = pl.BlockSpec((1, q_rows, wide), lambda g, i, m: (g, i, 0))
    last = docs - 1 + q_blocks + keys // k_rows
    moved = pl.BlockSpec((1, q_rows, wide), lambda g, i, m: (g, i ^ (2 * m[last]), 0))
    whole = pl.BlockSpec((1, keys, wide), lambda g, i, m: (g, 0, 0))
    stat = pl.BlockSpec((1, 1, 1, group * q_rows), lambda g, i, m: (g, i, 0, 0))
    return pl.pallas_call(
        functools.partial(attend_kernel, docs, k_rows),
        grid_spec=pltpu.PrefetchScalarGridSpec(
            num_scalar_prefetch=1,
            grid=(items, q_blocks),
            in_specs=[block, whole, whole],
            out_specs=[moved, stat],
            scratch_shapes=[
                pltpu.VMEM((wide, keys), jnp.bfloat16),
                pltpu.VMEM((keys, group * q_rows), jnp.float32),
                pltpu.VMEM((1, group * q_rows), jnp.float32),
                pltpu.VMEM((1, group * q_rows), jnp.float32),
                pltpu.VMEM((wide, q_rows), jnp.float32),
            ],
        ),
        out_shape=[
            jax.ShapeDtypeStruct(query.shape, jnp.bfloat16),
            jax.ShapeDtypeStruct((items, q_blocks, 1, group * q_rows), jnp.float32),
        ],
        compiler_params=pltpu.CompilerParams(vmem_limit_bytes=VMEM_LIMIT),
        name="attend",
    )(meta, query, key, value)


def attend_back_call(meta, query, key, value, out, grad_parts, log_total, docs, q_rows, k_rows):
    items, length, wide = query.shape
    keys = key.shape[1]
    group = wide // HEAD_DIM
    q_blocks = length // q_rows
    block = pl.BlockSpec((1, q_rows, wide), lambda g, i, m: (g, i, 0))
    last = docs - 1 + q_blocks + keys // k_rows
    moved = pl.BlockSpec((1, q_rows, wide), lambda g, i, m: (g, i ^ (2 * m[last]), 0))
    whole = pl.BlockSpec((1, keys, wide), lambda g, i, m: (g, 0, 0))
    stat = pl.BlockSpec((1, 1, 1, group * q_rows), lambda g, i, m: (g, i, 0, 0))
    return pl.pallas_call(
        functools.partial(attend_back_kernel, docs, k_rows),
        grid_spec=pltpu.PrefetchScalarGridSpec(
            num_scalar_prefetch=1,
            grid=(items, q_blocks),
            in_specs=[block, whole, whole, moved] + [full((q_rows, wide))] * 4 + [stat],
            out_specs=[block, whole, whole],
            scratch_shapes=[
                pltpu.VMEM((wide, keys), jnp.bfloat16),
                pltpu.VMEM((wide, q_rows), jnp.float32),
                pltpu.VMEM((keys, wide), jnp.float32),
                pltpu.VMEM((keys, wide), jnp.float32),
                pltpu.VMEM((q_rows, wide), jnp.bfloat16),
            ],
        ),
        out_shape=[
            jax.ShapeDtypeStruct(query.shape, jnp.bfloat16),
            jax.ShapeDtypeStruct(key.shape, jnp.bfloat16),
            jax.ShapeDtypeStruct(key.shape, jnp.bfloat16),
        ],
        compiler_params=pltpu.CompilerParams(vmem_limit_bytes=VMEM_LIMIT),
        name="attend_back",
    )(meta, query, key, value, out, *grad_parts, log_total)


def layer_norm(values, gain):
    mean_value = jnp.mean(values, -1, keepdims=True)
    centred = values - mean_value
    spread = jnp.mean(centred * centred, -1, keepdims=True)
    return centred * lax.rsqrt(spread + EPSILON) * gain


def norm_parts(values):
    centred = values - jnp.mean(values, -1, keepdims=True)
    inverse = lax.rsqrt(jnp.mean(centred * centred, -1, keepdims=True) + EPSILON)
    return centred * inverse, inverse


def turn_matrix(width):
    row = lax.broadcasted_iota(jnp.int32, (width, width), 0)
    col = lax.broadcasted_iota(jnp.int32, (width, width), 1)
    half = HEAD_DIM // 2
    first = (col % HEAD_DIM) < half
    plus = jnp.logical_not(first) & (row == col - half)
    minus = first & (row == col + half)
    return plus.astype(jnp.bfloat16) - minus.astype(jnp.bfloat16)


def angles(positions, width):
    half = HEAD_DIM // 2
    steps_index = (jnp.arange(width) % half).astype(jnp.float32)
    inverse = ROPE_THETA ** (-2.0 * steps_index / HEAD_DIM)
    return positions.astype(jnp.float32)[:, None] * inverse[None, :]


def turned_tables(cos_row, sin_row, base):
    cos_base, sin_base = base[0:1, :], base[1:2, :]
    return cos_row * cos_base - sin_row * sin_base, sin_row * cos_base + cos_row * sin_base


def full(shape):
    return pl.BlockSpec(shape, lambda *_: (0,) * len(shape))


def padded(wide):
    return -(-wide // 128) * 128


def project_kernel(meta, *refs):
    chunk_refs = refs[:8]
    w_ref, turn_ref, cos_ref, sin_ref, base_ref, normed_ref, q_ref, k_ref, v_ref, x_ref, w_all, gain_row = refs[8:]
    wide = q_ref.shape[2]
    slot = padded(wide)
    i = pl.program_id(0)
    bf16 = jnp.bfloat16

    @pl.when(i == 0)
    def _():
        for p, at in ((1, 0), (2, 2), (0, 3)):
            w_all[:, at * slot : at * slot + wide] = w_ref[:, p * wide : (p + 1) * wide]
        for p, at in ((1, 1), (0, 4)):
            turned = dot(w_ref[:, p * wide : (p + 1) * wide], turn_ref[...], NN)
            w_all[:, at * slot : at * slot + wide] = turned.astype(bf16)
        last = w_ref[:, w_ref.shape[1] - 128 :].astype(jnp.float32).T
        gain_row[...] = last[127:128, :]

    for n in range(8):
        @pl.when(i == n)
        def _(n=n):
            x_ref[...] = chunk_refs[n][...]

    normed, _ = norm_parts(x_ref[...].astype(jnp.float32))
    normed = (normed * gain_row[...]).astype(bf16)
    normed_ref[0] = normed.T
    cos, sin = turned_tables(cos_ref[...], sin_ref[...], base_ref[0])
    raw = dot(normed, w_all[:, : 3 * slot], NN)
    k_ref[0] = (raw[:, :wide] * cos + raw[:, slot : slot + wide] * sin).astype(bf16)
    v_ref[0] = raw[:, 2 * slot : 2 * slot + wide].astype(bf16)

    @pl.when(i % 2 == meta[0])
    def _():
        raw_q = dot(normed, w_all[:, 3 * slot : 5 * slot], NN)
        q_ref[0] = (raw_q[:, :wide] * cos + raw_q[:, slot : slot + wide] * sin).astype(bf16)


def project_call(meta, chunks, w, turn, cos_row, sin_row, bases, wide):
    block, width = chunks[0].shape
    bf16 = jnp.bfloat16
    one = lambda i, m: (i, 0, 0)
    return pl.pallas_call(
        project_kernel,
        grid_spec=pltpu.PrefetchScalarGridSpec(
            num_scalar_prefetch=1,
            grid=(8,),
            in_specs=[full((block, width))] * 8
            + [full(w.shape), full(turn.shape), full(cos_row.shape), full(sin_row.shape), pl.BlockSpec((1, 2, wide), one)],
            out_specs=[
                pl.BlockSpec((1, width, block), one),
                pl.BlockSpec((1, block, wide), lambda i, m: (i // 2, 0, 0)),
                pl.BlockSpec((1, block, wide), one),
                pl.BlockSpec((1, block, wide), one),
            ],
            scratch_shapes=[
                pltpu.VMEM((block, width), bf16),
                pltpu.VMEM((width, 5 * padded(wide)), bf16),
                pltpu.VMEM((1, width), jnp.float32),
            ],
        ),
        out_shape=[
            jax.ShapeDtypeStruct((8, width, block), bf16),
            jax.ShapeDtypeStruct((4, block, wide), bf16),
            jax.ShapeDtypeStruct((8, block, wide), bf16),
            jax.ShapeDtypeStruct((8, block, wide), bf16),
        ],
        compiler_params=pltpu.CompilerParams(vmem_limit_bytes=VMEM_LIMIT),
        name="project",
    )(meta, *chunks, w, turn, cos_row, sin_row, bases)


def feed_kernel(ff, meta, *refs):
    parts, slices = refs[0:4], refs[4:8]
    tok_ref, cot_ref = refs[8:10]
    out_ref, gh_ref, normed_ref, att_ref, cot_t_ref, gated_ref, ga_ref, gb_ref, gbr_ref, dgain_ref = refs[10:20]
    grad_parts = refs[20:24]
    w_a, w_b, w_dt, w_o, gain_row, att_scr = refs[24:30]
    wide = parts[0].shape[1]
    i = pl.program_id(0)
    bf16 = jnp.bfloat16

    @pl.when(i == 0)
    def _():
        for n in range(4):
            at = slice(n * ff, (n + 1) * ff)
            w_a[:, at] = slices[n][:, :ff]
            w_b[:, at] = slices[n][:, ff : 2 * ff]
            w_dt[:, at] = slices[n][:, 2 * ff : 3 * ff]
            for g in range(4):
                @pl.when(meta[n] == g)
                def _(n=n, g=g):
                    w_o[:, g * wide : (g + 1) * wide] = slices[n][:, 3 * ff : 3 * ff + wide]
        last = slices[0][:, slices[0].shape[1] - 128 :].astype(jnp.float32).T
        gain_row[...] = last[127:128, :]
        dgain_ref[...] = jnp.zeros_like(dgain_ref)

    for g in range(4):
        for n in range(4):
            @pl.when(meta[4 + n] == g)
            def _(n=n, g=g):
                att_scr[:, g * wide : (g + 1) * wide] = parts[n][...]

    attended = att_scr[...]
    att_ref[...] = attended.T
    gain = gain_row[...]
    hidden = tok_ref[...].astype(jnp.float32) + dot(attended, w_o[...], NN)
    normal, inverse = norm_parts(hidden)
    normed = (normal * gain).astype(bf16)
    normed_ref[...] = normed.T
    half_a = dot(normed, w_a[...], NN)
    half_b = dot(normed, w_b[...], NN)
    phi = 0.5 * (1.0 + lax.erf(half_a * ROOT_HALF))
    gelu = half_a * phi
    slope = phi + half_a * (jnp.exp(-0.5 * half_a * half_a) * INVERSE_ROOT_TAU)
    gated = (gelu * half_b).astype(bf16)
    out_ref[...] = (hidden + dot(gated, w_dt[...], NT)).astype(bf16)
    cot = cot_ref[...]
    cot_t_ref[...] = cot.T
    grad_gated = dot(cot, w_dt[...], NN)
    grad_a = (grad_gated * half_b * slope).astype(bf16)
    grad_b = (grad_gated * gelu).astype(bf16)
    for n in range(4):
        at = slice(n * ff, (n + 1) * ff)
        gated_ref[n] = gated[:, at]
        ga_ref[n] = grad_a[:, at]
        gb_ref[n] = grad_b[:, at]
    grad_normed = dot(grad_a, w_a[...], NT) + dot(grad_b, w_b[...], NT)
    dgain_ref[...] += jnp.sum(grad_normed * normal, 0, keepdims=True)
    scaled = grad_normed * gain
    inner = jnp.mean(scaled * normal, -1, keepdims=True)
    grad_hidden = cot.astype(jnp.float32) + inverse * (
        scaled - jnp.mean(scaled, -1, keepdims=True) - normal * inner
    )
    gh_ref[...] = grad_hidden
    grad_branch = grad_hidden.astype(bf16)
    for g in range(4):
        gbr_ref[g] = grad_branch[:, g * wide : (g + 1) * wide]
    grad_mixed = dot(grad_branch, w_o[...], NT).astype(bf16)
    for g in range(4):
        for n in range(4):
            @pl.when(meta[4 + n] == g)
            def _(n=n, g=g):
                grad_parts[n][...] = grad_mixed[:, g * wide : (g + 1) * wide]


def feed_call(meta, parts, slices, tokens, cotangent, ff):
    block, width = tokens.shape
    wide = parts[0].shape[1]
    bf16, f32 = jnp.bfloat16, jnp.float32
    rows = min(256, block)
    part = pl.BlockSpec((rows, wide), lambda i, m: (i, 0))
    row = pl.BlockSpec((rows, width), lambda i, m: (i, 0))
    hid = pl.BlockSpec((4, rows, ff), lambda i, m: (0, i, 0))
    flat = pl.BlockSpec((width, rows), lambda i, m: (0, i))
    grp = pl.BlockSpec((4, rows, wide), lambda i, m: (0, i, 0))
    sds = jax.ShapeDtypeStruct
    return pl.pallas_call(
        functools.partial(feed_kernel, ff),
        grid_spec=pltpu.PrefetchScalarGridSpec(
            num_scalar_prefetch=1,
            grid=(block // rows,),
            in_specs=[part] * 4 + [full(slices[0].shape)] * 4 + [row, row],
            out_specs=[row, row, flat, flat, flat, hid, hid, hid, grp, full((1, width))] + [part] * 4,
            scratch_shapes=[pltpu.VMEM((width, 4 * ff), bf16)] * 3
            + [pltpu.VMEM((width, width), bf16), pltpu.VMEM((1, width), f32), pltpu.VMEM((rows, width), bf16)],
        ),
        out_shape=[
            sds((block, width), bf16),
            sds((block, width), f32),
            sds((width, block), bf16),
            sds((width, block), bf16),
            sds((width, block), bf16),
            sds((4, block, ff), bf16),
            sds((4, block, ff), bf16),
            sds((4, block, ff), bf16),
            sds((4, block, wide), bf16),
            sds((1, width), f32),
        ]
        + [sds((block, wide), bf16)] * 4,
        compiler_params=pltpu.CompilerParams(vmem_limit_bytes=VMEM_LIMIT),
        name="feed",
    )(meta, *parts, *slices, tokens, cotangent)


def pack_kernel(meta, nm_t, cot_t, att_t, ga_ref, gb_ref, gated_ref, gbr_ref, dgain_ref, out_ref):
    ff, wide = ga_ref.shape[2], gbr_ref.shape[2]
    bf16 = jnp.bfloat16

    width = nm_t.shape[0]
    gain = jnp.broadcast_to(dgain_ref[...], (128, width)).T
    last = out_ref.shape[2] - (3 * ff + wide)
    out_ref[0] = jnp.concatenate(
        [
            dot(nm_t[...], ga_ref[0], NN),
            dot(nm_t[...], gb_ref[0], NN),
            dot(cot_t[...], gated_ref[0], NN),
            dot(att_t[...], gbr_ref[0], NN),
            gain[:, :last],
        ],
        1,
    ).astype(bf16)


def pack_call(meta, normed, cotangent, attended, grad_a, grad_b, gated, grad_branch, d_gain, first):
    width, block = normed.shape
    ff, wide = grad_a.shape[2], grad_branch.shape[2]
    bf16 = jnp.bfloat16
    packed = padded(3 * ff + wide + 1)
    hid = pl.BlockSpec((1, block, ff), lambda i, m: (first + i, 0, 0))
    return pl.pallas_call(
        pack_kernel,
        grid_spec=pltpu.PrefetchScalarGridSpec(
            num_scalar_prefetch=1,
            grid=(2,),
            in_specs=[full((width, block))] * 3
            + [hid] * 3
            + [pl.BlockSpec((1, block, wide), lambda i, m: (m[first + i], 0, 0)), full((1, width))],
            out_specs=pl.BlockSpec((1, width, packed), lambda i, m: (i, 0, 0)),
        ),
        out_shape=jax.ShapeDtypeStruct((2, width, packed), bf16),
        compiler_params=pltpu.CompilerParams(vmem_limit_bytes=VMEM_LIMIT),
        name="pack",
    )(meta, normed, cotangent, attended, grad_a, grad_b, gated, grad_branch, d_gain)


def unproject_kernel(
    core, meta, normed_ref, dq_ref, dk_ref, dv_ref, w_ref, turn_ref, cos_ref, sin_ref, base_ref, *refs
):
    before_ref, (partial_ref, dw_ref, raw_ref, acc_ref) = refs[:-4], refs[-4:]
    wide = dk_ref.shape[2]
    i = pl.program_id(0)

    @pl.when(i == 0)
    def _():
        acc_ref[...] = before_ref[0][...] if before_ref else jnp.zeros_like(acc_ref)

    cos, sin = turned_tables(cos_ref[...], sin_ref[...], base_ref[0])

    def turn_back(grad):
        return (grad.astype(jnp.float32) * cos + dot(grad, turn_ref[...], NT) * sin).astype(jnp.bfloat16)

    mine = meta[0] == core
    raw_ref[:, wide : 2 * wide] = turn_back(dk_ref[0])
    raw_ref[:, 2 * wide : 3 * wide] = dv_ref[0]

    @pl.when(mine)
    def _():
        raw_ref[:, :wide] = turn_back(dq_ref[0])

    @pl.when(jnp.logical_not(mine))
    def _():
        raw_ref[:, :wide] = jnp.zeros_like(dk_ref[0])

    raw = raw_ref[...]
    partial_ref[0] = dot(raw, w_ref[:, : 3 * wide], NT).astype(jnp.bfloat16)
    acc_ref[...] += dot(normed_ref[0], raw, NN)

    @pl.when(i == pl.num_programs(0) - 1)
    def _():
        dw_ref[...] = acc_ref[...].astype(dw_ref.dtype)


def unproject_call(core, meta, normed_t, dq, dk, dv, w, turn, cos_row, sin_row, bases, *before):
    _, width, block = normed_t.shape
    wide = dk.shape[2]
    chunk = lambda i, m: (2 * i + core, 0, 0)
    one = lambda i, m: (i, 0, 0)
    return pl.pallas_call(
        functools.partial(unproject_kernel, core),
        grid_spec=pltpu.PrefetchScalarGridSpec(
            num_scalar_prefetch=1,
            grid=(4,),
            in_specs=[
                pl.BlockSpec((1, width, block), chunk),
                pl.BlockSpec((1, block, wide), one),
                pl.BlockSpec((1, block, wide), chunk),
                pl.BlockSpec((1, block, wide), chunk),
                full(w.shape),
                full(turn.shape),
                full(cos_row.shape),
                full(sin_row.shape),
                pl.BlockSpec((1, 2, wide), chunk),
            ]
            + [full((width, 3 * wide))] * len(before),
            out_specs=[pl.BlockSpec((1, block, width), one), full((width, 3 * wide))],
            scratch_shapes=[pltpu.VMEM((block, 3 * wide), jnp.bfloat16), pltpu.VMEM((width, 3 * wide), jnp.float32)],
        ),
        out_shape=[
            jax.ShapeDtypeStruct((4, block, width), jnp.bfloat16),
            jax.ShapeDtypeStruct((width, 3 * wide), jnp.bfloat16 if before else jnp.float32),
        ],
        compiler_params=pltpu.CompilerParams(vmem_limit_bytes=VMEM_LIMIT),
        name="unproject",
    )(meta, normed_t, dq, dk, dv, w, turn, cos_row, sin_row, bases, *before)


PLANE = ("ctx", "tensor")


def plane_permute(array, target):
    pairs = []
    for c in range(2):
        for x in range(2):
            for h in range(2):
                to_c, to_x, to_h = target(c, x, h)
                pairs.append((c * 4 + x * 2 + h, to_c * 4 + to_x * 2 + to_h))
    return lax.ppermute(array, PLANE, pairs)


def tensor_permute(array, flip):
    return lax.ppermute(array, "tensor", [(t, t ^ flip) for t in range(4)])


def pick(array, index, axis):
    return lax.dynamic_index_in_dim(array, index, axis, keepdims=False)


def local(tokens, doc_lengths, attn_gain, mlp_gain, w_qkv, w_attn_out, w_in, w_down, cotangent):
    _, block, width = tokens.shape
    assert lax.axis_size("ctx") == 2 and lax.axis_size("tensor") == 4 and tokens.shape[0] == 1
    rows = w_qkv.shape[0]
    ff = w_in.shape[2]
    docs = doc_lengths.shape[1]
    c = lax.axis_index("ctx")
    t = lax.axis_index("tensor")
    x, h = t // 2, t % 2
    wide = width // 4
    bf16 = jnp.bfloat16

    own = tokens[0]
    over_y = lambda c, x, h: (1 - c, x, h)
    shards = lax.axis_size("shard")
    shard_at = lax.axis_index("shard")

    def shard_gather(part):
        whole = jnp.zeros((shards,) + part.shape, part.dtype)
        pieces = [part]
        for k in range(1, shards):
            pieces.append(lax.ppermute(part, "shard", [(z, (z + k) % shards) for z in range(shards)]))
        for k, piece in enumerate(pieces):
            whole = lax.dynamic_update_index_in_dim(whole, piece, lax.rem(shard_at + shards - k, shards), 0)
        return whole

    def both_ctx(mine, other, axis):
        return jnp.where(c == 0, jnp.stack([mine, other], axis), jnp.stack([other, mine], axis))

    group_cols = pick(w_qkv.reshape(rows, 3, 4, wide), t, 2).reshape(rows, 3 * wide)
    gain_cols = padded(3 * wide + 1) - 3 * wide
    pack_1 = jnp.concatenate([group_cols, jnp.broadcast_to(attn_gain[:, None], (rows, gain_cols))], 1)
    own_cols = pick(w_attn_out.reshape(rows, 4, wide), t, 1)
    gain_cols = padded(3 * ff + wide + 1) - 3 * ff - wide
    pack_2 = jnp.concatenate(
        [w_in.reshape(rows, 2 * ff), w_down.T, own_cols, jnp.broadcast_to(mlp_gain[:, None], (rows, gain_cols))], 1
    )
    slice_flips = (0, 2, 1, 3)

    by_x = tensor_permute(own, 2)
    by_y = plane_permute(own, over_y)
    by_xy = plane_permute(own, lambda c, x, h: (1 - c, 1 - x, h))
    row_angles = angles(jnp.arange(block), wide)
    cos_row, sin_row = jnp.cos(row_angles), jnp.sin(row_angles)
    pack_1 = shard_gather(pack_1)
    pack_1, pack_2, cos_row, sin_row = lax.optimization_barrier((pack_1, pack_2, cos_row, sin_row))
    pack_1 = both_ctx(pack_1, plane_permute(pack_1, over_y), 1).reshape(width, -1)
    pack_2 = shard_gather(pack_2)
    pack_2_y = plane_permute(pack_2, over_y)
    chunks = [chunk for part in (own, by_x, by_y, by_xy) for chunk in (part, tensor_permute(part, 1))]

    chunk_at = []
    for dc in range(2):
        for dx in range(2):
            for dh in range(2):
                chunk_at.append(((c ^ dc) * 4 + (x ^ dx) * 2 + (h ^ dh)) * block)
    base_angles = angles(jnp.stack(chunk_at), wide)
    bases = jnp.stack([jnp.cos(base_angles), jnp.sin(base_angles)], 1)
    q_rows = block
    k_rows = min(512, block)
    pick_core = h ^ c
    key_starts = [at + k * k_rows for at in chunk_at for k in range(block // k_rows)]
    query_starts = [
        ((c ^ dc) * 4 + (x ^ dx) * 2 + c) * block
        for dc in range(2)
        for dx in range(2)
    ]
    doc_ends = jnp.cumsum(doc_lengths[0])[: docs - 1].astype(jnp.int32)
    meta = jnp.concatenate([doc_ends, jnp.stack(query_starts + key_starts + [pick_core]).astype(jnp.int32)])
    core_meta = jnp.stack([pick_core]).astype(jnp.int32)
    steps = [(a, b) for b in range(2) for a in range(2)]
    feed_meta = jnp.stack(
        [t ^ flip for flip in slice_flips] + [(x ^ b) * 2 + (c ^ a) for a, b in steps]
    ).astype(jnp.int32)

    turn = turn_matrix(wide)
    normed_t, query, key, value = project_call(core_meta, chunks, pack_1, turn, cos_row, sin_row, bases, wide)
    query, pack_2_y = lax.optimization_barrier((query, pack_2_y))
    pack_2 = both_ctx(pack_2, pack_2_y, 1).reshape(width, -1)
    query, pack_2 = lax.optimization_barrier((query, pack_2))
    slices = [pack_2, tensor_permute(pack_2, 2), tensor_permute(pack_2, 1)]
    query = query.reshape(1, 4 * block, wide)
    key = key.reshape(1, 8 * block, wide)
    value = value.reshape(1, 8 * block, wide)
    out, log_total = attend_call(meta, query, key, value, docs, q_rows, k_rows)

    out, slices[1] = lax.optimization_barrier((out, slices[1]))
    slices.append(tensor_permute(slices[1], 1))

    def forth(a, b):
        return lambda c, x, h: (h ^ a, x ^ b, c)

    def back(a, b):
        return lambda c, x, h: (h, x ^ b, c ^ a)

    out_parts = out.reshape(2, 2, block, wide)
    arrived = [plane_permute(out_parts[a, b], forth(a, b)) for a, b in steps]

    (layer_out, grad_hidden, normed_m, attended, cot_t, gated, grad_a, grad_b, grad_branch, d_gain_mlp, *grad_parts) = feed_call(
        feed_meta, arrived, slices, own, cotangent[0], ff
    )
    grad_parts = [plane_permute(part, back(a, b)) for part, (a, b) in zip(grad_parts, steps)]

    def add(one, two):
        return (one.astype(jnp.float32) + two.astype(jnp.float32)).astype(bf16)

    grads = (normed_m, cot_t, attended, grad_a, grad_b, gated, grad_branch, d_gain_mlp)
    sent_packs, grad_parts = lax.optimization_barrier((pack_call(feed_meta, *grads, 2), grad_parts))
    sent_packs = tensor_permute(sent_packs, 1)
    packs = add(pack_call(feed_meta, *grads, 0), sent_packs)
    packed = packs.shape[2]
    cut = padded(packed // 2)
    packs = packs.reshape(2, -1, 2, rows, packed)
    one_x = tensor_permute(packs[1, ..., :cut], 2)
    one_y = plane_permute(pick(packs[..., cut:], 1 - c, 2), over_y)
    kept_x, kept_y = packs[0, ..., :cut], pick(packs[..., cut:], c, 2)
    grad_parts, kept_x, kept_y = lax.optimization_barrier((grad_parts, kept_x, kept_y))

    grad_query, grad_key, grad_value = attend_back_call(
        meta, query, key, value, out, grad_parts, log_total, docs, q_rows, k_rows
    )
    kept_x, kept_y = add(kept_x, one_x), add(kept_y, one_y)
    grad_key, kept_x, kept_y = lax.optimization_barrier((grad_key, kept_x, kept_y))
    two_y = plane_permute(pick(kept_x, 1 - c, 1), over_y)
    two_x = tensor_permute(kept_y[1], 2)
    grad_query = grad_query.reshape(4, block, wide)
    grad_key = grad_key.reshape(8, block, wide)
    grad_value = grad_value.reshape(8, block, wide)
    rest = (grad_query, grad_key, grad_value, pack_1, turn, cos_row, sin_row, bases)
    partial, d_qkv = unproject_call(1, core_meta, normed_t, *rest)
    partial, d_qkv, two_x, two_y = lax.optimization_barrier((partial, d_qkv, two_x, two_y))
    pack = jnp.concatenate([add(pick(kept_x, c, 1), two_y), add(kept_y[0], two_x)], 2)
    from_core = tensor_permute(partial, 1)
    partial, d_qkv = unproject_call(0, core_meta, normed_t, *rest, d_qkv)

    chip_sum = [add(partial[n], from_core[n]) for n in range(4)]
    sent = [
        tensor_permute(chip_sum[1], 2),
        plane_permute(chip_sum[2], over_y),
        plane_permute(chip_sum[3], lambda c, x, h: (1 - c, 1 - x, h)),
    ]
    d_qkv, chip_sum = lax.optimization_barrier((d_qkv, chip_sum))
    d_qkv = d_qkv.reshape(-1, 2, rows, 3 * wide)
    d_qkv_y = plane_permute(pick(d_qkv, 1 - c, 1), over_y)
    d_qkv_own = pick(d_qkv, c, 1)

    def shard_sum(parts):
        total = pick(parts, shard_at, 0).astype(jnp.float32)
        for k in range(1, shards):
            part = pick(parts, lax.rem(shard_at + k, shards), 0)
            total = total + lax.ppermute(part, "shard", [(z, (z + k) % shards) for z in range(shards)]).astype(jnp.float32)
        return total

    pack = shard_sum(pack)
    d_in = pack[:, : 2 * ff].reshape(rows, 2, ff)
    d_down = pack[:, 2 * ff : 3 * ff].T
    d_group_out = pack[:, 3 * ff : 3 * ff + wide].astype(bf16)
    d_gain_mlp = pick(pack[:, 3 * ff + wide].reshape(4, rows // 4), t, 0)
    d_qkv = shard_sum(add(d_qkv_own, d_qkv_y)).astype(bf16)
    d_qkv, sent = lax.optimization_barrier((d_qkv, sent))
    d_both = jnp.concatenate([d_qkv, d_group_out], 1).reshape(4, rows // 4, 4 * wide)
    d_both = lax.all_to_all(d_both, "tensor", split_axis=0, concat_axis=0, tiled=True)
    d_both = d_both.reshape(4, rows // 4, 4, wide).transpose(1, 2, 0, 3).reshape(rows // 4, 4 * width)
    d_both = d_both.astype(jnp.float32)
    d_qkv, d_attn_out = d_both[:, : 3 * width], d_both[:, 3 * width :]
    own_rows = pick(w_qkv.reshape(4, rows // 4, 3 * width), t, 0).astype(jnp.float32)
    own_gain = pick(attn_gain.reshape(4, rows // 4), t, 0).astype(jnp.float32)
    d_gain_attn = jnp.sum(d_qkv * own_rows, 1) / own_gain

    grad_normed = chip_sum[0].astype(jnp.float32)
    for part in sent:
        grad_normed = grad_normed + part.astype(jnp.float32)
    gain_attn = pack_1[:, 3 * wide].astype(jnp.float32)
    _, norm_pull_attn = jax.vjp(lambda values: layer_norm(values, gain_attn), own.astype(jnp.float32))
    grad_tokens = grad_hidden + norm_pull_attn(grad_normed)[0]
    return (layer_out[None], grad_tokens[None], d_gain_attn, d_gain_mlp, d_qkv, d_attn_out, d_in, d_down)


def solution(mesh):
    return jax.shard_map(
        local,
        mesh=mesh,
        in_specs=(
            P("shard", ("ctx", "tensor"), None),
            P("shard", None),
            P(("shard", "ctx")),
            P(("shard", "ctx")),
            P(("shard", "ctx"), None),
            P(("shard", "ctx"), None),
            P(("shard", "ctx"), None, "tensor"),
            P("tensor", ("shard", "ctx")),
            P("shard", ("ctx", "tensor"), None),
        ),
        out_specs=(
            P("shard", ("ctx", "tensor"), None),
            P("shard", ("ctx", "tensor"), None),
            P(("shard", "ctx", "tensor")),
            P(("shard", "ctx", "tensor")),
            P(("shard", "ctx", "tensor"), None),
            P(("shard", "ctx", "tensor"), None),
            P(("shard", "ctx"), None, "tensor"),
            P("tensor", ("shard", "ctx")),
        ),
        check_vma=False,
    )
```

```python
import functools

import jax
import jax.numpy as jnp
from jax import lax
from jax.experimental import pallas as pl
from jax.experimental.pallas import tpu as pltpu
from jax.sharding import PartitionSpec as P

HEAD_DIM = 64
EPSILON = 1e-05
ROPE_THETA = 160000.0
SCORE_SCALE = 0.125
MASKED_SCORE = -1e30
ROOT_HALF = 0.7071067811865476
INVERSE_ROOT_TAU = 0.3989422804014327
VMEM_LIMIT = 56 * 1024 * 1024

NT = (((1,), (1,)), ((), ()))
NN = (((1,), (0,)), ((), ()))


def dot(a, b, dims):
    return lax.dot_general(a, b, dims, preferred_element_type=jnp.float32)


def seg_of(position, ends):
    seg = (position >= ends[0]).astype(jnp.int32)
    for end in ends[1:]:
        seg = seg + (position >= end).astype(jnp.int32)
    return seg


def stack_heads(values, group):
    lane_head = lax.broadcasted_iota(jnp.int32, values.shape, 1) // HEAD_DIM
    return jnp.concatenate(
        [jnp.where(lane_head == h, values, jnp.zeros_like(values)) for h in range(group)], 0
    )


def each_key_block(meta, docs, q_at, q_rows, k_first, k_rows, k_blocks, group, body, masked=True):
    ends = [meta[i] for i in range(docs - 1)]
    q_lo, q_hi = seg_of(q_at, ends), seg_of(q_at + q_rows - 1, ends)
    q_seg = seg_of(q_at + lax.broadcasted_iota(jnp.int32, (1, q_rows), 1), ends)
    q_seg = jnp.concatenate([q_seg] * group, 1)

    def step(j, carry):
        k_at = meta[k_first + j]
        half = k_rows // 2
        marks = [seg_of(k_at + n, ends) for n in (0, half - 1, half, k_rows - 1)]
        low = (marks[0] <= q_hi) & (q_lo <= marks[1])
        high = (marks[2] <= q_hi) & (q_lo <= marks[3])
        same = (marks[0] == marks[3]) & (q_lo == q_hi)

        def run(first, count):
            if not masked:
                return body(j * k_rows + first, count, None)
            k_seg = seg_of(k_at + first + lax.broadcasted_iota(jnp.int32, (count, 1), 0), ends)
            return body(j * k_rows + first, count, k_seg == q_seg)

        if masked:
            pl.when(low & high & same)(lambda: body(j * k_rows, k_rows, None))
        pl.when(low & high & jnp.logical_not(same) if masked else low & high)(lambda: run(0, k_rows))
        pl.when(low & jnp.logical_not(high))(lambda: run(0, half))
        pl.when(high & jnp.logical_not(low))(lambda: run(half, half))
        return carry

    lax.fori_loop(0, k_blocks, step, 0)


def attend_kernel(docs, k_rows, meta, q_ref, k_ref, v_ref, o_0, o_1, o_2, o_3, lse_ref, vt_ref, s_ref, m_ref, l_ref, acc_ref):
    q_rows, wide = q_ref.shape[1], q_ref.shape[2]
    group = wide // HEAD_DIM
    k_blocks = k_ref.shape[1] // k_rows
    q_blocks = pl.num_programs(1)
    i = pl.program_id(1)

    @pl.when(i == 0)
    def _():
        for j in range(k_blocks):
            at = pl.ds(j * k_rows, k_rows)
            vt_ref[:, at] = v_ref[0, at, :].T

    q_st = stack_heads(q_ref[0] * SCORE_SCALE, group)
    m_ref[...] = jnp.full(m_ref.shape, MASKED_SCORE, jnp.float32)
    l_ref[...] = jnp.zeros_like(l_ref)
    acc_ref[...] = jnp.zeros_like(acc_ref)
    place = (docs, meta[docs - 1 + i], q_rows, docs - 1 + q_blocks, k_rows, k_blocks, group)

    def find_top(first, count, mask):
        at = pl.ds(pl.multiple_of(first, k_rows // 2), count)
        scores = dot(k_ref[0, at, :], q_st, NT)
        if mask is not None:
            scores = jnp.where(mask, scores, MASKED_SCORE)
        s_ref[at, :] = scores
        m_ref[...] = jnp.maximum(m_ref[...], jnp.max(scores, 0, keepdims=True))

    each_key_block(meta, *place, find_top)
    row_top = m_ref[...]

    def add_up(first, count, mask):
        at = pl.ds(pl.multiple_of(first, k_rows // 2), count)
        weights = jnp.exp(s_ref[at, :] - row_top)
        l_ref[...] += jnp.sum(weights, 0, keepdims=True)
        low = weights.astype(jnp.bfloat16)
        for h in range(group):
            rows = pl.ds(h * HEAD_DIM, HEAD_DIM)
            cols = slice(h * q_rows, (h + 1) * q_rows)
            acc_ref[rows, :] += dot(vt_ref[rows, at], low[:, cols], NN)

    each_key_block(meta, *place, add_up, False)
    total = l_ref[...]
    outs = []
    for h in range(group):
        cols = slice(h * q_rows, (h + 1) * q_rows)
        outs.append(acc_ref[h * HEAD_DIM : (h + 1) * HEAD_DIM, :] / total[:, cols])
    result = jnp.concatenate(outs, 0).T.astype(jnp.bfloat16)
    goal = (i % 2) * 2 + ((i // 2) ^ meta[docs - 1 + q_blocks + k_blocks])
    for n, part in enumerate((o_0, o_1, o_2, o_3)):
        @pl.when(goal == n)
        def _(part=part):
            part[...] = result

    lse_ref[0, 0] = row_top + jnp.log(total)


def attend_back_kernel(
    docs, k_rows, meta, q_ref, k_ref, v_ref, o_0, o_1, o_2, o_3, do_0, do_1, do_2, do_3, lse_ref, dq_ref, dk_ref, dv_ref,
    kt_ref, dqt_ref, dk_acc, dv_acc, do_ref, o_ref,
):
    q_rows, wide = q_ref.shape[1], q_ref.shape[2]
    group = wide // HEAD_DIM
    k_blocks = k_ref.shape[1] // k_rows
    q_blocks = pl.num_programs(1)
    i = pl.program_id(1)

    @pl.when(i == 0)
    def _():
        dk_acc[...] = jnp.zeros_like(dk_acc)
        dv_acc[...] = jnp.zeros_like(dv_acc)
        for j in range(k_blocks):
            at = pl.ds(j * k_rows, k_rows)
            kt_ref[:, at] = k_ref[0, at, :].T

    q_st = stack_heads(q_ref[0] * SCORE_SCALE, group)
    source = (i % 2) * 2 + ((i // 2) ^ meta[docs - 1 + q_blocks + k_blocks])
    for n, (part, out) in enumerate(((do_0, o_0), (do_1, o_1), (do_2, o_2), (do_3, o_3))):
        @pl.when(source == n)
        def _(part=part, out=out):
            do_ref[...] = part[...]
            o_ref[...] = out[...]

    grad_out = do_ref[...]
    do_st = stack_heads(grad_out, group)
    product = (grad_out.astype(jnp.float32) * o_ref[...].astype(jnp.float32)).T
    delta = jnp.concatenate(
        [jnp.sum(product[h * HEAD_DIM : (h + 1) * HEAD_DIM], 0, keepdims=True) for h in range(group)], 1
    )
    log_total = lse_ref[0, 0]
    dqt_ref[...] = jnp.zeros_like(dqt_ref)

    def body(first, count, mask):
        at = pl.ds(pl.multiple_of(first, k_rows // 2), count)
        scores = dot(k_ref[0, at, :], q_st, NT)
        if mask is not None:
            scores = jnp.where(mask, scores, MASKED_SCORE)
        probs = jnp.exp(scores - log_total)
        dv_acc[at, :] += dot(probs.astype(jnp.bfloat16), do_st, NN)
        grad_probs = dot(v_ref[0, at, :], do_st, NT)
        grad_scores = (probs * (grad_probs - delta)).astype(jnp.bfloat16)
        dk_acc[at, :] += dot(grad_scores, q_st, NN)
        for h in range(group):
            rows = pl.ds(h * HEAD_DIM, HEAD_DIM)
            cols = slice(h * q_rows, (h + 1) * q_rows)
            dqt_ref[rows, :] += dot(kt_ref[rows, at], grad_scores[:, cols], NN)

    each_key_block(meta, docs, meta[docs - 1 + i], q_rows, docs - 1 + q_blocks, k_rows, k_blocks, group, body)
    dq_ref[0] = (dqt_ref[...].T * SCORE_SCALE).astype(jnp.bfloat16)

    @pl.when(i == q_blocks - 1)
    def _():
        dk_ref[0] = dk_acc[...].astype(jnp.bfloat16)
        dv_ref[0] = dv_acc[...].astype(jnp.bfloat16)


def attend_call(meta, query, key, value, docs, q_rows, k_rows):
    items, length, wide = query.shape
    keys = key.shape[1]
    group = wide // HEAD_DIM
    q_blocks = length // q_rows
    block = pl.BlockSpec((1, q_rows, wide), lambda g, i, m: (g, i, 0))
    whole = pl.BlockSpec((1, keys, wide), lambda g, i, m: (g, 0, 0))
    stat = pl.BlockSpec((1, 1, 1, group * q_rows), lambda g, i, m: (g, i, 0, 0))
    return pl.pallas_call(
        functools.partial(attend_kernel, docs, k_rows),
        grid_spec=pltpu.PrefetchScalarGridSpec(
            num_scalar_prefetch=1,
            grid=(items, q_blocks),
            in_specs=[block, whole, whole],
            out_specs=[full((q_rows, wide))] * 4 + [stat],
            scratch_shapes=[
                pltpu.VMEM((wide, keys), jnp.bfloat16),
                pltpu.VMEM((keys, group * q_rows), jnp.float32),
                pltpu.VMEM((1, group * q_rows), jnp.float32),
                pltpu.VMEM((1, group * q_rows), jnp.float32),
                pltpu.VMEM((wide, q_rows), jnp.float32),
            ],
        ),
        out_shape=[jax.ShapeDtypeStruct((q_rows, wide), jnp.bfloat16)] * 4
        + [jax.ShapeDtypeStruct((items, q_blocks, 1, group * q_rows), jnp.float32)],
        compiler_params=pltpu.CompilerParams(vmem_limit_bytes=VMEM_LIMIT),
        name="attend",
    )(meta, query, key, value)


def attend_back_call(meta, query, key, value, out, grad_parts, log_total, docs, q_rows, k_rows):
    items, length, wide = query.shape
    keys = key.shape[1]
    group = wide // HEAD_DIM
    q_blocks = length // q_rows
    block = pl.BlockSpec((1, q_rows, wide), lambda g, i, m: (g, i, 0))
    whole = pl.BlockSpec((1, keys, wide), lambda g, i, m: (g, 0, 0))
    stat = pl.BlockSpec((1, 1, 1, group * q_rows), lambda g, i, m: (g, i, 0, 0))
    return pl.pallas_call(
        functools.partial(attend_back_kernel, docs, k_rows),
        grid_spec=pltpu.PrefetchScalarGridSpec(
            num_scalar_prefetch=1,
            grid=(items, q_blocks),
            in_specs=[block, whole, whole] + [full((q_rows, wide))] * 8 + [stat],
            out_specs=[block, whole, whole],
            scratch_shapes=[
                pltpu.VMEM((wide, keys), jnp.bfloat16),
                pltpu.VMEM((wide, q_rows), jnp.float32),
                pltpu.VMEM((keys, wide), jnp.float32),
                pltpu.VMEM((keys, wide), jnp.float32),
                pltpu.VMEM((q_rows, wide), jnp.bfloat16),
                pltpu.VMEM((q_rows, wide), jnp.bfloat16),
            ],
        ),
        out_shape=[
            jax.ShapeDtypeStruct(query.shape, jnp.bfloat16),
            jax.ShapeDtypeStruct(key.shape, jnp.bfloat16),
            jax.ShapeDtypeStruct(key.shape, jnp.bfloat16),
        ],
        compiler_params=pltpu.CompilerParams(vmem_limit_bytes=VMEM_LIMIT),
        name="attend_back",
    )(meta, query, key, value, *out, *grad_parts, log_total)


def layer_norm(values, gain):
    mean_value = jnp.mean(values, -1, keepdims=True)
    centred = values - mean_value
    spread = jnp.mean(centred * centred, -1, keepdims=True)
    return centred * lax.rsqrt(spread + EPSILON) * gain


def norm_parts(values):
    centred = values - jnp.mean(values, -1, keepdims=True)
    inverse = lax.rsqrt(jnp.mean(centred * centred, -1, keepdims=True) + EPSILON)
    return centred * inverse, inverse


def turn_matrix(width):
    row = lax.broadcasted_iota(jnp.int32, (width, width), 0)
    col = lax.broadcasted_iota(jnp.int32, (width, width), 1)
    half = HEAD_DIM // 2
    first = (col % HEAD_DIM) < half
    plus = jnp.logical_not(first) & (row == col - half)
    minus = first & (row == col + half)
    return plus.astype(jnp.bfloat16) - minus.astype(jnp.bfloat16)


def angles(positions, width):
    half = HEAD_DIM // 2
    steps_index = (jnp.arange(width) % half).astype(jnp.float32)
    inverse = ROPE_THETA ** (-2.0 * steps_index / HEAD_DIM)
    return positions.astype(jnp.float32)[:, None] * inverse[None, :]


def turned_tables(cos_row, sin_row, base):
    cos_base, sin_base = base[0:1, :], base[1:2, :]
    return cos_row * cos_base - sin_row * sin_base, sin_row * cos_base + cos_row * sin_base


def full(shape):
    return pl.BlockSpec(shape, lambda *_: (0,) * len(shape))


def padded(wide):
    return -(-wide // 128) * 128


def project_kernel(meta, *refs):
    chunk_refs = refs[:8]
    w_ref, turn_ref, cos_ref, sin_ref, base_ref, normed_ref, q_ref, k_ref, v_ref, x_ref, w_all, gain_row = refs[8:]
    wide = q_ref.shape[2]
    slot = padded(wide)
    i = pl.program_id(0)
    bf16 = jnp.bfloat16

    @pl.when(i == 0)
    def _():
        for p, at in ((1, 0), (2, 2), (0, 3)):
            w_all[:, at * slot : at * slot + wide] = w_ref[:, p * wide : (p + 1) * wide]
        for p, at in ((1, 1), (0, 4)):
            turned = dot(w_ref[:, p * wide : (p + 1) * wide], turn_ref[...], NN)
            w_all[:, at * slot : at * slot + wide] = turned.astype(bf16)
        last = w_ref[:, w_ref.shape[1] - 128 :].astype(jnp.float32).T
        gain_row[...] = last[127:128, :]

    for n in range(8):
        @pl.when(i == n)
        def _(n=n):
            x_ref[...] = chunk_refs[n][...]

    normed, _ = norm_parts(x_ref[...].astype(jnp.float32))
    normed = (normed * gain_row[...]).astype(bf16)
    normed_ref[0] = normed.T
    cos, sin = turned_tables(cos_ref[...], sin_ref[...], base_ref[0])
    raw = dot(normed, w_all[:, : 3 * slot], NN)
    k_ref[0] = (raw[:, :wide] * cos + raw[:, slot : slot + wide] * sin).astype(bf16)
    v_ref[0] = raw[:, 2 * slot : 2 * slot + wide].astype(bf16)

    @pl.when(i % 2 == meta[0])
    def _():
        raw_q = dot(normed, w_all[:, 3 * slot : 5 * slot], NN)
        q_ref[0] = (raw_q[:, :wide] * cos + raw_q[:, slot : slot + wide] * sin).astype(bf16)


def project_call(meta, chunks, w, turn, cos_row, sin_row, bases, wide):
    block, width = chunks[0].shape
    bf16 = jnp.bfloat16
    one = lambda i, m: (i, 0, 0)
    return pl.pallas_call(
        project_kernel,
        grid_spec=pltpu.PrefetchScalarGridSpec(
            num_scalar_prefetch=1,
            grid=(8,),
            in_specs=[full((block, width))] * 8
            + [full(w.shape), full(turn.shape), full(cos_row.shape), full(sin_row.shape), pl.BlockSpec((1, 2, wide), one)],
            out_specs=[
                pl.BlockSpec((1, width, block), one),
                pl.BlockSpec((1, block, wide), lambda i, m: (i // 2, 0, 0)),
                pl.BlockSpec((1, block, wide), one),
                pl.BlockSpec((1, block, wide), one),
            ],
            scratch_shapes=[
                pltpu.VMEM((block, width), bf16),
                pltpu.VMEM((width, 5 * padded(wide)), bf16),
                pltpu.VMEM((1, width), jnp.float32),
            ],
        ),
        out_shape=[
            jax.ShapeDtypeStruct((8, width, block), bf16),
            jax.ShapeDtypeStruct((4, block, wide), bf16),
            jax.ShapeDtypeStruct((8, block, wide), bf16),
            jax.ShapeDtypeStruct((8, block, wide), bf16),
        ],
        compiler_params=pltpu.CompilerParams(vmem_limit_bytes=VMEM_LIMIT),
        name="project",
    )(meta, *chunks, w, turn, cos_row, sin_row, bases)


def feed_kernel(ff, meta, *refs):
    parts, slices = refs[0:4], refs[4:8]
    tok_ref, cot_ref = refs[8:10]
    out_ref, gh_ref, normed_ref, att_ref, cot_t_ref, gated_ref, ga_ref, gb_ref, gbr_ref, dgain_ref = refs[10:20]
    grad_parts = refs[20:24]
    w_a, w_b, w_dt, w_o, gain_row, att_scr = refs[24:30]
    wide = parts[0].shape[1]
    i = pl.program_id(0)
    bf16 = jnp.bfloat16

    @pl.when(i == 0)
    def _():
        for n in range(4):
            at = slice(n * ff, (n + 1) * ff)
            w_a[:, at] = slices[n][:, :ff]
            w_b[:, at] = slices[n][:, ff : 2 * ff]
            w_dt[:, at] = slices[n][:, 2 * ff : 3 * ff]
            for g in range(4):
                @pl.when(meta[n] == g)
                def _(n=n, g=g):
                    w_o[:, g * wide : (g + 1) * wide] = slices[n][:, 3 * ff : 3 * ff + wide]
        last = slices[0][:, slices[0].shape[1] - 128 :].astype(jnp.float32).T
        gain_row[...] = last[127:128, :]
        dgain_ref[...] = jnp.zeros_like(dgain_ref)

    for g in range(4):
        for n in range(4):
            @pl.when(meta[4 + n] == g)
            def _(n=n, g=g):
                att_scr[:, g * wide : (g + 1) * wide] = parts[n][...]

    attended = att_scr[...]
    att_ref[...] = attended.T
    gain = gain_row[...]
    hidden = tok_ref[...].astype(jnp.float32) + dot(attended, w_o[...], NN)
    normal, inverse = norm_parts(hidden)
    normed = (normal * gain).astype(bf16)
    normed_ref[...] = normed.T
    half_a = dot(normed, w_a[...], NN)
    half_b = dot(normed, w_b[...], NN)
    phi = 0.5 * (1.0 + lax.erf(half_a * ROOT_HALF))
    gelu = half_a * phi
    slope = phi + half_a * (jnp.exp(-0.5 * half_a * half_a) * INVERSE_ROOT_TAU)
    gated = (gelu * half_b).astype(bf16)
    out_ref[...] = (hidden + dot(gated, w_dt[...], NT)).astype(bf16)
    cot = cot_ref[...]
    cot_t_ref[...] = cot.T
    grad_gated = dot(cot, w_dt[...], NN)
    grad_a = (grad_gated * half_b * slope).astype(bf16)
    grad_b = (grad_gated * gelu).astype(bf16)
    for n in range(4):
        at = slice(n * ff, (n + 1) * ff)
        gated_ref[n] = gated[:, at]
        ga_ref[n] = grad_a[:, at]
        gb_ref[n] = grad_b[:, at]
    grad_normed = dot(grad_a, w_a[...], NT) + dot(grad_b, w_b[...], NT)
    dgain_ref[...] += jnp.sum(grad_normed * normal, 0, keepdims=True)
    scaled = grad_normed * gain
    inner = jnp.mean(scaled * normal, -1, keepdims=True)
    grad_hidden = cot.astype(jnp.float32) + inverse * (
        scaled - jnp.mean(scaled, -1, keepdims=True) - normal * inner
    )
    gh_ref[...] = grad_hidden
    grad_branch = grad_hidden.astype(bf16)
    for g in range(4):
        gbr_ref[g] = grad_branch[:, g * wide : (g + 1) * wide]
    grad_mixed = dot(grad_branch, w_o[...], NT).astype(bf16)
    for g in range(4):
        for n in range(4):
            @pl.when(meta[4 + n] == g)
            def _(n=n, g=g):
                grad_parts[n][...] = grad_mixed[:, g * wide : (g + 1) * wide]


def feed_call(meta, parts, slices, tokens, cotangent, ff):
    block, width = tokens.shape
    wide = parts[0].shape[1]
    bf16, f32 = jnp.bfloat16, jnp.float32
    rows = min(256, block)
    part = pl.BlockSpec((rows, wide), lambda i, m: (i, 0))
    row = pl.BlockSpec((rows, width), lambda i, m: (i, 0))
    hid = pl.BlockSpec((4, rows, ff), lambda i, m: (0, i, 0))
    flat = pl.BlockSpec((width, rows), lambda i, m: (0, i))
    grp = pl.BlockSpec((4, rows, wide), lambda i, m: (0, i, 0))
    sds = jax.ShapeDtypeStruct
    return pl.pallas_call(
        functools.partial(feed_kernel, ff),
        grid_spec=pltpu.PrefetchScalarGridSpec(
            num_scalar_prefetch=1,
            grid=(block // rows,),
            in_specs=[part] * 4 + [full(slices[0].shape)] * 4 + [row, row],
            out_specs=[row, row, flat, flat, flat, hid, hid, hid, grp, full((1, width))] + [part] * 4,
            scratch_shapes=[pltpu.VMEM((width, 4 * ff), bf16)] * 3
            + [pltpu.VMEM((width, width), bf16), pltpu.VMEM((1, width), f32), pltpu.VMEM((rows, width), bf16)],
        ),
        out_shape=[
            sds((block, width), bf16),
            sds((block, width), f32),
            sds((width, block), bf16),
            sds((width, block), bf16),
            sds((width, block), bf16),
            sds((4, block, ff), bf16),
            sds((4, block, ff), bf16),
            sds((4, block, ff), bf16),
            sds((4, block, wide), bf16),
            sds((1, width), f32),
        ]
        + [sds((block, wide), bf16)] * 4,
        compiler_params=pltpu.CompilerParams(vmem_limit_bytes=VMEM_LIMIT),
        name="feed",
    )(meta, *parts, *slices, tokens, cotangent)


def pack_kernel(meta, nm_t, cot_t, att_t, ga_ref, gb_ref, gated_ref, gbr_ref, dgain_ref, out_ref):
    ff, wide = ga_ref.shape[2], gbr_ref.shape[2]
    bf16 = jnp.bfloat16

    width = nm_t.shape[0]
    gain = jnp.broadcast_to(dgain_ref[...], (128, width)).T
    last = out_ref.shape[2] - (3 * ff + wide)
    out_ref[0] = jnp.concatenate(
        [
            dot(nm_t[...], ga_ref[0], NN),
            dot(nm_t[...], gb_ref[0], NN),
            dot(cot_t[...], gated_ref[0], NN),
            dot(att_t[...], gbr_ref[0], NN),
            gain[:, :last],
        ],
        1,
    ).astype(bf16)


def pack_call(meta, normed, cotangent, attended, grad_a, grad_b, gated, grad_branch, d_gain, first):
    width, block = normed.shape
    ff, wide = grad_a.shape[2], grad_branch.shape[2]
    bf16 = jnp.bfloat16
    packed = padded(3 * ff + wide + 1)
    hid = pl.BlockSpec((1, block, ff), lambda i, m: (first + i, 0, 0))
    return pl.pallas_call(
        pack_kernel,
        grid_spec=pltpu.PrefetchScalarGridSpec(
            num_scalar_prefetch=1,
            grid=(2,),
            in_specs=[full((width, block))] * 3
            + [hid] * 3
            + [pl.BlockSpec((1, block, wide), lambda i, m: (m[first + i], 0, 0)), full((1, width))],
            out_specs=pl.BlockSpec((1, width, packed), lambda i, m: (i, 0, 0)),
        ),
        out_shape=jax.ShapeDtypeStruct((2, width, packed), bf16),
        compiler_params=pltpu.CompilerParams(vmem_limit_bytes=VMEM_LIMIT),
        name="pack",
    )(meta, normed, cotangent, attended, grad_a, grad_b, gated, grad_branch, d_gain)


def unturn_kernel(meta, normed_ref, dq_ref, dk_ref, dv_ref, turn_ref, cos_ref, sin_ref, base_ref, raw_ref, dw_ref, acc_ref):
    wide = dk_ref.shape[2]
    i = pl.program_id(0)

    @pl.when(i == 0)
    def _():
        acc_ref[...] = jnp.zeros_like(acc_ref)

    cos, sin = turned_tables(cos_ref[...], sin_ref[...], base_ref[0])

    def turn_back(grad):
        return (grad.astype(jnp.float32) * cos + dot(grad, turn_ref[...], NT) * sin).astype(jnp.bfloat16)

    mine = meta[0] == i % 2
    raw_ref[0, :, wide : 2 * wide] = turn_back(dk_ref[0])
    raw_ref[0, :, 2 * wide : 3 * wide] = dv_ref[0]

    @pl.when(mine)
    def _():
        raw_ref[0, :, :wide] = turn_back(dq_ref[0])

    @pl.when(jnp.logical_not(mine))
    def _():
        raw_ref[0, :, :wide] = jnp.zeros_like(dk_ref[0])

    acc_ref[...] += dot(normed_ref[0], raw_ref[0], NN)

    @pl.when(i == pl.num_programs(0) - 1)
    def _():
        dw_ref[...] = acc_ref[...].astype(jnp.bfloat16)


def unturn_call(meta, normed_t, dq, dk, dv, turn, cos_row, sin_row, bases):
    _, width, block = normed_t.shape
    wide = dk.shape[2]
    one = lambda i, m: (i, 0, 0)
    return pl.pallas_call(
        unturn_kernel,
        grid_spec=pltpu.PrefetchScalarGridSpec(
            num_scalar_prefetch=1,
            grid=(8,),
            in_specs=[
                pl.BlockSpec((1, width, block), one),
                pl.BlockSpec((1, block, wide), lambda i, m: (i // 2, 0, 0)),
                pl.BlockSpec((1, block, wide), one),
                pl.BlockSpec((1, block, wide), one),
                full(turn.shape),
                full(cos_row.shape),
                full(sin_row.shape),
                pl.BlockSpec((1, 2, wide), one),
            ],
            out_specs=[pl.BlockSpec((1, block, 3 * wide), one), full((width, 3 * wide))],
            scratch_shapes=[pltpu.VMEM((width, 3 * wide), jnp.float32)],
        ),
        out_shape=[
            jax.ShapeDtypeStruct((8, block, 3 * wide), jnp.bfloat16),
            jax.ShapeDtypeStruct((width, 3 * wide), jnp.bfloat16),
        ],
        compiler_params=pltpu.CompilerParams(vmem_limit_bytes=VMEM_LIMIT),
        name="unturn",
    )(meta, normed_t, dq, dk, dv, turn, cos_row, sin_row, bases)


def unproject_kernel(raw_ref, w_ref, partial_ref):
    partial_ref[0] = dot(raw_ref[0], w_ref[:, : raw_ref.shape[2]], NT).astype(jnp.bfloat16)


def unproject_call(core, grad_raw, w):
    _, block, columns = grad_raw.shape
    width = w.shape[0]
    return pl.pallas_call(
        unproject_kernel,
        grid=(4,),
        in_specs=[pl.BlockSpec((1, block, columns), lambda i: (2 * i + core, 0, 0)), full(w.shape)],
        out_specs=pl.BlockSpec((1, block, width), lambda i: (i, 0, 0)),
        out_shape=jax.ShapeDtypeStruct((4, block, width), jnp.bfloat16),
        compiler_params=pltpu.CompilerParams(vmem_limit_bytes=VMEM_LIMIT),
        name="unproject",
    )(grad_raw, w)


PLANE = ("ctx", "tensor")


def plane_permute(array, target):
    pairs = []
    for c in range(2):
        for x in range(2):
            for h in range(2):
                to_c, to_x, to_h = target(c, x, h)
                pairs.append((c * 4 + x * 2 + h, to_c * 4 + to_x * 2 + to_h))
    return lax.ppermute(array, PLANE, pairs)


def tensor_permute(array, flip):
    return lax.ppermute(array, "tensor", [(t, t ^ flip) for t in range(4)])


def pick(array, index, axis):
    return lax.dynamic_index_in_dim(array, index, axis, keepdims=False)


def local(tokens, doc_lengths, attn_gain, mlp_gain, w_qkv, w_attn_out, w_in, w_down, cotangent):
    _, block, width = tokens.shape
    assert lax.axis_size("ctx") == 2 and lax.axis_size("tensor") == 4 and tokens.shape[0] == 1
    rows = w_qkv.shape[0]
    ff = w_in.shape[2]
    docs = doc_lengths.shape[1]
    c = lax.axis_index("ctx")
    t = lax.axis_index("tensor")
    x, h = t // 2, t % 2
    wide = width // 4
    bf16 = jnp.bfloat16

    own = tokens[0]
    over_y = lambda c, x, h: (1 - c, x, h)
    shards = lax.axis_size("shard")
    shard_at = lax.axis_index("shard")

    def shard_gather(part):
        whole = jnp.zeros((shards,) + part.shape, part.dtype)
        pieces = [part]
        for k in range(1, shards):
            pieces.append(lax.ppermute(part, "shard", [(z, (z + k) % shards) for z in range(shards)]))
        for k, piece in enumerate(pieces):
            whole = lax.dynamic_update_index_in_dim(whole, piece, lax.rem(shard_at + shards - k, shards), 0)
        return whole

    def both_ctx(mine, other, axis):
        return jnp.where(c == 0, jnp.stack([mine, other], axis), jnp.stack([other, mine], axis))

    group_cols = pick(w_qkv.reshape(rows, 3, 4, wide), t, 2).reshape(rows, 3 * wide)
    gain_cols = padded(3 * wide + 1) - 3 * wide
    pack_1 = jnp.concatenate([group_cols, jnp.broadcast_to(attn_gain[:, None], (rows, gain_cols))], 1)
    own_cols = pick(w_attn_out.reshape(rows, 4, wide), t, 1)
    gain_cols = padded(3 * ff + wide + 1) - 3 * ff - wide
    pack_2 = jnp.concatenate(
        [w_in.reshape(rows, 2 * ff), w_down.T, own_cols, jnp.broadcast_to(mlp_gain[:, None], (rows, gain_cols))], 1
    )
    slice_flips = (0, 2, 1, 3)

    by_x = tensor_permute(own, 2)
    by_y = plane_permute(own, over_y)
    by_xy = plane_permute(own, lambda c, x, h: (1 - c, 1 - x, h))
    row_angles = angles(jnp.arange(block), wide)
    cos_row, sin_row = jnp.cos(row_angles), jnp.sin(row_angles)
    pack_1 = shard_gather(pack_1)
    pack_1, pack_2, cos_row, sin_row = lax.optimization_barrier((pack_1, pack_2, cos_row, sin_row))
    pack_1_y, pack_2 = lax.optimization_barrier((plane_permute(pack_1, over_y), shard_gather(pack_2)))
    pack_1 = both_ctx(pack_1, pack_1_y, 1).reshape(width, -1)
    pack_2_y = plane_permute(pack_2, over_y)
    chunks = [chunk for part in (own, by_x, by_y, by_xy) for chunk in (part, tensor_permute(part, 1))]

    chunk_at = []
    for dc in range(2):
        for dx in range(2):
            for dh in range(2):
                chunk_at.append(((c ^ dc) * 4 + (x ^ dx) * 2 + (h ^ dh)) * block)
    base_angles = angles(jnp.stack(chunk_at), wide)
    bases = jnp.stack([jnp.cos(base_angles), jnp.sin(base_angles)], 1)
    q_rows = block
    k_rows = min(512, block)
    pick_core = h ^ c
    key_starts = [at + k * k_rows for at in chunk_at for k in range(block // k_rows)]
    query_starts = [
        ((c ^ dc) * 4 + (x ^ dx) * 2 + c) * block
        for dc in range(2)
        for dx in range(2)
    ]
    doc_ends = jnp.cumsum(doc_lengths[0])[: docs - 1].astype(jnp.int32)
    meta = jnp.concatenate([doc_ends, jnp.stack(query_starts + key_starts + [pick_core]).astype(jnp.int32)])
    core_meta = jnp.stack([pick_core]).astype(jnp.int32)
    steps = [(a, b) for b in range(2) for a in range(2)]
    feed_meta = jnp.stack(
        [t ^ flip for flip in slice_flips] + [(x ^ b) * 2 + (c ^ a) for a, b in steps]
    ).astype(jnp.int32)

    turn = turn_matrix(wide)
    normed_t, query, key, value = project_call(core_meta, chunks, pack_1, turn, cos_row, sin_row, bases, wide)
    query, pack_2_y = lax.optimization_barrier((query, pack_2_y))
    pack_2 = both_ctx(pack_2, pack_2_y, 1).reshape(width, -1)
    query, pack_2 = lax.optimization_barrier((query, pack_2))
    slices = [pack_2, tensor_permute(pack_2, 2), tensor_permute(pack_2, 1)]
    query = query.reshape(1, 4 * block, wide)
    key = key.reshape(1, 8 * block, wide)
    value = value.reshape(1, 8 * block, wide)
    *out, log_total = attend_call(meta, query, key, value, docs, q_rows, k_rows)

    out, slices[1] = lax.optimization_barrier((out, slices[1]))
    slices.append(tensor_permute(slices[1], 1))

    def forth(a, b):
        return lambda c, x, h: (h ^ a, x ^ b, c)

    def back(a, b):
        return lambda c, x, h: (h, x ^ b, c ^ a)

    arrived = [plane_permute(part, forth(a, b)) for part, (a, b) in zip(out, steps)]

    (layer_out, grad_hidden, normed_m, attended, cot_t, gated, grad_a, grad_b, grad_branch, d_gain_mlp, *grad_parts) = feed_call(
        feed_meta, arrived, slices, own, cotangent[0], ff
    )
    grad_parts = [plane_permute(part, back(a, b)) for part, (a, b) in zip(grad_parts, steps)]

    def add(one, two):
        return (one.astype(jnp.float32) + two.astype(jnp.float32)).astype(bf16)

    grads = (normed_m, cot_t, attended, grad_a, grad_b, gated, grad_branch, d_gain_mlp)
    sent_packs, grad_parts = lax.optimization_barrier((pack_call(feed_meta, *grads, 2), grad_parts))
    sent_packs = tensor_permute(sent_packs, 1)
    packs = add(pack_call(feed_meta, *grads, 0), sent_packs)
    packed = packs.shape[2]
    cut = padded(packed // 2)
    packs = packs.reshape(2, -1, 2, rows, packed)
    one_x = tensor_permute(packs[1, ..., :cut], 2)
    one_y = plane_permute(pick(packs[..., cut:], 1 - c, 2), over_y)
    kept_x, kept_y = packs[0, ..., :cut], pick(packs[..., cut:], c, 2)
    grad_parts, kept_x, kept_y = lax.optimization_barrier((grad_parts, kept_x, kept_y))

    grad_query, grad_key, grad_value = attend_back_call(
        meta, query, key, value, out, grad_parts, log_total, docs, q_rows, k_rows
    )
    kept_x, kept_y = add(kept_x, one_x), add(kept_y, one_y)
    grad_key, kept_x, kept_y = lax.optimization_barrier((grad_key, kept_x, kept_y))
    two_y = plane_permute(pick(kept_x, 1 - c, 1), over_y)
    two_x = tensor_permute(kept_y[1], 2)
    grad_query = grad_query.reshape(4, block, wide)
    grad_key = grad_key.reshape(8, block, wide)
    grad_value = grad_value.reshape(8, block, wide)
    grad_raw, d_qkv = unturn_call(
        core_meta, normed_t, grad_query, grad_key, grad_value, turn, cos_row, sin_row, bases
    )
    grad_raw, d_qkv, two_x, two_y = lax.optimization_barrier((grad_raw, d_qkv, two_x, two_y))
    pack = jnp.concatenate([add(pick(kept_x, c, 1), two_y), add(kept_y[0], two_x)], 2)
    d_qkv = d_qkv.reshape(-1, 2, rows, 3 * wide)
    d_qkv_y = plane_permute(pick(d_qkv, 1 - c, 1), over_y)
    d_qkv_own = pick(d_qkv, c, 1)
    from_core = tensor_permute(unproject_call(1, grad_raw, pack_1), 1)
    partial = unproject_call(0, grad_raw, pack_1)

    chip_sum = [add(partial[n], from_core[n]) for n in range(4)]
    sent = [
        tensor_permute(chip_sum[1], 2),
        plane_permute(chip_sum[2], over_y),
        plane_permute(chip_sum[3], lambda c, x, h: (1 - c, 1 - x, h)),
    ]
    pack, d_qkv_y, chip_sum = lax.optimization_barrier((pack, d_qkv_y, chip_sum))
    d_qkv_y, sent[0] = lax.optimization_barrier((d_qkv_y, sent[0]))

    def shard_sum(parts):
        total = pick(parts, shard_at, 0).astype(jnp.float32)
        for k in range(1, shards):
            part = pick(parts, lax.rem(shard_at + k, shards), 0)
            total = total + lax.ppermute(part, "shard", [(z, (z + k) % shards) for z in range(shards)]).astype(jnp.float32)
        return total

    pack = shard_sum(pack)
    d_in = pack[:, : 2 * ff].reshape(rows, 2, ff)
    d_down = pack[:, 2 * ff : 3 * ff].T
    d_group_out = pack[:, 3 * ff : 3 * ff + wide].astype(bf16)
    d_gain_mlp = pick(pack[:, 3 * ff + wide].reshape(4, rows // 4), t, 0)
    d_qkv = shard_sum(add(d_qkv_own, d_qkv_y)).astype(bf16)
    d_qkv, sent = lax.optimization_barrier((d_qkv, sent))
    d_both = jnp.concatenate([d_qkv, d_group_out], 1).reshape(4, rows // 4, 4 * wide)
    d_both = lax.all_to_all(d_both, "tensor", split_axis=0, concat_axis=0, tiled=True)
    d_both = d_both.reshape(4, rows // 4, 4, wide).transpose(1, 2, 0, 3).reshape(rows // 4, 4 * width)
    d_both = d_both.astype(jnp.float32)
    d_qkv, d_attn_out = d_both[:, : 3 * width], d_both[:, 3 * width :]
    own_rows = pick(w_qkv.reshape(4, rows // 4, 3 * width), t, 0).astype(jnp.float32)
    own_gain = pick(attn_gain.reshape(4, rows // 4), t, 0).astype(jnp.float32)
    d_gain_attn = jnp.sum(d_qkv * own_rows, 1) / own_gain

    grad_normed = chip_sum[0].astype(jnp.float32)
    for part in sent:
        grad_normed = grad_normed + part.astype(jnp.float32)
    gain_attn = pack_1[:, 3 * wide].astype(jnp.float32)
    _, norm_pull_attn = jax.vjp(lambda values: layer_norm(values, gain_attn), own.astype(jnp.float32))
    grad_tokens = grad_hidden + norm_pull_attn(grad_normed)[0]
    return (layer_out[None], grad_tokens[None], d_gain_attn, d_gain_mlp, d_qkv, d_attn_out, d_in, d_down)


def solution(mesh):
    return jax.shard_map(
        local,
        mesh=mesh,
        in_specs=(
            P("shard", ("ctx", "tensor"), None),
            P("shard", None),
            P(("shard", "ctx")),
            P(("shard", "ctx")),
            P(("shard", "ctx"), None),
            P(("shard", "ctx"), None),
            P(("shard", "ctx"), None, "tensor"),
            P("tensor", ("shard", "ctx")),
            P("shard", ("ctx", "tensor"), None),
        ),
        out_specs=(
            P("shard", ("ctx", "tensor"), None),
            P("shard", ("ctx", "tensor"), None),
            P(("shard", "ctx", "tensor")),
            P(("shard", "ctx", "tensor")),
            P(("shard", "ctx", "tensor"), None),
            P(("shard", "ctx", "tensor"), None),
            P(("shard", "ctx"), None, "tensor"),
            P("tensor", ("shard", "ctx")),
        ),
        check_vma=False,
    )
```

```python
import functools

import jax
import jax.numpy as jnp
from jax import lax
from jax.experimental import pallas as pl
from jax.experimental.pallas import tpu as pltpu
from jax.sharding import PartitionSpec as P

HEAD_DIM = 64
EPSILON = 1e-05
ROPE_THETA = 160000.0
SCORE_SCALE = 0.125
MASKED_SCORE = -1e30
ROOT_HALF = 0.7071067811865476
INVERSE_ROOT_TAU = 0.3989422804014327
VMEM_LIMIT = 56 * 1024 * 1024

NT = (((1,), (1,)), ((), ()))
NN = (((1,), (0,)), ((), ()))


def dot(a, b, dims):
    return lax.dot_general(a, b, dims, preferred_element_type=jnp.float32)


def seg_of(position, ends):
    seg = (position >= ends[0]).astype(jnp.int32)
    for end in ends[1:]:
        seg = seg + (position >= end).astype(jnp.int32)
    return seg


def stack_heads(values, group):
    lane_head = lax.broadcasted_iota(jnp.int32, values.shape, 1) // HEAD_DIM
    return jnp.concatenate(
        [jnp.where(lane_head == h, values, jnp.zeros_like(values)) for h in range(group)], 0
    )


def each_key_block(meta, docs, q_at, q_rows, k_first, k_rows, k_blocks, group, body, masked=True):
    ends = [meta[i] for i in range(docs - 1)]
    q_lo, q_hi = seg_of(q_at, ends), seg_of(q_at + q_rows - 1, ends)
    q_seg = seg_of(q_at + lax.broadcasted_iota(jnp.int32, (1, q_rows), 1), ends)
    q_seg = jnp.concatenate([q_seg] * group, 1)

    def step(j, carry):
        k_at = meta[k_first + j]
        half = k_rows // 2
        marks = [seg_of(k_at + n, ends) for n in (0, half - 1, half, k_rows - 1)]
        low = (marks[0] <= q_hi) & (q_lo <= marks[1])
        high = (marks[2] <= q_hi) & (q_lo <= marks[3])
        same = (marks[0] == marks[3]) & (q_lo == q_hi)

        def run(first, count):
            if not masked:
                return body(j * k_rows + first, count, None)
            k_seg = seg_of(k_at + first + lax.broadcasted_iota(jnp.int32, (count, 1), 0), ends)
            return body(j * k_rows + first, count, k_seg == q_seg)

        if masked:
            pl.when(low & high & same)(lambda: body(j * k_rows, k_rows, None))
        pl.when(low & high & jnp.logical_not(same) if masked else low & high)(lambda: run(0, k_rows))
        pl.when(low & jnp.logical_not(high))(lambda: run(0, half))
        pl.when(high & jnp.logical_not(low))(lambda: run(half, half))
        return carry

    lax.fori_loop(0, k_blocks, step, 0)


def attend_kernel(docs, k_rows, meta, q_ref, k_ref, v_ref, o_0, o_1, o_2, o_3, lse_ref, vt_ref, s_ref, m_ref, l_ref, acc_ref):
    q_rows, wide = q_ref.shape[1], q_ref.shape[2]
    group = wide // HEAD_DIM
    k_blocks = k_ref.shape[1] // k_rows
    q_blocks = pl.num_programs(1)
    i = pl.program_id(1)

    @pl.when(i == 0)
    def _():
        for j in range(k_blocks):
            at = pl.ds(j * k_rows, k_rows)
            vt_ref[:, at] = v_ref[0, at, :].T

    q_st = stack_heads(q_ref[0] * SCORE_SCALE, group)
    m_ref[...] = jnp.full(m_ref.shape, MASKED_SCORE, jnp.float32)
    l_ref[...] = jnp.zeros_like(l_ref)
    acc_ref[...] = jnp.zeros_like(acc_ref)
    place = (docs, meta[docs - 1 + i], q_rows, docs - 1 + q_blocks, k_rows, k_blocks, group)

    def find_top(first, count, mask):
        at = pl.ds(pl.multiple_of(first, k_rows // 2), count)
        scores = dot(k_ref[0, at, :], q_st, NT)
        if mask is not None:
            scores = jnp.where(mask, scores, MASKED_SCORE)
        s_ref[at, :] = scores
        m_ref[...] = jnp.maximum(m_ref[...], jnp.max(scores, 0, keepdims=True))

    each_key_block(meta, *place, find_top)
    row_top = m_ref[...]

    def add_up(first, count, mask):
        at = pl.ds(pl.multiple_of(first, k_rows // 2), count)
        weights = jnp.exp(s_ref[at, :] - row_top)
        l_ref[...] += jnp.sum(weights, 0, keepdims=True)
        low = weights.astype(jnp.bfloat16)
        for h in range(group):
            rows = pl.ds(h * HEAD_DIM, HEAD_DIM)
            cols = slice(h * q_rows, (h + 1) * q_rows)
            acc_ref[rows, :] += dot(vt_ref[rows, at], low[:, cols], NN)

    each_key_block(meta, *place, add_up, False)
    total = l_ref[...]
    outs = []
    for h in range(group):
        cols = slice(h * q_rows, (h + 1) * q_rows)
        outs.append(acc_ref[h * HEAD_DIM : (h + 1) * HEAD_DIM, :] / total[:, cols])
    result = jnp.concatenate(outs, 0).T.astype(jnp.bfloat16)
    goal = (i % 2) * 2 + ((i // 2) ^ meta[docs - 1 + q_blocks + k_blocks])
    for n, part in enumerate((o_0, o_1, o_2, o_3)):
        @pl.when(goal == n)
        def _(part=part):
            part[...] = result

    lse_ref[0, 0] = row_top + jnp.log(total)


def attend_back_kernel(
    docs, k_rows, meta, q_ref, k_ref, v_ref, o_0, o_1, o_2, o_3, do_0, do_1, do_2, do_3, lse_ref, dq_ref, dk_ref, dv_ref,
    kt_ref, dqt_ref, dk_acc, dv_acc, do_ref, o_ref,
):
    q_rows, wide = q_ref.shape[1], q_ref.shape[2]
    group = wide // HEAD_DIM
    k_blocks = k_ref.shape[1] // k_rows
    q_blocks = pl.num_programs(1)
    i = pl.program_id(1)

    @pl.when(i == 0)
    def _():
        dk_acc[...] = jnp.zeros_like(dk_acc)
        dv_acc[...] = jnp.zeros_like(dv_acc)
        for j in range(k_blocks):
            at = pl.ds(j * k_rows, k_rows)
            kt_ref[:, at] = k_ref[0, at, :].T

    q_st = stack_heads(q_ref[0] * SCORE_SCALE, group)
    source = (i % 2) * 2 + ((i // 2) ^ meta[docs - 1 + q_blocks + k_blocks])
    for n, (part, out) in enumerate(((do_0, o_0), (do_1, o_1), (do_2, o_2), (do_3, o_3))):
        @pl.when(source == n)
        def _(part=part, out=out):
            do_ref[...] = part[...]
            o_ref[...] = out[...]

    grad_out = do_ref[...]
    do_st = stack_heads(grad_out, group)
    product = (grad_out.astype(jnp.float32) * o_ref[...].astype(jnp.float32)).T
    delta = jnp.concatenate(
        [jnp.sum(product[h * HEAD_DIM : (h + 1) * HEAD_DIM], 0, keepdims=True) for h in range(group)], 1
    )
    log_total = lse_ref[0, 0]
    dqt_ref[...] = jnp.zeros_like(dqt_ref)

    def body(first, count, mask):
        at = pl.ds(pl.multiple_of(first, k_rows // 2), count)
        scores = dot(k_ref[0, at, :], q_st, NT)
        if mask is not None:
            scores = jnp.where(mask, scores, MASKED_SCORE)
        probs = jnp.exp(scores - log_total)
        dv_acc[at, :] += dot(probs.astype(jnp.bfloat16), do_st, NN)
        grad_probs = dot(v_ref[0, at, :], do_st, NT)
        grad_scores = (probs * (grad_probs - delta)).astype(jnp.bfloat16)
        dk_acc[at, :] += dot(grad_scores, q_st, NN)
        for h in range(group):
            rows = pl.ds(h * HEAD_DIM, HEAD_DIM)
            cols = slice(h * q_rows, (h + 1) * q_rows)
            dqt_ref[rows, :] += dot(kt_ref[rows, at], grad_scores[:, cols], NN)

    each_key_block(meta, docs, meta[docs - 1 + i], q_rows, docs - 1 + q_blocks, k_rows, k_blocks, group, body)
    dq_ref[0] = (dqt_ref[...].T * SCORE_SCALE).astype(jnp.bfloat16)

    @pl.when(i == q_blocks - 1)
    def _():
        dk_ref[0] = dk_acc[...].astype(jnp.bfloat16)
        dv_ref[0] = dv_acc[...].astype(jnp.bfloat16)


def attend_call(meta, query, key, value, docs, q_rows, k_rows):
    items, length, wide = query.shape
    keys = key.shape[1]
    group = wide // HEAD_DIM
    q_blocks = length // q_rows
    block = pl.BlockSpec((1, q_rows, wide), lambda g, i, m: (g, i, 0))
    whole = pl.BlockSpec((1, keys, wide), lambda g, i, m: (g, 0, 0))
    stat = pl.BlockSpec((1, 1, 1, group * q_rows), lambda g, i, m: (g, i, 0, 0))
    return pl.pallas_call(
        functools.partial(attend_kernel, docs, k_rows),
        grid_spec=pltpu.PrefetchScalarGridSpec(
            num_scalar_prefetch=1,
            grid=(items, q_blocks),
            in_specs=[block, whole, whole],
            out_specs=[full((q_rows, wide))] * 4 + [stat],
            scratch_shapes=[
                pltpu.VMEM((wide, keys), jnp.bfloat16),
                pltpu.VMEM((keys, group * q_rows), jnp.float32),
                pltpu.VMEM((1, group * q_rows), jnp.float32),
                pltpu.VMEM((1, group * q_rows), jnp.float32),
                pltpu.VMEM((wide, q_rows), jnp.float32),
            ],
        ),
        out_shape=[jax.ShapeDtypeStruct((q_rows, wide), jnp.bfloat16)] * 4
        + [jax.ShapeDtypeStruct((items, q_blocks, 1, group * q_rows), jnp.float32)],
        compiler_params=pltpu.CompilerParams(vmem_limit_bytes=VMEM_LIMIT),
        name="attend",
    )(meta, query, key, value)


def attend_back_call(meta, query, key, value, out, grad_parts, log_total, docs, q_rows, k_rows):
    items, length, wide = query.shape
    keys = key.shape[1]
    group = wide // HEAD_DIM
    q_blocks = length // q_rows
    block = pl.BlockSpec((1, q_rows, wide), lambda g, i, m: (g, i, 0))
    whole = pl.BlockSpec((1, keys, wide), lambda g, i, m: (g, 0, 0))
    stat = pl.BlockSpec((1, 1, 1, group * q_rows), lambda g, i, m: (g, i, 0, 0))
    return pl.pallas_call(
        functools.partial(attend_back_kernel, docs, k_rows),
        grid_spec=pltpu.PrefetchScalarGridSpec(
            num_scalar_prefetch=1,
            grid=(items, q_blocks),
            in_specs=[block, whole, whole] + [full((q_rows, wide))] * 8 + [stat],
            out_specs=[block, whole, whole],
            scratch_shapes=[
                pltpu.VMEM((wide, keys), jnp.bfloat16),
                pltpu.VMEM((wide, q_rows), jnp.float32),
                pltpu.VMEM((keys, wide), jnp.float32),
                pltpu.VMEM((keys, wide), jnp.float32),
                pltpu.VMEM((q_rows, wide), jnp.bfloat16),
                pltpu.VMEM((q_rows, wide), jnp.bfloat16),
            ],
        ),
        out_shape=[
            jax.ShapeDtypeStruct(query.shape, jnp.bfloat16),
            jax.ShapeDtypeStruct(key.shape, jnp.bfloat16),
            jax.ShapeDtypeStruct(key.shape, jnp.bfloat16),
        ],
        compiler_params=pltpu.CompilerParams(vmem_limit_bytes=VMEM_LIMIT),
        name="attend_back",
    )(meta, query, key, value, *out, *grad_parts, log_total)


def layer_norm(values, gain):
    mean_value = jnp.mean(values, -1, keepdims=True)
    centred = values - mean_value
    spread = jnp.mean(centred * centred, -1, keepdims=True)
    return centred * lax.rsqrt(spread + EPSILON) * gain


def norm_parts(values):
    centred = values - jnp.mean(values, -1, keepdims=True)
    inverse = lax.rsqrt(jnp.mean(centred * centred, -1, keepdims=True) + EPSILON)
    return centred * inverse, inverse


def turn_matrix(width):
    row = lax.broadcasted_iota(jnp.int32, (width, width), 0)
    col = lax.broadcasted_iota(jnp.int32, (width, width), 1)
    half = HEAD_DIM // 2
    first = (col % HEAD_DIM) < half
    plus = jnp.logical_not(first) & (row == col - half)
    minus = first & (row == col + half)
    return plus.astype(jnp.bfloat16) - minus.astype(jnp.bfloat16)


def angles(positions, width):
    half = HEAD_DIM // 2
    steps_index = (jnp.arange(width) % half).astype(jnp.float32)
    inverse = ROPE_THETA ** (-2.0 * steps_index / HEAD_DIM)
    return positions.astype(jnp.float32)[:, None] * inverse[None, :]


def turned_tables(cos_row, sin_row, base):
    cos_base, sin_base = base[0:1, :], base[1:2, :]
    return cos_row * cos_base - sin_row * sin_base, sin_row * cos_base + cos_row * sin_base


def full(shape):
    return pl.BlockSpec(shape, lambda *_: (0,) * len(shape))


def padded(wide):
    return -(-wide // 128) * 128


def project_kernel(meta, *refs):
    chunk_refs = refs[:8]
    w_ref, turn_ref, cos_ref, sin_ref, base_ref, normed_ref, q_ref, k_ref, v_ref, x_ref, w_all, gain_row = refs[8:]
    wide = q_ref.shape[2]
    slot = padded(wide)
    i = pl.program_id(0)
    bf16 = jnp.bfloat16

    @pl.when(i == 0)
    def _():
        for p, at in ((1, 0), (2, 2), (0, 3)):
            w_all[:, at * slot : at * slot + wide] = w_ref[:, p * wide : (p + 1) * wide]
        for p, at in ((1, 1), (0, 4)):
            turned = dot(w_ref[:, p * wide : (p + 1) * wide], turn_ref[...], NN)
            w_all[:, at * slot : at * slot + wide] = turned.astype(bf16)
        last = w_ref[:, w_ref.shape[1] - 128 :].astype(jnp.float32).T
        gain_row[...] = last[127:128, :]

    for n in range(8):
        @pl.when(i == n)
        def _(n=n):
            x_ref[...] = chunk_refs[n][...]

    normed, _ = norm_parts(x_ref[...].astype(jnp.float32))
    normed = (normed * gain_row[...]).astype(bf16)
    normed_ref[0] = normed.T
    cos, sin = turned_tables(cos_ref[...], sin_ref[...], base_ref[0])
    raw = dot(normed, w_all[:, : 3 * slot], NN)
    k_ref[0] = (raw[:, :wide] * cos + raw[:, slot : slot + wide] * sin).astype(bf16)
    v_ref[0] = raw[:, 2 * slot : 2 * slot + wide].astype(bf16)

    @pl.when(i % 2 == meta[0])
    def _():
        raw_q = dot(normed, w_all[:, 3 * slot : 5 * slot], NN)
        q_ref[0] = (raw_q[:, :wide] * cos + raw_q[:, slot : slot + wide] * sin).astype(bf16)


def project_call(meta, chunks, w, turn, cos_row, sin_row, bases, wide):
    block, width = chunks[0].shape
    bf16 = jnp.bfloat16
    one = lambda i, m: (i, 0, 0)
    return pl.pallas_call(
        project_kernel,
        grid_spec=pltpu.PrefetchScalarGridSpec(
            num_scalar_prefetch=1,
            grid=(8,),
            in_specs=[full((block, width))] * 8
            + [full(w.shape), full(turn.shape), full(cos_row.shape), full(sin_row.shape), pl.BlockSpec((1, 2, wide), one)],
            out_specs=[
                pl.BlockSpec((1, width, block), one),
                pl.BlockSpec((1, block, wide), lambda i, m: (i // 2, 0, 0)),
                pl.BlockSpec((1, block, wide), one),
                pl.BlockSpec((1, block, wide), one),
            ],
            scratch_shapes=[
                pltpu.VMEM((block, width), bf16),
                pltpu.VMEM((width, 5 * padded(wide)), bf16),
                pltpu.VMEM((1, width), jnp.float32),
            ],
        ),
        out_shape=[
            jax.ShapeDtypeStruct((8, width, block), bf16),
            jax.ShapeDtypeStruct((4, block, wide), bf16),
            jax.ShapeDtypeStruct((8, block, wide), bf16),
            jax.ShapeDtypeStruct((8, block, wide), bf16),
        ],
        compiler_params=pltpu.CompilerParams(vmem_limit_bytes=VMEM_LIMIT),
        name="project",
    )(meta, *chunks, w, turn, cos_row, sin_row, bases)


def feed_kernel(ff, meta, *refs):
    parts, slices = refs[0:4], refs[4:8]
    tok_ref, cot_ref = refs[8:10]
    out_ref, gh_ref, normed_ref, att_ref, cot_t_ref, gated_ref, ga_ref, gb_ref, gbr_ref, dgain_ref = refs[10:20]
    grad_parts = refs[20:24]
    w_a, w_b, w_dt, w_o, gain_row, att_scr = refs[24:30]
    wide = parts[0].shape[1]
    i = pl.program_id(0)
    bf16 = jnp.bfloat16

    @pl.when(i == 0)
    def _():
        for n in range(4):
            at = slice(n * ff, (n + 1) * ff)
            w_a[:, at] = slices[n][:, :ff]
            w_b[:, at] = slices[n][:, ff : 2 * ff]
            w_dt[:, at] = slices[n][:, 2 * ff : 3 * ff]
            for g in range(4):
                @pl.when(meta[n] == g)
                def _(n=n, g=g):
                    w_o[:, g * wide : (g + 1) * wide] = slices[n][:, 3 * ff : 3 * ff + wide]
        last = slices[0][:, slices[0].shape[1] - 128 :].astype(jnp.float32).T
        gain_row[...] = last[127:128, :]
        dgain_ref[...] = jnp.zeros_like(dgain_ref)

    for g in range(4):
        for n in range(4):
            @pl.when(meta[4 + n] == g)
            def _(n=n, g=g):
                att_scr[:, g * wide : (g + 1) * wide] = parts[n][...]

    attended = att_scr[...]
    att_ref[...] = attended.T
    gain = gain_row[...]
    hidden = tok_ref[...].astype(jnp.float32) + dot(attended, w_o[...], NN)
    normal, inverse = norm_parts(hidden)
    normed = (normal * gain).astype(bf16)
    normed_ref[...] = normed.T
    half_a = dot(normed, w_a[...], NN)
    half_b = dot(normed, w_b[...], NN)
    phi = 0.5 * (1.0 + lax.erf(half_a * ROOT_HALF))
    gelu = half_a * phi
    slope = phi + half_a * (jnp.exp(-0.5 * half_a * half_a) * INVERSE_ROOT_TAU)
    gated = (gelu * half_b).astype(bf16)
    out_ref[...] = (hidden + dot(gated, w_dt[...], NT)).astype(bf16)
    cot = cot_ref[...]
    cot_t_ref[...] = cot.T
    grad_gated = dot(cot, w_dt[...], NN)
    grad_a = (grad_gated * half_b * slope).astype(bf16)
    grad_b = (grad_gated * gelu).astype(bf16)
    for n in range(4):
        at = slice(n * ff, (n + 1) * ff)
        gated_ref[n] = gated[:, at]
        ga_ref[n] = grad_a[:, at]
        gb_ref[n] = grad_b[:, at]
    grad_normed = dot(grad_a, w_a[...], NT) + dot(grad_b, w_b[...], NT)
    dgain_ref[...] += jnp.sum(grad_normed * normal, 0, keepdims=True)
    scaled = grad_normed * gain
    inner = jnp.mean(scaled * normal, -1, keepdims=True)
    grad_hidden = cot.astype(jnp.float32) + inverse * (
        scaled - jnp.mean(scaled, -1, keepdims=True) - normal * inner
    )
    gh_ref[...] = grad_hidden
    grad_branch = grad_hidden.astype(bf16)
    for g in range(4):
        gbr_ref[g] = grad_branch[:, g * wide : (g + 1) * wide]
    grad_mixed = dot(grad_branch, w_o[...], NT).astype(bf16)
    for g in range(4):
        for n in range(4):
            @pl.when(meta[4 + n] == g)
            def _(n=n, g=g):
                grad_parts[n][...] = grad_mixed[:, g * wide : (g + 1) * wide]


def feed_call(meta, parts, slices, tokens, cotangent, ff):
    block, width = tokens.shape
    wide = parts[0].shape[1]
    bf16, f32 = jnp.bfloat16, jnp.float32
    rows = min(256, block)
    part = pl.BlockSpec((rows, wide), lambda i, m: (i, 0))
    row = pl.BlockSpec((rows, width), lambda i, m: (i, 0))
    hid = pl.BlockSpec((4, rows, ff), lambda i, m: (0, i, 0))
    flat = pl.BlockSpec((width, rows), lambda i, m: (0, i))
    grp = pl.BlockSpec((4, rows, wide), lambda i, m: (0, i, 0))
    sds = jax.ShapeDtypeStruct
    return pl.pallas_call(
        functools.partial(feed_kernel, ff),
        grid_spec=pltpu.PrefetchScalarGridSpec(
            num_scalar_prefetch=1,
            grid=(block // rows,),
            in_specs=[part] * 4 + [full(slices[0].shape)] * 4 + [row, row],
            out_specs=[row, row, flat, flat, flat, hid, hid, hid, grp, full((1, width))] + [part] * 4,
            scratch_shapes=[pltpu.VMEM((width, 4 * ff), bf16)] * 3
            + [pltpu.VMEM((width, width), bf16), pltpu.VMEM((1, width), f32), pltpu.VMEM((rows, width), bf16)],
        ),
        out_shape=[
            sds((block, width), bf16),
            sds((block, width), f32),
            sds((width, block), bf16),
            sds((width, block), bf16),
            sds((width, block), bf16),
            sds((4, block, ff), bf16),
            sds((4, block, ff), bf16),
            sds((4, block, ff), bf16),
            sds((4, block, wide), bf16),
            sds((1, width), f32),
        ]
        + [sds((block, wide), bf16)] * 4,
        compiler_params=pltpu.CompilerParams(vmem_limit_bytes=VMEM_LIMIT),
        name="feed",
    )(meta, *parts, *slices, tokens, cotangent)


def pack_kernel(meta, nm_t, cot_t, att_t, ga_ref, gb_ref, gated_ref, gbr_ref, dgain_ref, out_ref):
    ff, wide = ga_ref.shape[2], gbr_ref.shape[2]
    bf16 = jnp.bfloat16

    width = nm_t.shape[0]
    gain = jnp.broadcast_to(dgain_ref[...], (128, width)).T
    last = out_ref.shape[2] - (3 * ff + wide)
    out_ref[0] = jnp.concatenate(
        [
            dot(nm_t[...], ga_ref[0], NN),
            dot(nm_t[...], gb_ref[0], NN),
            dot(cot_t[...], gated_ref[0], NN),
            dot(att_t[...], gbr_ref[0], NN),
            gain[:, :last],
        ],
        1,
    ).astype(bf16)


def pack_call(meta, normed, cotangent, attended, grad_a, grad_b, gated, grad_branch, d_gain, first):
    width, block = normed.shape
    ff, wide = grad_a.shape[2], grad_branch.shape[2]
    bf16 = jnp.bfloat16
    packed = padded(3 * ff + wide + 1)
    hid = pl.BlockSpec((1, block, ff), lambda i, m: (first + i, 0, 0))
    return pl.pallas_call(
        pack_kernel,
        grid_spec=pltpu.PrefetchScalarGridSpec(
            num_scalar_prefetch=1,
            grid=(2,),
            in_specs=[full((width, block))] * 3
            + [hid] * 3
            + [pl.BlockSpec((1, block, wide), lambda i, m: (m[first + i], 0, 0)), full((1, width))],
            out_specs=pl.BlockSpec((1, width, packed), lambda i, m: (i, 0, 0)),
        ),
        out_shape=jax.ShapeDtypeStruct((2, width, packed), bf16),
        compiler_params=pltpu.CompilerParams(vmem_limit_bytes=VMEM_LIMIT),
        name="pack",
    )(meta, normed, cotangent, attended, grad_a, grad_b, gated, grad_branch, d_gain)


def unturn_kernel(meta, normed_ref, dq_ref, dk_ref, dv_ref, turn_ref, cos_ref, sin_ref, base_ref, raw_ref, dw_ref, acc_ref):
    wide = dk_ref.shape[2]
    i = pl.program_id(0)

    @pl.when(i == 0)
    def _():
        acc_ref[...] = jnp.zeros_like(acc_ref)

    cos, sin = turned_tables(cos_ref[...], sin_ref[...], base_ref[0])

    def turn_back(grad):
        return (grad.astype(jnp.float32) * cos + dot(grad, turn_ref[...], NT) * sin).astype(jnp.bfloat16)

    mine = meta[0] == i % 2
    raw_ref[0, :, wide : 2 * wide] = turn_back(dk_ref[0])
    raw_ref[0, :, 2 * wide : 3 * wide] = dv_ref[0]

    @pl.when(mine)
    def _():
        raw_ref[0, :, :wide] = turn_back(dq_ref[0])

    @pl.when(jnp.logical_not(mine))
    def _():
        raw_ref[0, :, :wide] = jnp.zeros_like(dk_ref[0])

    acc_ref[...] += dot(normed_ref[0], raw_ref[0], NN)

    @pl.when(i == pl.num_programs(0) - 1)
    def _():
        dw_ref[...] = acc_ref[...].astype(jnp.bfloat16)


def unturn_call(meta, normed_t, dq, dk, dv, turn, cos_row, sin_row, bases):
    _, width, block = normed_t.shape
    wide = dk.shape[2]
    one = lambda i, m: (i, 0, 0)
    return pl.pallas_call(
        unturn_kernel,
        grid_spec=pltpu.PrefetchScalarGridSpec(
            num_scalar_prefetch=1,
            grid=(8,),
            in_specs=[
                pl.BlockSpec((1, width, block), one),
                pl.BlockSpec((1, block, wide), lambda i, m: (i // 2, 0, 0)),
                pl.BlockSpec((1, block, wide), one),
                pl.BlockSpec((1, block, wide), one),
                full(turn.shape),
                full(cos_row.shape),
                full(sin_row.shape),
                pl.BlockSpec((1, 2, wide), one),
            ],
            out_specs=[pl.BlockSpec((1, block, 3 * wide), one), full((width, 3 * wide))],
            scratch_shapes=[pltpu.VMEM((width, 3 * wide), jnp.float32)],
        ),
        out_shape=[
            jax.ShapeDtypeStruct((8, block, 3 * wide), jnp.bfloat16),
            jax.ShapeDtypeStruct((width, 3 * wide), jnp.bfloat16),
        ],
        compiler_params=pltpu.CompilerParams(vmem_limit_bytes=VMEM_LIMIT),
        name="unturn",
    )(meta, normed_t, dq, dk, dv, turn, cos_row, sin_row, bases)


def unproject_kernel(raw_ref, w_ref, partial_ref):
    partial_ref[0] = dot(raw_ref[0], w_ref[:, : raw_ref.shape[2]], NT).astype(jnp.bfloat16)


def unproject_call(core, grad_raw, w):
    _, block, columns = grad_raw.shape
    width = w.shape[0]
    return pl.pallas_call(
        unproject_kernel,
        grid=(4,),
        in_specs=[pl.BlockSpec((1, block, columns), lambda i: (2 * i + core, 0, 0)), full(w.shape)],
        out_specs=pl.BlockSpec((1, block, width), lambda i: (i, 0, 0)),
        out_shape=jax.ShapeDtypeStruct((4, block, width), jnp.bfloat16),
        compiler_params=pltpu.CompilerParams(vmem_limit_bytes=VMEM_LIMIT),
        name="unproject",
    )(grad_raw, w)


PLANE = ("ctx", "tensor")


def plane_permute(array, target):
    pairs = []
    for c in range(2):
        for x in range(2):
            for h in range(2):
                to_c, to_x, to_h = target(c, x, h)
                pairs.append((c * 4 + x * 2 + h, to_c * 4 + to_x * 2 + to_h))
    return lax.ppermute(array, PLANE, pairs)


def tensor_permute(array, flip):
    return lax.ppermute(array, "tensor", [(t, t ^ flip) for t in range(4)])


def pick(array, index, axis):
    return lax.dynamic_index_in_dim(array, index, axis, keepdims=False)


def local(tokens, doc_lengths, attn_gain, mlp_gain, w_qkv, w_attn_out, w_in, w_down, cotangent):
    _, block, width = tokens.shape
    assert lax.axis_size("ctx") == 2 and lax.axis_size("tensor") == 4 and tokens.shape[0] == 1
    rows = w_qkv.shape[0]
    ff = w_in.shape[2]
    docs = doc_lengths.shape[1]
    c = lax.axis_index("ctx")
    t = lax.axis_index("tensor")
    x, h = t // 2, t % 2
    wide = width // 4
    bf16 = jnp.bfloat16

    own = tokens[0]
    over_y = lambda c, x, h: (1 - c, x, h)
    shards = lax.axis_size("shard")
    shard_at = lax.axis_index("shard")

    def shard_gather(part):
        whole = jnp.zeros((shards,) + part.shape, part.dtype)
        pieces = [part]
        for k in range(1, shards):
            pieces.append(lax.ppermute(part, "shard", [(z, (z + k) % shards) for z in range(shards)]))
        for k, piece in enumerate(pieces):
            whole = lax.dynamic_update_index_in_dim(whole, piece, lax.rem(shard_at + shards - k, shards), 0)
        return whole

    def both_ctx(mine, other, axis):
        return jnp.where(c == 0, jnp.stack([mine, other], axis), jnp.stack([other, mine], axis))

    group_cols = pick(w_qkv.reshape(rows, 3, 4, wide), t, 2).reshape(rows, 3 * wide)
    gain_cols = padded(3 * wide + 1) - 3 * wide
    pack_1 = jnp.concatenate([group_cols, jnp.broadcast_to(attn_gain[:, None], (rows, gain_cols))], 1)
    own_cols = pick(w_attn_out.reshape(rows, 4, wide), t, 1)
    gain_cols = padded(3 * ff + wide + 1) - 3 * ff - wide
    pack_2 = jnp.concatenate(
        [w_in.reshape(rows, 2 * ff), w_down.T, own_cols, jnp.broadcast_to(mlp_gain[:, None], (rows, gain_cols))], 1
    )
    slice_flips = (0, 2, 1, 3)

    by_x = tensor_permute(own, 2)
    by_y = plane_permute(own, over_y)
    by_xy = plane_permute(own, lambda c, x, h: (1 - c, 1 - x, h))
    row_angles = angles(jnp.arange(block), wide)
    cos_row, sin_row = jnp.cos(row_angles), jnp.sin(row_angles)
    pack_1 = shard_gather(pack_1)
    pack_1, pack_2, cos_row, sin_row = lax.optimization_barrier((pack_1, pack_2, cos_row, sin_row))
    pack_1_y, pack_2 = lax.optimization_barrier((plane_permute(pack_1, over_y), shard_gather(pack_2)))
    pack_1 = both_ctx(pack_1, pack_1_y, 1).reshape(width, -1)
    pack_2_y = plane_permute(pack_2, over_y)
    chunks = [chunk for part in (own, by_x, by_y, by_xy) for chunk in (part, tensor_permute(part, 1))]

    chunk_at = []
    for dc in range(2):
        for dx in range(2):
            for dh in range(2):
                chunk_at.append(((c ^ dc) * 4 + (x ^ dx) * 2 + (h ^ dh)) * block)
    base_angles = angles(jnp.stack(chunk_at), wide)
    bases = jnp.stack([jnp.cos(base_angles), jnp.sin(base_angles)], 1)
    q_rows = block
    k_rows = min(512, block)
    pick_core = h ^ c
    key_starts = [at + k * k_rows for at in chunk_at for k in range(block // k_rows)]
    query_starts = [
        ((c ^ dc) * 4 + (x ^ dx) * 2 + c) * block
        for dc in range(2)
        for dx in range(2)
    ]
    doc_ends = jnp.cumsum(doc_lengths[0])[: docs - 1].astype(jnp.int32)
    meta = jnp.concatenate([doc_ends, jnp.stack(query_starts + key_starts + [pick_core]).astype(jnp.int32)])
    core_meta = jnp.stack([pick_core]).astype(jnp.int32)
    steps = [(a, b) for b in range(2) for a in range(2)]
    feed_meta = jnp.stack(
        [t ^ flip for flip in slice_flips] + [(x ^ b) * 2 + (c ^ a) for a, b in steps]
    ).astype(jnp.int32)

    turn = turn_matrix(wide)
    normed_t, query, key, value = project_call(core_meta, chunks, pack_1, turn, cos_row, sin_row, bases, wide)
    query, pack_2_y = lax.optimization_barrier((query, pack_2_y))
    pack_2 = both_ctx(pack_2, pack_2_y, 1).reshape(width, -1)
    query, pack_2 = lax.optimization_barrier((query, pack_2))
    slices = [pack_2, tensor_permute(pack_2, 2), tensor_permute(pack_2, 1)]
    query = query.reshape(1, 4 * block, wide)
    key = key.reshape(1, 8 * block, wide)
    value = value.reshape(1, 8 * block, wide)
    *out, log_total = attend_call(meta, query, key, value, docs, q_rows, k_rows)

    def forth(a, b):
        return lambda c, x, h: (h ^ a, x ^ b, c)

    def back(a, b):
        return lambda c, x, h: (h, x ^ b, c ^ a)

    arrived = [plane_permute(part, forth(a, b)) for part, (a, b) in zip(out, steps)]
    arrived[0], slices[1] = lax.optimization_barrier((arrived[0], slices[1]))
    slices.append(tensor_permute(slices[1], 1))

    (layer_out, grad_hidden, normed_m, attended, cot_t, gated, grad_a, grad_b, grad_branch, d_gain_mlp, *grad_parts) = feed_call(
        feed_meta, arrived, slices, own, cotangent[0], ff
    )
    grad_parts = [plane_permute(part, back(a, b)) for part, (a, b) in zip(grad_parts, steps)]

    def add(one, two):
        return (one.astype(jnp.float32) + two.astype(jnp.float32)).astype(bf16)

    grads = (normed_m, cot_t, attended, grad_a, grad_b, gated, grad_branch, d_gain_mlp)
    sent_packs, grad_parts = lax.optimization_barrier((pack_call(feed_meta, *grads, 2), grad_parts))
    sent_packs = tensor_permute(sent_packs, 1)
    packs = add(pack_call(feed_meta, *grads, 0), sent_packs)
    packed = packs.shape[2]
    cut = padded(packed // 2)
    packs = packs.reshape(2, -1, 2, rows, packed)
    one_x = tensor_permute(packs[1, ..., :cut], 2)
    one_y = plane_permute(pick(packs[..., cut:], 1 - c, 2), over_y)
    kept_x, kept_y = packs[0, ..., :cut], pick(packs[..., cut:], c, 2)
    grad_parts, kept_x, kept_y = lax.optimization_barrier((grad_parts, kept_x, kept_y))

    grad_query, grad_key, grad_value = attend_back_call(
        meta, query, key, value, out, grad_parts, log_total, docs, q_rows, k_rows
    )
    kept_x, kept_y = add(kept_x, one_x), add(kept_y, one_y)
    grad_key, kept_x, kept_y = lax.optimization_barrier((grad_key, kept_x, kept_y))
    two_y = plane_permute(pick(kept_x, 1 - c, 1), over_y)
    two_x = tensor_permute(kept_y[1], 2)
    grad_query = grad_query.reshape(4, block, wide)
    grad_key = grad_key.reshape(8, block, wide)
    grad_value = grad_value.reshape(8, block, wide)
    grad_raw, d_qkv = unturn_call(
        core_meta, normed_t, grad_query, grad_key, grad_value, turn, cos_row, sin_row, bases
    )
    grad_raw, d_qkv, two_x, two_y = lax.optimization_barrier((grad_raw, d_qkv, two_x, two_y))
    pack = jnp.concatenate([add(pick(kept_x, c, 1), two_y), add(kept_y[0], two_x)], 2)
    d_qkv = d_qkv.reshape(-1, 2, rows, 3 * wide)
    d_qkv_y = plane_permute(pick(d_qkv, 1 - c, 1), over_y)
    d_qkv_own = pick(d_qkv, c, 1)
    from_core = tensor_permute(unproject_call(1, grad_raw, pack_1), 1)
    partial = unproject_call(0, grad_raw, pack_1)

    chip_sum = [add(partial[n], from_core[n]) for n in range(4)]
    sent = [
        tensor_permute(chip_sum[1], 2),
        plane_permute(chip_sum[2], over_y),
        plane_permute(chip_sum[3], lambda c, x, h: (1 - c, 1 - x, h)),
    ]
    pack, d_qkv_y, chip_sum = lax.optimization_barrier((pack, d_qkv_y, chip_sum))
    d_qkv_y, sent[0] = lax.optimization_barrier((d_qkv_y, sent[0]))

    def shard_sum(parts):
        total = pick(parts, shard_at, 0).astype(jnp.float32)
        for k in range(1, shards):
            part = pick(parts, lax.rem(shard_at + k, shards), 0)
            total = total + lax.ppermute(part, "shard", [(z, (z + k) % shards) for z in range(shards)]).astype(jnp.float32)
        return total

    pack = shard_sum(pack)
    d_in = pack[:, : 2 * ff].reshape(rows, 2, ff)
    d_down = pack[:, 2 * ff : 3 * ff].T
    d_group_out = pack[:, 3 * ff : 3 * ff + wide].astype(bf16)
    d_gain_mlp = pick(pack[:, 3 * ff + wide].reshape(4, rows // 4), t, 0)
    d_qkv = shard_sum(add(d_qkv_own, d_qkv_y)).astype(bf16)
    d_qkv, sent = lax.optimization_barrier((d_qkv, sent))
    d_both = jnp.concatenate([d_qkv, d_group_out], 1).reshape(4, rows // 4, 4 * wide)
    d_both = lax.all_to_all(d_both, "tensor", split_axis=0, concat_axis=0, tiled=True)
    d_both = d_both.reshape(4, rows // 4, 4, wide).transpose(1, 2, 0, 3).reshape(rows // 4, 4 * width)
    d_both = d_both.astype(jnp.float32)
    d_qkv, d_attn_out = d_both[:, : 3 * width], d_both[:, 3 * width :]
    own_rows = pick(w_qkv.reshape(4, rows // 4, 3 * width), t, 0).astype(jnp.float32)
    own_gain = pick(attn_gain.reshape(4, rows // 4), t, 0).astype(jnp.float32)
    d_gain_attn = jnp.sum(d_qkv * own_rows, 1) / own_gain

    grad_normed = chip_sum[0].astype(jnp.float32)
    for part in sent:
        grad_normed = grad_normed + part.astype(jnp.float32)
    gain_attn = pack_1[:, 3 * wide].astype(jnp.float32)
    _, norm_pull_attn = jax.vjp(lambda values: layer_norm(values, gain_attn), own.astype(jnp.float32))
    grad_tokens = grad_hidden + norm_pull_attn(grad_normed)[0]
    return (layer_out[None], grad_tokens[None], d_gain_attn, d_gain_mlp, d_qkv, d_attn_out, d_in, d_down)


def solution(mesh):
    return jax.shard_map(
        local,
        mesh=mesh,
        in_specs=(
            P("shard", ("ctx", "tensor"), None),
            P("shard", None),
            P(("shard", "ctx")),
            P(("shard", "ctx")),
            P(("shard", "ctx"), None),
            P(("shard", "ctx"), None),
            P(("shard", "ctx"), None, "tensor"),
            P("tensor", ("shard", "ctx")),
            P("shard", ("ctx", "tensor"), None),
        ),
        out_specs=(
            P("shard", ("ctx", "tensor"), None),
            P("shard", ("ctx", "tensor"), None),
            P(("shard", "ctx", "tensor")),
            P(("shard", "ctx", "tensor")),
            P(("shard", "ctx", "tensor"), None),
            P(("shard", "ctx", "tensor"), None),
            P(("shard", "ctx"), None, "tensor"),
            P("tensor", ("shard", "ctx")),
        ),
        check_vma=False,
    )
```

```python
import functools

import jax
import jax.numpy as jnp
from jax import lax
from jax.experimental import pallas as pl
from jax.experimental.pallas import tpu as pltpu
from jax.sharding import PartitionSpec as P

HEAD_DIM = 64
EPSILON = 1e-05
ROPE_THETA = 160000.0
SCORE_SCALE = 0.125
MASKED_SCORE = -1e30
ROOT_HALF = 0.7071067811865476
INVERSE_ROOT_TAU = 0.3989422804014327
VMEM_LIMIT = 56 * 1024 * 1024

NT = (((1,), (1,)), ((), ()))
NN = (((1,), (0,)), ((), ()))


def dot(a, b, dims):
    return lax.dot_general(a, b, dims, preferred_element_type=jnp.float32)


def seg_of(position, ends):
    seg = (position >= ends[0]).astype(jnp.int32)
    for end in ends[1:]:
        seg = seg + (position >= end).astype(jnp.int32)
    return seg


def stack_heads(values, group):
    lane_head = lax.broadcasted_iota(jnp.int32, values.shape, 1) // HEAD_DIM
    return jnp.concatenate(
        [jnp.where(lane_head == h, values, jnp.zeros_like(values)) for h in range(group)], 0
    )


def each_key_block(meta, docs, q_at, q_rows, k_first, k_rows, k_blocks, group, body, masked=True):
    ends = [meta[i] for i in range(docs - 1)]
    q_lo, q_hi = seg_of(q_at, ends), seg_of(q_at + q_rows - 1, ends)
    q_seg = seg_of(q_at + lax.broadcasted_iota(jnp.int32, (1, q_rows), 1), ends)
    q_seg = jnp.concatenate([q_seg] * group, 1)

    def step(j, carry):
        k_at = meta[k_first + j]
        half = k_rows // 2
        marks = [seg_of(k_at + n, ends) for n in (0, half - 1, half, k_rows - 1)]
        low = (marks[0] <= q_hi) & (q_lo <= marks[1])
        high = (marks[2] <= q_hi) & (q_lo <= marks[3])
        same = (marks[0] == marks[3]) & (q_lo == q_hi)

        def run(first, count):
            if not masked:
                return body(j * k_rows + first, count, None)
            k_seg = seg_of(k_at + first + lax.broadcasted_iota(jnp.int32, (count, 1), 0), ends)
            return body(j * k_rows + first, count, k_seg == q_seg)

        if masked:
            pl.when(low & high & same)(lambda: body(j * k_rows, k_rows, None))
        pl.when(low & high & jnp.logical_not(same) if masked else low & high)(lambda: run(0, k_rows))
        pl.when(low & jnp.logical_not(high))(lambda: run(0, half))
        pl.when(high & jnp.logical_not(low))(lambda: run(half, half))
        return carry

    lax.fori_loop(0, k_blocks, step, 0)


def attend_kernel(docs, k_rows, meta, q_ref, k_ref, v_ref, o_0, o_1, o_2, o_3, lse_ref, vt_ref, s_ref, m_ref, l_ref, acc_ref):
    q_rows, wide = q_ref.shape[1], q_ref.shape[2]
    group = wide // HEAD_DIM
    k_blocks = k_ref.shape[1] // k_rows
    q_blocks = pl.num_programs(1)
    i = pl.program_id(1)

    @pl.when(i == 0)
    def _():
        for j in range(k_blocks):
            at = pl.ds(j * k_rows, k_rows)
            vt_ref[:, at] = v_ref[0, at, :].T

    q_st = stack_heads(q_ref[0] * SCORE_SCALE, group)
    m_ref[...] = jnp.full(m_ref.shape, MASKED_SCORE, jnp.float32)
    l_ref[...] = jnp.zeros_like(l_ref)
    acc_ref[...] = jnp.zeros_like(acc_ref)
    place = (docs, meta[docs - 1 + i], q_rows, docs - 1 + q_blocks, k_rows, k_blocks, group)

    def find_top(first, count, mask):
        at = pl.ds(pl.multiple_of(first, k_rows // 2), count)
        scores = dot(k_ref[0, at, :], q_st, NT)
        if mask is not None:
            scores = jnp.where(mask, scores, MASKED_SCORE)
        s_ref[at, :] = scores
        m_ref[...] = jnp.maximum(m_ref[...], jnp.max(scores, 0, keepdims=True))

    each_key_block(meta, *place, find_top)
    row_top = m_ref[...]

    def add_up(first, count, mask):
        at = pl.ds(pl.multiple_of(first, k_rows // 2), count)
        weights = jnp.exp(s_ref[at, :] - row_top)
        l_ref[...] += jnp.sum(weights, 0, keepdims=True)
        low = weights.astype(jnp.bfloat16)
        for h in range(group):
            rows = pl.ds(h * HEAD_DIM, HEAD_DIM)
            cols = slice(h * q_rows, (h + 1) * q_rows)
            acc_ref[rows, :] += dot(vt_ref[rows, at], low[:, cols], NN)

    each_key_block(meta, *place, add_up, False)
    total = l_ref[...]
    outs = []
    for h in range(group):
        cols = slice(h * q_rows, (h + 1) * q_rows)
        outs.append(acc_ref[h * HEAD_DIM : (h + 1) * HEAD_DIM, :] / total[:, cols])
    result = jnp.concatenate(outs, 0).T.astype(jnp.bfloat16)
    goal = (i % 2) * 2 + ((i // 2) ^ meta[docs - 1 + q_blocks + k_blocks])
    for n, part in enumerate((o_0, o_1, o_2, o_3)):
        @pl.when(goal == n)
        def _(part=part):
            part[...] = result

    lse_ref[0, 0] = row_top + jnp.log(total)


def attend_back_kernel(
    docs, k_rows, meta, q_ref, k_ref, v_ref, o_0, o_1, o_2, o_3, do_0, do_1, do_2, do_3, lse_ref, dq_ref, dk_ref, dv_ref,
    kt_ref, dqt_ref, dk_acc, dv_acc, do_ref, o_ref,
):
    q_rows, wide = q_ref.shape[1], q_ref.shape[2]
    group = wide // HEAD_DIM
    k_blocks = k_ref.shape[1] // k_rows
    q_blocks = pl.num_programs(1)
    i = pl.program_id(1)

    @pl.when(i == 0)
    def _():
        dk_acc[...] = jnp.zeros_like(dk_acc)
        dv_acc[...] = jnp.zeros_like(dv_acc)
        for j in range(k_blocks):
            at = pl.ds(j * k_rows, k_rows)
            kt_ref[:, at] = k_ref[0, at, :].T

    q_st = stack_heads(q_ref[0] * SCORE_SCALE, group)
    source = (i % 2) * 2 + ((i // 2) ^ meta[docs - 1 + q_blocks + k_blocks])
    for n, (part, out) in enumerate(((do_0, o_0), (do_1, o_1), (do_2, o_2), (do_3, o_3))):
        @pl.when(source == n)
        def _(part=part, out=out):
            do_ref[...] = part[...]
            o_ref[...] = out[...]

    grad_out = do_ref[...]
    do_st = stack_heads(grad_out, group)
    product = (grad_out.astype(jnp.float32) * o_ref[...].astype(jnp.float32)).T
    delta = jnp.concatenate(
        [jnp.sum(product[h * HEAD_DIM : (h + 1) * HEAD_DIM], 0, keepdims=True) for h in range(group)], 1
    )
    log_total = lse_ref[0, 0]
    dqt_ref[...] = jnp.zeros_like(dqt_ref)

    def body(first, count, mask):
        at = pl.ds(pl.multiple_of(first, k_rows // 2), count)
        scores = dot(k_ref[0, at, :], q_st, NT)
        if mask is not None:
            scores = jnp.where(mask, scores, MASKED_SCORE)
        probs = jnp.exp(scores - log_total)
        dv_acc[at, :] += dot(probs.astype(jnp.bfloat16), do_st, NN)
        grad_probs = dot(v_ref[0, at, :], do_st, NT)
        grad_scores = (probs * (grad_probs - delta)).astype(jnp.bfloat16)
        dk_acc[at, :] += dot(grad_scores, q_st, NN)
        for h in range(group):
            rows = pl.ds(h * HEAD_DIM, HEAD_DIM)
            cols = slice(h * q_rows, (h + 1) * q_rows)
            dqt_ref[rows, :] += dot(kt_ref[rows, at], grad_scores[:, cols], NN)

    each_key_block(meta, docs, meta[docs - 1 + i], q_rows, docs - 1 + q_blocks, k_rows, k_blocks, group, body)
    dq_ref[0] = (dqt_ref[...].T * SCORE_SCALE).astype(jnp.bfloat16)

    @pl.when(i == q_blocks - 1)
    def _():
        dk_ref[0] = dk_acc[...].astype(jnp.bfloat16)
        dv_ref[0] = dv_acc[...].astype(jnp.bfloat16)


def attend_call(meta, query, key, value, docs, q_rows, k_rows):
    items, length, wide = query.shape
    keys = key.shape[1]
    group = wide // HEAD_DIM
    q_blocks = length // q_rows
    block = pl.BlockSpec((1, q_rows, wide), lambda g, i, m: (g, i, 0))
    whole = pl.BlockSpec((1, keys, wide), lambda g, i, m: (g, 0, 0))
    stat = pl.BlockSpec((1, 1, 1, group * q_rows), lambda g, i, m: (g, i, 0, 0))
    return pl.pallas_call(
        functools.partial(attend_kernel, docs, k_rows),
        grid_spec=pltpu.PrefetchScalarGridSpec(
            num_scalar_prefetch=1,
            grid=(items, q_blocks),
            in_specs=[block, whole, whole],
            out_specs=[full((q_rows, wide))] * 4 + [stat],
            scratch_shapes=[
                pltpu.VMEM((wide, keys), jnp.bfloat16),
                pltpu.VMEM((keys, group * q_rows), jnp.float32),
                pltpu.VMEM((1, group * q_rows), jnp.float32),
                pltpu.VMEM((1, group * q_rows), jnp.float32),
                pltpu.VMEM((wide, q_rows), jnp.float32),
            ],
        ),
        out_shape=[jax.ShapeDtypeStruct((q_rows, wide), jnp.bfloat16)] * 4
        + [jax.ShapeDtypeStruct((items, q_blocks, 1, group * q_rows), jnp.float32)],
        compiler_params=pltpu.CompilerParams(vmem_limit_bytes=VMEM_LIMIT),
        name="attend",
    )(meta, query, key, value)


def attend_back_call(meta, query, key, value, out, grad_parts, log_total, docs, q_rows, k_rows):
    items, length, wide = query.shape
    keys = key.shape[1]
    group = wide // HEAD_DIM
    q_blocks = length // q_rows
    block = pl.BlockSpec((1, q_rows, wide), lambda g, i, m: (g, i, 0))
    whole = pl.BlockSpec((1, keys, wide), lambda g, i, m: (g, 0, 0))
    stat = pl.BlockSpec((1, 1, 1, group * q_rows), lambda g, i, m: (g, i, 0, 0))
    return pl.pallas_call(
        functools.partial(attend_back_kernel, docs, k_rows),
        grid_spec=pltpu.PrefetchScalarGridSpec(
            num_scalar_prefetch=1,
            grid=(items, q_blocks),
            in_specs=[block, whole, whole] + [full((q_rows, wide))] * 8 + [stat],
            out_specs=[block, whole, whole],
            scratch_shapes=[
                pltpu.VMEM((wide, keys), jnp.bfloat16),
                pltpu.VMEM((wide, q_rows), jnp.float32),
                pltpu.VMEM((keys, wide), jnp.float32),
                pltpu.VMEM((keys, wide), jnp.float32),
                pltpu.VMEM((q_rows, wide), jnp.bfloat16),
                pltpu.VMEM((q_rows, wide), jnp.bfloat16),
            ],
        ),
        out_shape=[
            jax.ShapeDtypeStruct(query.shape, jnp.bfloat16),
            jax.ShapeDtypeStruct(key.shape, jnp.bfloat16),
            jax.ShapeDtypeStruct(key.shape, jnp.bfloat16),
        ],
        compiler_params=pltpu.CompilerParams(vmem_limit_bytes=VMEM_LIMIT),
        name="attend_back",
    )(meta, query, key, value, *out, *grad_parts, log_total)


def layer_norm(values, gain):
    mean_value = jnp.mean(values, -1, keepdims=True)
    centred = values - mean_value
    spread = jnp.mean(centred * centred, -1, keepdims=True)
    return centred * lax.rsqrt(spread + EPSILON) * gain


def norm_parts(values):
    centred = values - jnp.mean(values, -1, keepdims=True)
    inverse = lax.rsqrt(jnp.mean(centred * centred, -1, keepdims=True) + EPSILON)
    return centred * inverse, inverse


def turn_matrix(width):
    row = lax.broadcasted_iota(jnp.int32, (width, width), 0)
    col = lax.broadcasted_iota(jnp.int32, (width, width), 1)
    half = HEAD_DIM // 2
    first = (col % HEAD_DIM) < half
    plus = jnp.logical_not(first) & (row == col - half)
    minus = first & (row == col + half)
    return plus.astype(jnp.bfloat16) - minus.astype(jnp.bfloat16)


def angles(positions, width):
    half = HEAD_DIM // 2
    steps_index = (jnp.arange(width) % half).astype(jnp.float32)
    inverse = ROPE_THETA ** (-2.0 * steps_index / HEAD_DIM)
    return positions.astype(jnp.float32)[:, None] * inverse[None, :]


def turned_tables(cos_row, sin_row, base):
    cos_base, sin_base = base[0:1, :], base[1:2, :]
    return cos_row * cos_base - sin_row * sin_base, sin_row * cos_base + cos_row * sin_base


def full(shape):
    return pl.BlockSpec(shape, lambda *_: (0,) * len(shape))


def padded(wide):
    return -(-wide // 128) * 128


def project_kernel(meta, *refs):
    chunk_refs = refs[:8]
    w_ref, turn_ref, cos_ref, sin_ref, base_ref, normed_ref, q_ref, k_ref, v_ref, x_ref, w_all, gain_row = refs[8:]
    wide = q_ref.shape[2]
    slot = padded(wide)
    i = pl.program_id(0)
    bf16 = jnp.bfloat16

    @pl.when(i == 0)
    def _():
        for p, at in ((1, 0), (2, 2), (0, 3)):
            w_all[:, at * slot : at * slot + wide] = w_ref[:, p * wide : (p + 1) * wide]
        for p, at in ((1, 1), (0, 4)):
            turned = dot(w_ref[:, p * wide : (p + 1) * wide], turn_ref[...], NN)
            w_all[:, at * slot : at * slot + wide] = turned.astype(bf16)
        last = w_ref[:, w_ref.shape[1] - 128 :].astype(jnp.float32).T
        gain_row[...] = last[127:128, :]

    for n in range(8):
        @pl.when(i == n)
        def _(n=n):
            x_ref[...] = chunk_refs[n][...]

    normed, _ = norm_parts(x_ref[...].astype(jnp.float32))
    normed = (normed * gain_row[...]).astype(bf16)
    normed_ref[0] = normed.T
    cos, sin = turned_tables(cos_ref[...], sin_ref[...], base_ref[0])
    raw = dot(normed, w_all[:, : 3 * slot], NN)
    k_ref[0] = (raw[:, :wide] * cos + raw[:, slot : slot + wide] * sin).astype(bf16)
    v_ref[0] = raw[:, 2 * slot : 2 * slot + wide].astype(bf16)

    @pl.when(i % 2 == meta[0])
    def _():
        raw_q = dot(normed, w_all[:, 3 * slot : 5 * slot], NN)
        q_ref[0] = (raw_q[:, :wide] * cos + raw_q[:, slot : slot + wide] * sin).astype(bf16)


def project_call(meta, chunks, w, turn, cos_row, sin_row, bases, wide):
    block, width = chunks[0].shape
    bf16 = jnp.bfloat16
    one = lambda i, m: (i, 0, 0)
    return pl.pallas_call(
        project_kernel,
        grid_spec=pltpu.PrefetchScalarGridSpec(
            num_scalar_prefetch=1,
            grid=(8,),
            in_specs=[full((block, width))] * 8
            + [full(w.shape), full(turn.shape), full(cos_row.shape), full(sin_row.shape), pl.BlockSpec((1, 2, wide), one)],
            out_specs=[
                pl.BlockSpec((1, width, block), one),
                pl.BlockSpec((1, block, wide), lambda i, m: (i // 2, 0, 0)),
                pl.BlockSpec((1, block, wide), one),
                pl.BlockSpec((1, block, wide), one),
            ],
            scratch_shapes=[
                pltpu.VMEM((block, width), bf16),
                pltpu.VMEM((width, 5 * padded(wide)), bf16),
                pltpu.VMEM((1, width), jnp.float32),
            ],
        ),
        out_shape=[
            jax.ShapeDtypeStruct((8, width, block), bf16),
            jax.ShapeDtypeStruct((4, block, wide), bf16),
            jax.ShapeDtypeStruct((8, block, wide), bf16),
            jax.ShapeDtypeStruct((8, block, wide), bf16),
        ],
        compiler_params=pltpu.CompilerParams(vmem_limit_bytes=VMEM_LIMIT),
        name="project",
    )(meta, *chunks, w, turn, cos_row, sin_row, bases)


def feed_kernel(ff, meta, *refs):
    parts, slices = refs[0:4], refs[4:8]
    tok_ref, cot_ref = refs[8:10]
    out_ref, gh_ref, normed_ref, att_ref, cot_t_ref, gated_ref, ga_ref, gb_ref, gbr_ref, dgain_ref = refs[10:20]
    grad_parts = refs[20:24]
    w_a, w_b, w_dt, w_o, gain_row, att_scr = refs[24:30]
    wide = parts[0].shape[1]
    i = pl.program_id(0)
    bf16 = jnp.bfloat16

    @pl.when(i == 0)
    def _():
        for n in range(4):
            at = slice(n * ff, (n + 1) * ff)
            w_a[:, at] = slices[n][:, :ff]
            w_b[:, at] = slices[n][:, ff : 2 * ff]
            w_dt[:, at] = slices[n][:, 2 * ff : 3 * ff]
            for g in range(4):
                @pl.when(meta[n] == g)
                def _(n=n, g=g):
                    w_o[:, g * wide : (g + 1) * wide] = slices[n][:, 3 * ff : 3 * ff + wide]
        last = slices[0][:, slices[0].shape[1] - 128 :].astype(jnp.float32).T
        gain_row[...] = last[127:128, :]
        dgain_ref[...] = jnp.zeros_like(dgain_ref)

    for g in range(4):
        for n in range(4):
            @pl.when(meta[4 + n] == g)
            def _(n=n, g=g):
                att_scr[:, g * wide : (g + 1) * wide] = parts[n][...]

    attended = att_scr[...]
    att_ref[...] = attended.T
    gain = gain_row[...]
    hidden = tok_ref[...].astype(jnp.float32) + dot(attended, w_o[...], NN)
    normal, inverse = norm_parts(hidden)
    normed = (normal * gain).astype(bf16)
    normed_ref[...] = normed.T
    half_a = dot(normed, w_a[...], NN)
    half_b = dot(normed, w_b[...], NN)
    phi = 0.5 * (1.0 + lax.erf(half_a * ROOT_HALF))
    gelu = half_a * phi
    slope = phi + half_a * (jnp.exp(-0.5 * half_a * half_a) * INVERSE_ROOT_TAU)
    gated = (gelu * half_b).astype(bf16)
    out_ref[...] = (hidden + dot(gated, w_dt[...], NT)).astype(bf16)
    cot = cot_ref[...]
    cot_t_ref[...] = cot.T
    grad_gated = dot(cot, w_dt[...], NN)
    grad_a = (grad_gated * half_b * slope).astype(bf16)
    grad_b = (grad_gated * gelu).astype(bf16)
    for n in range(4):
        at = slice(n * ff, (n + 1) * ff)
        gated_ref[n] = gated[:, at]
        ga_ref[n] = grad_a[:, at]
        gb_ref[n] = grad_b[:, at]
    grad_normed = dot(grad_a, w_a[...], NT) + dot(grad_b, w_b[...], NT)
    dgain_ref[...] += jnp.sum(grad_normed * normal, 0, keepdims=True)
    scaled = grad_normed * gain
    inner = jnp.mean(scaled * normal, -1, keepdims=True)
    grad_hidden = cot.astype(jnp.float32) + inverse * (
        scaled - jnp.mean(scaled, -1, keepdims=True) - normal * inner
    )
    gh_ref[...] = grad_hidden
    grad_branch = grad_hidden.astype(bf16)
    for g in range(4):
        gbr_ref[g] = grad_branch[:, g * wide : (g + 1) * wide]
    grad_mixed = dot(grad_branch, w_o[...], NT).astype(bf16)
    for g in range(4):
        for n in range(4):
            @pl.when(meta[4 + n] == g)
            def _(n=n, g=g):
                grad_parts[n][...] = grad_mixed[:, g * wide : (g + 1) * wide]


def feed_call(meta, parts, slices, tokens, cotangent, ff):
    block, width = tokens.shape
    wide = parts[0].shape[1]
    bf16, f32 = jnp.bfloat16, jnp.float32
    rows = min(256, block)
    part = pl.BlockSpec((rows, wide), lambda i, m: (i, 0))
    row = pl.BlockSpec((rows, width), lambda i, m: (i, 0))
    hid = pl.BlockSpec((4, rows, ff), lambda i, m: (0, i, 0))
    flat = pl.BlockSpec((width, rows), lambda i, m: (0, i))
    grp = pl.BlockSpec((4, rows, wide), lambda i, m: (0, i, 0))
    sds = jax.ShapeDtypeStruct
    return pl.pallas_call(
        functools.partial(feed_kernel, ff),
        grid_spec=pltpu.PrefetchScalarGridSpec(
            num_scalar_prefetch=1,
            grid=(block // rows,),
            in_specs=[part] * 4 + [full(slices[0].shape)] * 4 + [row, row],
            out_specs=[row, row, flat, flat, flat, hid, hid, hid, grp, full((1, width))] + [part] * 4,
            scratch_shapes=[pltpu.VMEM((width, 4 * ff), bf16)] * 3
            + [pltpu.VMEM((width, width), bf16), pltpu.VMEM((1, width), f32), pltpu.VMEM((rows, width), bf16)],
        ),
        out_shape=[
            sds((block, width), bf16),
            sds((block, width), f32),
            sds((width, block), bf16),
            sds((width, block), bf16),
            sds((width, block), bf16),
            sds((4, block, ff), bf16),
            sds((4, block, ff), bf16),
            sds((4, block, ff), bf16),
            sds((4, block, wide), bf16),
            sds((1, width), f32),
        ]
        + [sds((block, wide), bf16)] * 4,
        compiler_params=pltpu.CompilerParams(vmem_limit_bytes=VMEM_LIMIT),
        name="feed",
    )(meta, *parts, *slices, tokens, cotangent)


def pack_kernel(meta, nm_t, cot_t, att_t, ga_ref, gb_ref, gated_ref, gbr_ref, dgain_ref, out_ref):
    ff, wide = ga_ref.shape[2], gbr_ref.shape[2]
    bf16 = jnp.bfloat16

    width = nm_t.shape[0]
    gain = jnp.broadcast_to(dgain_ref[...], (128, width)).T
    last = out_ref.shape[2] - (3 * ff + wide)
    out_ref[0] = jnp.concatenate(
        [
            dot(nm_t[...], ga_ref[0], NN),
            dot(nm_t[...], gb_ref[0], NN),
            dot(cot_t[...], gated_ref[0], NN),
            dot(att_t[...], gbr_ref[0], NN),
            gain[:, :last],
        ],
        1,
    ).astype(bf16)


def pack_call(meta, normed, cotangent, attended, grad_a, grad_b, gated, grad_branch, d_gain, first):
    width, block = normed.shape
    ff, wide = grad_a.shape[2], grad_branch.shape[2]
    bf16 = jnp.bfloat16
    packed = padded(3 * ff + wide + 1)
    hid = pl.BlockSpec((1, block, ff), lambda i, m: (first + i, 0, 0))
    return pl.pallas_call(
        pack_kernel,
        grid_spec=pltpu.PrefetchScalarGridSpec(
            num_scalar_prefetch=1,
            grid=(2,),
            in_specs=[full((width, block))] * 3
            + [hid] * 3
            + [pl.BlockSpec((1, block, wide), lambda i, m: (m[first + i], 0, 0)), full((1, width))],
            out_specs=pl.BlockSpec((1, width, packed), lambda i, m: (i, 0, 0)),
        ),
        out_shape=jax.ShapeDtypeStruct((2, width, packed), bf16),
        compiler_params=pltpu.CompilerParams(vmem_limit_bytes=VMEM_LIMIT),
        name="pack",
    )(meta, normed, cotangent, attended, grad_a, grad_b, gated, grad_branch, d_gain)


def unturn_kernel(meta, normed_ref, dq_ref, dk_ref, dv_ref, turn_ref, cos_ref, sin_ref, base_ref, raw_ref, dw_ref, acc_ref):
    wide = dk_ref.shape[2]
    i = pl.program_id(0)

    @pl.when(i == 0)
    def _():
        acc_ref[...] = jnp.zeros_like(acc_ref)

    cos, sin = turned_tables(cos_ref[...], sin_ref[...], base_ref[0])

    def turn_back(grad):
        return (grad.astype(jnp.float32) * cos + dot(grad, turn_ref[...], NT) * sin).astype(jnp.bfloat16)

    mine = meta[0] == i % 2
    raw_ref[0, :, wide : 2 * wide] = turn_back(dk_ref[0])
    raw_ref[0, :, 2 * wide : 3 * wide] = dv_ref[0]

    @pl.when(mine)
    def _():
        raw_ref[0, :, :wide] = turn_back(dq_ref[0])

    @pl.when(jnp.logical_not(mine))
    def _():
        raw_ref[0, :, :wide] = jnp.zeros_like(dk_ref[0])

    acc_ref[...] += dot(normed_ref[0], raw_ref[0], NN)

    @pl.when(i == pl.num_programs(0) - 1)
    def _():
        dw_ref[...] = acc_ref[...].astype(jnp.bfloat16)


def unturn_call(meta, normed_t, dq, dk, dv, turn, cos_row, sin_row, bases):
    _, width, block = normed_t.shape
    wide = dk.shape[2]
    one = lambda i, m: (i, 0, 0)
    return pl.pallas_call(
        unturn_kernel,
        grid_spec=pltpu.PrefetchScalarGridSpec(
            num_scalar_prefetch=1,
            grid=(8,),
            in_specs=[
                pl.BlockSpec((1, width, block), one),
                pl.BlockSpec((1, block, wide), lambda i, m: (i // 2, 0, 0)),
                pl.BlockSpec((1, block, wide), one),
                pl.BlockSpec((1, block, wide), one),
                full(turn.shape),
                full(cos_row.shape),
                full(sin_row.shape),
                pl.BlockSpec((1, 2, wide), one),
            ],
            out_specs=[pl.BlockSpec((1, block, 3 * wide), one), full((width, 3 * wide))],
            scratch_shapes=[pltpu.VMEM((width, 3 * wide), jnp.float32)],
        ),
        out_shape=[
            jax.ShapeDtypeStruct((8, block, 3 * wide), jnp.bfloat16),
            jax.ShapeDtypeStruct((width, 3 * wide), jnp.bfloat16),
        ],
        compiler_params=pltpu.CompilerParams(vmem_limit_bytes=VMEM_LIMIT),
        name="unturn",
    )(meta, normed_t, dq, dk, dv, turn, cos_row, sin_row, bases)


def unproject_kernel(raw_ref, w_ref, partial_ref):
    partial_ref[0] = dot(raw_ref[0], w_ref[:, : raw_ref.shape[2]], NT).astype(jnp.bfloat16)


def unproject_call(core, grad_raw, w):
    _, block, columns = grad_raw.shape
    width = w.shape[0]
    return pl.pallas_call(
        unproject_kernel,
        grid=(4,),
        in_specs=[pl.BlockSpec((1, block, columns), lambda i: (2 * i + core, 0, 0)), full(w.shape)],
        out_specs=pl.BlockSpec((1, block, width), lambda i: (i, 0, 0)),
        out_shape=jax.ShapeDtypeStruct((4, block, width), jnp.bfloat16),
        compiler_params=pltpu.CompilerParams(vmem_limit_bytes=VMEM_LIMIT),
        name="unproject",
    )(grad_raw, w)


PLANE = ("ctx", "tensor")


def plane_permute(array, target):
    pairs = []
    for c in range(2):
        for x in range(2):
            for h in range(2):
                to_c, to_x, to_h = target(c, x, h)
                pairs.append((c * 4 + x * 2 + h, to_c * 4 + to_x * 2 + to_h))
    return lax.ppermute(array, PLANE, pairs)


def tensor_permute(array, flip):
    return lax.ppermute(array, "tensor", [(t, t ^ flip) for t in range(4)])


def pick(array, index, axis):
    return lax.dynamic_index_in_dim(array, index, axis, keepdims=False)


def local(tokens, doc_lengths, attn_gain, mlp_gain, w_qkv, w_attn_out, w_in, w_down, cotangent):
    _, block, width = tokens.shape
    assert lax.axis_size("ctx") == 2 and lax.axis_size("tensor") == 4 and tokens.shape[0] == 1
    rows = w_qkv.shape[0]
    ff = w_in.shape[2]
    docs = doc_lengths.shape[1]
    c = lax.axis_index("ctx")
    t = lax.axis_index("tensor")
    x, h = t // 2, t % 2
    wide = width // 4
    bf16 = jnp.bfloat16

    own = tokens[0]
    over_y = lambda c, x, h: (1 - c, x, h)
    shards = lax.axis_size("shard")
    shard_at = lax.axis_index("shard")

    def shard_gather(part):
        whole = jnp.zeros((shards,) + part.shape, part.dtype)
        pieces = [part]
        for k in range(1, shards):
            pieces.append(lax.ppermute(part, "shard", [(z, (z + k) % shards) for z in range(shards)]))
        for k, piece in enumerate(pieces):
            whole = lax.dynamic_update_index_in_dim(whole, piece, lax.rem(shard_at + shards - k, shards), 0)
        return whole

    def both_ctx(mine, other, axis):
        return jnp.where(c == 0, jnp.stack([mine, other], axis), jnp.stack([other, mine], axis))

    group_cols = pick(w_qkv.reshape(rows, 3, 4, wide), t, 2).reshape(rows, 3 * wide)
    gain_cols = padded(3 * wide + 1) - 3 * wide
    pack_1 = jnp.concatenate([group_cols, jnp.broadcast_to(attn_gain[:, None], (rows, gain_cols))], 1)
    own_cols = pick(w_attn_out.reshape(rows, 4, wide), t, 1)
    gain_cols = padded(3 * ff + wide + 1) - 3 * ff - wide
    pack_2 = jnp.concatenate(
        [w_in.reshape(rows, 2 * ff), w_down.T, own_cols, jnp.broadcast_to(mlp_gain[:, None], (rows, gain_cols))], 1
    )
    slice_flips = (0, 2, 1, 3)

    by_x = tensor_permute(own, 2)
    by_y = plane_permute(own, over_y)
    by_xy = plane_permute(own, lambda c, x, h: (1 - c, 1 - x, h))
    row_angles = angles(jnp.arange(block), wide)
    cos_row, sin_row = jnp.cos(row_angles), jnp.sin(row_angles)
    pack_1 = shard_gather(pack_1)
    pack_1, pack_2, cos_row, sin_row = lax.optimization_barrier((pack_1, pack_2, cos_row, sin_row))
    pack_1_y, pack_2 = lax.optimization_barrier((plane_permute(pack_1, over_y), shard_gather(pack_2)))
    pack_1 = both_ctx(pack_1, pack_1_y, 1).reshape(width, -1)
    pack_2_y = plane_permute(pack_2, over_y)
    chunks = [chunk for part in (own, by_x, by_y, by_xy) for chunk in (part, tensor_permute(part, 1))]

    chunk_at = []
    for dc in range(2):
        for dx in range(2):
            for dh in range(2):
                chunk_at.append(((c ^ dc) * 4 + (x ^ dx) * 2 + (h ^ dh)) * block)
    base_angles = angles(jnp.stack(chunk_at), wide)
    bases = jnp.stack([jnp.cos(base_angles), jnp.sin(base_angles)], 1)
    q_rows = block
    k_rows = min(512, block)
    pick_core = h ^ c
    key_starts = [at + k * k_rows for at in chunk_at for k in range(block // k_rows)]
    query_starts = [
        ((c ^ dc) * 4 + (x ^ dx) * 2 + c) * block
        for dc in range(2)
        for dx in range(2)
    ]
    doc_ends = jnp.cumsum(doc_lengths[0])[: docs - 1].astype(jnp.int32)
    meta = jnp.concatenate([doc_ends, jnp.stack(query_starts + key_starts + [pick_core]).astype(jnp.int32)])
    core_meta = jnp.stack([pick_core]).astype(jnp.int32)
    steps = [(a, b) for b in range(2) for a in range(2)]
    feed_meta = jnp.stack(
        [t ^ flip for flip in slice_flips] + [(x ^ b) * 2 + (c ^ a) for a, b in steps]
    ).astype(jnp.int32)

    turn = turn_matrix(wide)
    normed_t, query, key, value = project_call(core_meta, chunks, pack_1, turn, cos_row, sin_row, bases, wide)
    query, pack_2_y = lax.optimization_barrier((query, pack_2_y))
    pack_2 = both_ctx(pack_2, pack_2_y, 1).reshape(width, -1)
    query, pack_2 = lax.optimization_barrier((query, pack_2))
    slices = [pack_2, tensor_permute(pack_2, 2), tensor_permute(pack_2, 1)]
    query = query.reshape(1, 4 * block, wide)
    key = key.reshape(1, 8 * block, wide)
    value = value.reshape(1, 8 * block, wide)
    *out, log_total = attend_call(meta, query, key, value, docs, q_rows, k_rows)

    def forth(a, b):
        return lambda c, x, h: (h ^ a, x ^ b, c)

    def back(a, b):
        return lambda c, x, h: (h, x ^ b, c ^ a)

    arrived = [plane_permute(part, forth(a, b)) for part, (a, b) in zip(out, steps)]
    arrived[0], slices[1] = lax.optimization_barrier((arrived[0], slices[1]))
    slices.append(tensor_permute(slices[1], 1))

    (layer_out, grad_hidden, normed_m, attended, cot_t, gated, grad_a, grad_b, grad_branch, d_gain_mlp, *grad_parts) = feed_call(
        feed_meta, arrived, slices, own, cotangent[0], ff
    )
    grad_parts = [plane_permute(part, back(a, b)) for part, (a, b) in zip(grad_parts, steps)]

    def add(one, two):
        return (one.astype(jnp.float32) + two.astype(jnp.float32)).astype(bf16)

    grads = (normed_m, cot_t, attended, grad_a, grad_b, gated, grad_branch, d_gain_mlp)
    sent_packs, *grad_parts[:2] = lax.optimization_barrier((pack_call(feed_meta, *grads, 2), *grad_parts[:2]))
    sent_packs = tensor_permute(sent_packs, 1)
    packs = add(pack_call(feed_meta, *grads, 0), sent_packs)
    packed = packs.shape[2]
    cut = padded(packed // 2)
    packs = packs.reshape(2, -1, 2, rows, packed)
    one_x = tensor_permute(packs[1, ..., :cut], 2)
    one_y = plane_permute(pick(packs[..., cut:], 1 - c, 2), over_y)
    kept_x, kept_y = packs[0, ..., :cut], pick(packs[..., cut:], c, 2)
    grad_parts, kept_x, kept_y = lax.optimization_barrier((grad_parts, kept_x, kept_y))

    grad_query, grad_key, grad_value = attend_back_call(
        meta, query, key, value, out, grad_parts, log_total, docs, q_rows, k_rows
    )
    kept_x, kept_y = add(kept_x, one_x), add(kept_y, one_y)
    grad_key, kept_x, kept_y = lax.optimization_barrier((grad_key, kept_x, kept_y))
    two_y = plane_permute(pick(kept_x, 1 - c, 1), over_y)
    two_x = tensor_permute(kept_y[1], 2)
    grad_query = grad_query.reshape(4, block, wide)
    grad_key = grad_key.reshape(8, block, wide)
    grad_value = grad_value.reshape(8, block, wide)
    grad_raw, d_qkv = unturn_call(
        core_meta, normed_t, grad_query, grad_key, grad_value, turn, cos_row, sin_row, bases
    )
    grad_raw, d_qkv, two_x, two_y = lax.optimization_barrier((grad_raw, d_qkv, two_x, two_y))
    pack = jnp.concatenate([add(pick(kept_x, c, 1), two_y), add(kept_y[0], two_x)], 2)
    d_qkv = d_qkv.reshape(-1, 2, rows, 3 * wide)
    d_qkv_y = plane_permute(pick(d_qkv, 1 - c, 1), over_y)
    d_qkv_own = pick(d_qkv, c, 1)
    from_core = tensor_permute(unproject_call(1, grad_raw, pack_1), 1)
    partial = unproject_call(0, grad_raw, pack_1)

    chip_sum = [add(partial[n], from_core[n]) for n in range(4)]
    sent = [
        tensor_permute(chip_sum[1], 2),
        plane_permute(chip_sum[2], over_y),
        plane_permute(chip_sum[3], lambda c, x, h: (1 - c, 1 - x, h)),
    ]
    pack, d_qkv_y, chip_sum = lax.optimization_barrier((pack, d_qkv_y, chip_sum))
    d_qkv_y, sent[0] = lax.optimization_barrier((d_qkv_y, sent[0]))

    def shard_sum(parts):
        total = pick(parts, shard_at, 0).astype(jnp.float32)
        for k in range(1, shards):
            part = pick(parts, lax.rem(shard_at + k, shards), 0)
            total = total + lax.ppermute(part, "shard", [(z, (z + k) % shards) for z in range(shards)]).astype(jnp.float32)
        return total

    pack = shard_sum(pack)
    d_in = pack[:, : 2 * ff].reshape(rows, 2, ff)
    d_down = pack[:, 2 * ff : 3 * ff].T
    d_group_out = pack[:, 3 * ff : 3 * ff + wide].astype(bf16)
    d_gain_mlp = pick(pack[:, 3 * ff + wide].reshape(4, rows // 4), t, 0)
    d_qkv = shard_sum(add(d_qkv_own, d_qkv_y)).astype(bf16)
    d_qkv, sent = lax.optimization_barrier((d_qkv, sent))
    d_both = jnp.concatenate([d_qkv, d_group_out], 1).reshape(4, rows // 4, 4 * wide)
    d_both = lax.all_to_all(d_both, "tensor", split_axis=0, concat_axis=0, tiled=True)
    d_both = d_both.reshape(4, rows // 4, 4, wide).transpose(1, 2, 0, 3).reshape(rows // 4, 4 * width)
    d_both = d_both.astype(jnp.float32)
    d_qkv, d_attn_out = d_both[:, : 3 * width], d_both[:, 3 * width :]
    own_rows = pick(w_qkv.reshape(4, rows // 4, 3 * width), t, 0).astype(jnp.float32)
    own_gain = pick(attn_gain.reshape(4, rows // 4), t, 0).astype(jnp.float32)
    d_gain_attn = jnp.sum(d_qkv * own_rows, 1) / own_gain

    grad_normed = chip_sum[0].astype(jnp.float32)
    for part in sent:
        grad_normed = grad_normed + part.astype(jnp.float32)
    gain_attn = pack_1[:, 3 * wide].astype(jnp.float32)
    _, norm_pull_attn = jax.vjp(lambda values: layer_norm(values, gain_attn), own.astype(jnp.float32))
    grad_tokens = grad_hidden + norm_pull_attn(grad_normed)[0]
    return (layer_out[None], grad_tokens[None], d_gain_attn, d_gain_mlp, d_qkv, d_attn_out, d_in, d_down)


def solution(mesh):
    return jax.shard_map(
        local,
        mesh=mesh,
        in_specs=(
            P("shard", ("ctx", "tensor"), None),
            P("shard", None),
            P(("shard", "ctx")),
            P(("shard", "ctx")),
            P(("shard", "ctx"), None),
            P(("shard", "ctx"), None),
            P(("shard", "ctx"), None, "tensor"),
            P("tensor", ("shard", "ctx")),
            P("shard", ("ctx", "tensor"), None),
        ),
        out_specs=(
            P("shard", ("ctx", "tensor"), None),
            P("shard", ("ctx", "tensor"), None),
            P(("shard", "ctx", "tensor")),
            P(("shard", "ctx", "tensor")),
            P(("shard", "ctx", "tensor"), None),
            P(("shard", "ctx", "tensor"), None),
            P(("shard", "ctx"), None, "tensor"),
            P("tensor", ("shard", "ctx")),
        ),
        check_vma=False,
    )
```
